32 devices in a mesh: ctx: 16 (over z, y, core), fsdp: 2 (over x).
Axes of the slice: x: 2, y: 2, z: 4, core: 2. Of those that a mesh axis runs over, the one named last changes fastest.
Arguments:
- tokens: bfloat16 [4, 2048, 768], P('fsdp', 'ctx'), may hold values from -6 to 6
- cotangent: bfloat16 [4, 2048, 768], P('fsdp', 'ctx'), may hold values from -6 to 6
- lengths: int32 [4], P('fsdp'), may hold values from 512 to 2048, as said below
- ln1_gain: bfloat16 [768], P('fsdp'), may hold values from 0.5 to 1.5
- ln1_bias: bfloat16 [768], P('fsdp'), may hold values from -1.796875 to 1.796875
- w_qkv: bfloat16 [768, 2304], P('fsdp'), may hold values from -0.21875 to 0.21875
- w_conv: bfloat16 [3, 2304], P(None, 'fsdp'), may hold values from -3 to 3
- w_out: bfloat16 [768, 768], P('fsdp'), may hold values from -1.75 to 1.75
- ln2_gain: bfloat16 [768], P('fsdp'), may hold values from 0.5 to 1.5
- ln2_bias: bfloat16 [768], P('fsdp'), may hold values from -1.796875 to 1.796875
- w_up: bfloat16 [768, 3072], P('fsdp'), may hold values from -0.21875 to 0.21875
- w_down: bfloat16 [3072, 768], P('fsdp'), may hold values from -0.109375 to 0.109375
Outputs:
- output: bfloat16 [4, 2048, 768], P('fsdp', 'ctx')
- input_grad: float32 [4, 2048, 768], P('fsdp', 'ctx')
- ln1_gain_grad: float32 [768], P('fsdp')
- ln1_bias_grad: float32 [768], P('fsdp')
- w_qkv_grad: float32 [768, 2304], P('fsdp')
- w_conv_grad: float32 [3, 2304], P(None, 'fsdp')
- w_out_grad: float32 [768, 768], P('fsdp')
- ln2_gain_grad: float32 [768], P('fsdp')
- ln2_bias_grad: float32 [768], P('fsdp')
- w_up_grad: float32 [768, 3072], P('fsdp')
- w_down_grad: float32 [3072, 768], P('fsdp')
The draws below stay inside these ranges and needn't reach their ends.
Inputs may be any that keep to these rules, and one draw needn't show every extreme that they name: `lengths`: each sequence's number of valid positions; positions at or past it are padding; among each 2 consecutive sequences, one has all 2048 positions valid.
All inputs are finite; a program needn't handle non-finite values.
Results may differ from the reference program's by a relative error of at most 0.025.
Values may be sent and summed in bfloat16 or wider, within the bound.
No kernel may reach another device: no remote copies, remote signals or barrier semaphores. Data moves between devices by JAX's collectives and lax.ppermute only.
A program may use at most 192 MiB of HBM per device.

```python
import jax
import jax.numpy as jnp
from jax import lax

D = 768
HEADS = 12
HEAD = 64
FF = 3072
SEQS = 2
SEQ_LEN = 2048
SEQUENCES = 4


def draw_lengths(key, part):
    first, second = jax.random.split(jax.random.fold_in(key, 11))
    drawn = jax.random.randint(first, (SEQUENCES,), SEQ_LEN // 4, SEQ_LEN + 1)
    groups = SEQUENCES // SEQS
    chosen = jax.random.randint(second, (groups,), 0, SEQS)
    where_full = jnp.arange(groups, dtype=jnp.int32) * SEQS + chosen
    drawn = drawn.at[where_full].set(SEQ_LEN)
    return drawn.astype(jnp.int32)


def block_scale(rng, shape, cuts, low, largest):
    def one(dim, parts):
        heights = jax.random.uniform(jax.random.fold_in(jax.random.fold_in(rng, 6), dim), (parts,), jnp.float32, low / len(cuts), largest / len(cuts))
        return jnp.repeat(jnp.exp(heights), shape[dim] // parts).reshape((-1,) + (1,) * (len(shape) - dim - 1))

    level = one(*cuts[0])
    for cut in cuts[1:]:
        level = level * one(*cut)
    return level


def centred(own_key, extent, scale, bound, shards=(), kind=jnp.bfloat16):
    entries = scale * jax.random.normal(own_key, extent, jnp.float32)
    if shards:
        entries = entries * block_scale(own_key, extent, shards, -0.22, 0.18)
    return jnp.clip(entries, -bound, bound).astype(kind)


def setup_inputs(seed: int = 0) -> dict:
    seeds = jax.random.split(jax.random.key(seed), 13)
    tokens = centred(seeds[0], (SEQUENCES, SEQ_LEN, D), 1.0, 6.0, ((0, 2), (1, 16)))
    cotangent = centred(seeds[1], (SEQUENCES, SEQ_LEN, D), 1.0, 6.0, ((0, 2), (1, 16)))
    lengths = draw_lengths(jax.random.fold_in(seeds[12], 71), 0)
    ln1_gain = jnp.clip(1.0 + 0.1 * jax.random.normal(seeds[3], (D,), jnp.float32), 0.5, 1.5).astype(jnp.bfloat16)
    ln1_bias = centred(seeds[4], (D,), 0.3, 1.796875, ((0, 2),))
    w_qkv = centred(seeds[5], (D, 3 * D), D ** -0.5, 0.21875, ((0, 2),))
    w_conv = centred(seeds[6], (3, 3 * D), 0.6, 3.0, ((1, 2),))
    w_out = centred(seeds[7], (D, D), (D // 64) ** -0.5, 1.75, ((0, 2),))
    ln2_gain = jnp.clip(1.0 + 0.1 * jax.random.normal(seeds[8], (D,), jnp.float32), 0.5, 1.5).astype(jnp.bfloat16)
    ln2_bias = centred(seeds[9], (D,), 0.3, 1.796875, ((0, 2),))
    w_up = centred(seeds[10], (D, FF), D ** -0.5, 0.21875, ((0, 2),))
    w_down = centred(seeds[11], (FF, D), FF ** -0.5, 0.109375, ((0, 2),))
    return dict(tokens=tokens, cotangent=cotangent, lengths=lengths, ln1_gain=ln1_gain, ln1_bias=ln1_bias, w_qkv=w_qkv, w_conv=w_conv, w_out=w_out, ln2_gain=ln2_gain, ln2_bias=ln2_bias, w_up=w_up, w_down=w_down)


@jax.custom_vjp
def low(v):
    return lax.optimization_barrier(v.astype(jnp.bfloat16)).astype(jnp.float32)

@jax.custom_vjp
def low_back(v):
    return v

def low_keep(v):
    return (low(v), None)

def low_pass(kept, grad):
    return (grad,)

def back_keep(v):
    return (v, None)

def back_low(kept, grad):
    return (low(grad),)
low.defvjp(low_keep, low_pass)
low_back.defvjp(back_keep, back_low)
highest = lax.Precision.HIGHEST
epsilon = 1e-05

def layer_norm(values, gain, bias):
    centre = values - lax.optimization_barrier(jnp.mean(values, axis=-1, keepdims=True))
    spread = lax.optimization_barrier(jnp.mean(centre * centre, axis=-1, keepdims=True))
    return centre * lax.rsqrt(spread + epsilon) * gain + bias

def forward(inputs, length, gain_one, bias_one, w_qkv, w_conv, w_out, gain_two, bias_two, w_up, w_down):
    total = inputs.shape[0]
    width = inputs.shape[1]
    position = jnp.arange(total, dtype=jnp.int32)
    valid = (position < length).astype(inputs.dtype)
    h_one = low(layer_norm(inputs, gain_one, bias_one))
    pre = low_back(low(jnp.dot(h_one, w_qkv, precision=highest)))
    padded = jnp.concatenate([jnp.zeros((2, pre.shape[1]), pre.dtype), pre], axis=0)
    conv = w_conv[0] * pre + w_conv[1] * padded[1:total + 1] + w_conv[2] * padded[:total]
    query = low(conv[:, :width]).reshape(total, HEADS, HEAD)
    keys = low(conv[:, width:2 * width]).reshape(total, HEADS, HEAD)
    values = low(conv[:, 2 * width:]).reshape(total, HEADS, HEAD)
    block_rows = min(512, total)
    nblocks = total // block_rows

    def attend(item):
        q_block, q_pos = item
        scores = jnp.einsum('chd,khd->hck', q_block, keys, precision=highest) * 0.125
        scores = low_back(scores)
        allowed = (position[None, :] <= q_pos[:, None]) & (position[None, :] < length)
        scores = jnp.where(allowed[None], scores, -1e+30)
        top = lax.optimization_barrier(jnp.max(scores, axis=-1, keepdims=True))
        expo = jnp.exp(scores - top)
        probs = expo / lax.optimization_barrier(jnp.sum(expo, axis=-1, keepdims=True))
        return jnp.einsum('hck,khd->chd', low(probs), values, precision=highest)
    blocks = lax.map(jax.checkpoint(attend), (query.reshape(nblocks, block_rows, HEADS, HEAD), position.reshape(nblocks, block_rows)))
    attn = low_back(low(blocks.reshape(total, width)))
    y_one = inputs + low_back(jnp.dot(attn, w_out, precision=highest))
    h_two = low(layer_norm(y_one, gain_two, bias_two))
    upper = low_back(jnp.dot(h_two, w_up, precision=highest))
    hidden = low(jnp.square(jnp.maximum(upper, 0.0)))
    return (y_one + jnp.dot(hidden, w_down, precision=highest)) * valid[:, None]

def reference(tokens, cotangent, lengths, ln1_gain, ln1_bias, w_qkv, w_conv, w_out, ln2_gain, ln2_bias, w_up, w_down):
    params = (ln1_gain.astype(jnp.float32), ln1_bias.astype(jnp.float32), w_qkv.astype(jnp.float32), w_conv.astype(jnp.float32), w_out.astype(jnp.float32), ln2_gain.astype(jnp.float32), ln2_bias.astype(jnp.float32), w_up.astype(jnp.float32), w_down.astype(jnp.float32))

    def one_sequence(totals, item):
        seq_tokens, seq_cot, seq_len = item

        def local(inputs, *weights):
            return forward(inputs, seq_len, *weights)
        result, pull = jax.vjp(local, seq_tokens.astype(jnp.float32), *params)
        grads = pull(seq_cot.astype(jnp.float32))
        summed = tuple((acc + g for acc, g in zip(totals, grads[1:])))
        return (summed, (result.astype(jnp.bfloat16), grads[0]))
    start = tuple((jnp.zeros_like(p) for p in params))
    totals, (outputs, input_grads) = lax.scan(one_sequence, start, (tokens, cotangent, lengths))
    return (outputs, input_grads, totals[0], totals[1], totals[2], totals[3], totals[4], totals[5], totals[6], totals[7], totals[8])
```

```python
import functools

import jax
import jax.numpy as jnp
from jax import lax
from jax.experimental import pallas as pl
from jax.experimental.pallas import tpu as pltpu
from jax.sharding import PartitionSpec as P

HEADS = 12
GROUPS = 4
EPS = 1e-05
RIM = 16
MASKED = -1e30
VMEM = 48 * 1024 * 1024
F32 = jnp.float32
BF16 = jnp.bfloat16


def exch(value, axis, mask):
    count = lax.axis_size(axis)
    return lax.ppermute(value, axis, [(i, i ^ mask) for i in range(count)])


def bits(count):
    return [1 << b for b in range(count.bit_length() - 1)]


def at(stack, index):
    return lax.dynamic_index_in_dim(stack, index, 0, keepdims=False)


def flip(stack, index):
    return jnp.stack([at(stack, k ^ index) for k in range(stack.shape[0])])


def gather_bits(value, axis, masks):
    held = value[None]
    for mask in masks:
        held = jnp.concatenate([held, exch(held, axis, mask)])
    return held


def gather_fsdp(value):
    count = lax.axis_size("fsdp")
    return flip(gather_bits(value, "fsdp", bits(count)), lax.axis_index("fsdp"))


def reduce_fsdp(stack):
    held = flip(stack, lax.axis_index("fsdp"))
    for mask in reversed(bits(lax.axis_size("fsdp"))):
        held = held[:mask].astype(F32) + exch(held[mask:].astype(BF16), "fsdp", mask).astype(F32)
    return held[0]


def core_pair(value, core):
    other = exch(value, "ctx", 1)
    first = jnp.where(core == 0, value, other)
    second = jnp.where(core == 0, other, value)
    return jnp.stack([first, second])


def normed_parts(values):
    centre = values - jnp.mean(values, axis=-1, keepdims=True)
    scale = lax.rsqrt(jnp.mean(centre * centre, axis=-1, keepdims=True) + EPS)
    return centre * scale, scale


def norm_back(grad, normed, scale, gain):
    dnorm = grad * gain
    return scale * (
        dnorm
        - jnp.mean(dnorm, axis=-1, keepdims=True)
        - normed * jnp.mean(dnorm * normed, axis=-1, keepdims=True)
    )


def nn(a, b):
    return lax.dot_general(a, b, (((1,), (0,)), ((), ())), preferred_element_type=F32)


def nt(a, b):
    return lax.dot_general(a, b, (((1,), (1,)), ((), ())), preferred_element_type=F32)


def tn(a, b):
    return lax.dot_general(a, b, (((0,), (0,)), ((), ())), preferred_element_type=F32)


def project_kernel(share, hp, hd, rows, sc, left, right, w, taps, gain, bias, h_ref, pre_ref, q_ref, k_ref, kt_ref,
                   v_ref, vt_ref, buf):
    step = pl.program_id(0)
    mine = sc[1]
    length = sc[2]
    gw = hp * hd
    size = share * rows
    parts = []
    for j in range(share):
        k = j ^ mine
        parts.append(jnp.concatenate([left[k, 0], right[k, 0]], axis=1).astype(F32))
    x = jnp.concatenate(parts, axis=0)
    n, _ = normed_parts(x)
    h = (n * gain[...] + bias[...]).astype(BF16)
    h_ref[...] = h
    pre = nn(h, w[...]).astype(BF16)
    pre_ref[...] = pre

    @pl.when(step == 0)
    def _():
        buf[0:8, :] = jnp.zeros((8, 3 * gw), F32)

    buf[8:, :] = pre.astype(F32)
    conv = (
        taps[0:1, :] * buf[8 : 8 + size, :]
        + taps[1:2, :] * buf[7 : 7 + size, :]
        + taps[2:3, :] * buf[6 : 6 + size, :]
    )
    buf[0:8, :] = buf[size : size + 8, :]
    qs = conv[:, :gw].astype(BF16)
    kf = conv[:, gw : 2 * gw]
    vf = conv[:, 2 * gw :]
    q_own = qs[:rows]
    for j in range(1, share):
        q_own = jnp.where(mine == j, qs[j * rows : (j + 1) * rows], q_own)
    q_own = (q_own.astype(F32) * 0.125).astype(BF16)
    lane = lax.broadcasted_iota(jnp.int32, (rows, hd), 1)
    ones = jnp.where(lane == 0, 1.0, 0.0).astype(BF16)
    lane = lax.broadcasted_iota(jnp.int32, (size, hd), 1)
    pos = step * size + lax.broadcasted_iota(jnp.int32, (size, hd), 0)
    mask = jnp.where((lane == 0) & (pos >= length), MASKED, 0.0).astype(BF16)
    ks = kf.astype(BF16)
    vs = vf.astype(BF16)
    kt = kf.T.astype(BF16)
    vt = vf.T.astype(BF16)
    for h in range(hp):
        cols = slice(h * hd, (h + 1) * hd)
        q_ref[h] = jnp.concatenate([q_own[:, cols], ones], axis=1)
        k_ref[h] = jnp.concatenate([ks[:, cols], mask], axis=1)
        v_ref[h] = vs[:, cols]
        kt_ref[h] = kt[cols]
        vt_ref[h] = vt[cols]


def project(scalars, left, right, w, taps, gain, bias, share, hp, hd):
    _, zys, rows, half = left.shape
    width = 2 * half
    gw = hp * hd
    size = share * rows
    total = zys * size
    body = functools.partial(project_kernel, share, hp, hd, rows)
    whole = lambda *shape: pl.BlockSpec(shape, lambda t, sc: (0,) * len(shape))
    piece = pl.BlockSpec((share, 1, rows, half), lambda t, sc: (0, t ^ sc[0], 0, 0))
    return pl.pallas_call(
        body,
        grid_spec=pltpu.PrefetchScalarGridSpec(
            num_scalar_prefetch=1,
            grid=(zys,),
            in_specs=[piece, piece, whole(width, 3 * gw), whole(3, 3 * gw), whole(1, width), whole(1, width)],
            out_specs=[
                pl.BlockSpec((size, width), lambda t, sc: (t, 0)),
                pl.BlockSpec((size, 3 * gw), lambda t, sc: (t, 0)),
                pl.BlockSpec((hp, rows, 2 * hd), lambda t, sc: (0, t, 0)),
                pl.BlockSpec((hp, size, 2 * hd), lambda t, sc: (0, t, 0)),
                pl.BlockSpec((hp, hd, size), lambda t, sc: (0, 0, t)),
                pl.BlockSpec((hp, size, hd), lambda t, sc: (0, t, 0)),
                pl.BlockSpec((hp, hd, size), lambda t, sc: (0, 0, t)),
            ],
            scratch_shapes=[pltpu.VMEM((8 + size, 3 * gw), F32)],
        ),
        out_shape=[
            jax.ShapeDtypeStruct((total, width), BF16),
            jax.ShapeDtypeStruct((total, 3 * gw), BF16),
            jax.ShapeDtypeStruct((hp, zys * rows, 2 * hd), BF16),
            jax.ShapeDtypeStruct((hp, total, 2 * hd), BF16),
            jax.ShapeDtypeStruct((hp, hd, total), BF16),
            jax.ShapeDtypeStruct((hp, total, hd), BF16),
            jax.ShapeDtypeStruct((hp, hd, total), BF16),
        ],
        compiler_params=pltpu.CompilerParams(vmem_limit_bytes=VMEM),
        cost_estimate=pl.CostEstimate(
            flops=2 * total * width * 3 * gw, bytes_accessed=10 * total * width, transcendentals=0
        ),
        name="project",
    )(scalars, left, right, w, taps, gain, bias)


def seen(share, rows, mine, shape):
    key = lax.broadcasted_iota(jnp.int32, shape, 0)
    col = lax.broadcasted_iota(jnp.int32, shape, 1)
    query = jnp.where(col >= rows, share * rows + col - rows, col) + mine * rows
    return key <= query


def attend_kernel(share, rows, sc, q, k, vt, at_ref, o_ref, lse_ref):
    mine = sc[1]
    tile = 2 * rows
    step = share * tile
    hd = vt.shape[1]
    tiles = q.shape[1] // tile
    for t in range(tiles):
        queries = q[0, t * tile : (t + 1) * tile, :]
        top = jnp.full((1, tile), MASKED, F32)
        total = jnp.zeros((1, tile), F32)
        accum = jnp.zeros((hd, tile), F32)
        for j in [t] + list(range(t)):
            scores = nt(k[0, j * step : (j + 1) * step, :], queries)
            if j == t:
                scores = jnp.where(seen(share, rows, mine, scores.shape), scores, MASKED)
            higher = jnp.maximum(top, jnp.max(scores, axis=0, keepdims=True))
            probs = jnp.exp(scores - higher)
            factor = jnp.exp(top - higher)
            total = total * factor + jnp.sum(probs, axis=0, keepdims=True)
            accum = accum * factor + nn(vt[0, :, j * step : (j + 1) * step], probs.astype(BF16))
            top = higher
        out = accum / total
        o_ref[0, :, t * tile : (t + 1) * tile] = out
        lse_ref[0, :, t * tile : (t + 1) * tile] = top + jnp.log(total)
        low = out.astype(BF16)
        at_ref[2 * t] = low[:, :rows]
        at_ref[2 * t + 1] = low[:, rows:]


def attend(scalars, q, k, vt, share, rows):
    hp, own, wide = q.shape
    total = k.shape[1]
    hd = vt.shape[1]
    head = lambda *shape: pl.BlockSpec((1, *shape), lambda h, sc: (h, 0, 0))
    return pl.pallas_call(
        functools.partial(attend_kernel, share, rows),
        grid_spec=pltpu.PrefetchScalarGridSpec(
            num_scalar_prefetch=1,
            grid=(hp,),
            in_specs=[head(own, wide), head(total, wide), head(hd, total)],
            out_specs=[
                pl.BlockSpec((own // rows, hd, rows), lambda h, sc: (0, h, 0)),
                head(hd, own),
                head(1, own),
            ],
        ),
        out_shape=[
            jax.ShapeDtypeStruct((own // rows, hp * hd, rows), BF16),
            jax.ShapeDtypeStruct((hp, hd, own), F32),
            jax.ShapeDtypeStruct((hp, 1, own), F32),
        ],
        compiler_params=pltpu.CompilerParams(vmem_limit_bytes=VMEM),
        cost_estimate=pl.CostEstimate(
            flops=8 * hp * own * total * hd, bytes_accessed=8 * hp * total * wide, transcendentals=hp * own * total
        ),
        name="attend",
    )(scalars, q, k, vt)


def attend_back_kernel(share, rows, sc, q, k, kt, v, dot_ref, o, lse, mine_ref, send_ref, dq_acc, dk_acc, dv_acc):
    mine = sc[1]
    hp, own, _ = q.shape
    hd = v.shape[2]
    total = k.shape[1]
    tile = 2 * rows
    step = share * tile
    tiles = own // tile
    dq_acc[...] = jnp.zeros(dq_acc.shape, F32)
    dk_acc[...] = jnp.zeros(dk_acc.shape, F32)
    dv_acc[...] = jnp.zeros(dv_acc.shape, F32)
    for t in range(tiles):

        def one_head(h, carry, t=t):
            queries = q[h, t * tile : (t + 1) * tile, :]
            chan = pl.ds(pl.multiple_of(h * hd, hd), hd)
            douts = jnp.concatenate([dot_ref[2 * t, chan, :], dot_ref[2 * t + 1, chan, :]], axis=1)
            outs = o[h, :, t * tile : (t + 1) * tile]
            logs = lse[h, :, t * tile : (t + 1) * tile]
            inner = jnp.sum(outs * douts.astype(F32), axis=0, keepdims=True)
            dqt = jnp.zeros((hd, tile), F32)
            for j in [t] + list(range(t)):
                at_j = slice(j * step, (j + 1) * step)
                probs = jnp.exp(nt(k[h, at_j, :], queries) - logs)
                if j == t:
                    probs = jnp.where(seen(share, rows, mine, probs.shape), probs, 0.0)
                dv_acc[h, at_j, :] += nt(probs.astype(BF16), douts)
                dprobs = nn(v[h, at_j, :], douts)
                dscores = (probs * (dprobs - inner)).astype(BF16)
                dk_acc[h, at_j, :] += nn(dscores, queries)[:, :hd]
                dqt += nn(kt[h, :, at_j], dscores)
            dq = (dqt * 0.125).T
            for b in (2 * t, 2 * t + 1):
                at_b = pl.ds(pl.multiple_of((b * share + mine) * rows, rows), rows)
                dq_acc[h, at_b, :] = dq[(b % 2) * rows : (b % 2 + 1) * rows]
            return carry

        lax.fori_loop(0, hp, one_head, 0)

    def pack(b, carry):
        for r in range(share):
            start = (b * share + (mine ^ r)) * rows
            rows_i = pl.ds(pl.multiple_of(start, rows), rows + RIM)
            block = jnp.concatenate(
                [acc[h, rows_i, :] for acc in (dq_acc, dk_acc, dv_acc) for h in range(hp)], axis=1
            )
            if r == 0:
                mine_ref[b] = block
            else:
                send_ref[r - 1, b] = block.astype(BF16)
        return carry

    lax.fori_loop(0, own // rows, pack, 0)


def attend_back(scalars, q, k, kt, v, dout_t, o, lse, share, rows):
    hp, own, wide = q.shape
    total = k.shape[1]
    hd = v.shape[2]
    blocks = own // rows
    whole = lambda a: pl.BlockSpec(a.shape, lambda i, sc: (0,) * a.ndim)
    out_shape = [
        jax.ShapeDtypeStruct((blocks, rows + RIM, 3 * hp * hd), F32),
        jax.ShapeDtypeStruct((share - 1, blocks, rows + RIM, 3 * hp * hd), BF16),
    ]
    args = (q, k, kt, v, dout_t, o, lse)
    return pl.pallas_call(
        functools.partial(attend_back_kernel, share, rows),
        grid_spec=pltpu.PrefetchScalarGridSpec(
            num_scalar_prefetch=1,
            grid=(1,),
            in_specs=[whole(a) for a in args],
            out_specs=[whole(a) for a in out_shape],
            scratch_shapes=[pltpu.VMEM((hp, total + RIM, hd), F32)] * 3,
        ),
        out_shape=out_shape,
        compiler_params=pltpu.CompilerParams(vmem_limit_bytes=VMEM),
        cost_estimate=pl.CostEstimate(
            flops=20 * hp * own * total * hd, bytes_accessed=16 * hp * total * wide, transcendentals=hp * own * total
        ),
        name="attend_back",
    )(scalars, *args)


def project_back_kernel(share, rows, extra, sc, mine_ref, *refs):
    recv = refs[:extra]
    left, right, h_ref, pre_ref, w, taps, gain, bias, dh_ref, dw_ref, small_ref, conv_ref, buf = refs[extra:]
    step = pl.program_id(0)
    total = mine_ref[0]
    for r in recv:
        total = total + r[0, 0].astype(F32)
    buf[...] = total
    now = buf[0:rows, :]
    one = buf[1 : rows + 1, :]
    two = buf[2 : rows + 2, :]
    dpre = (taps[0:1, :] * now + taps[1:2, :] * one + taps[2:3, :] * two).astype(BF16)
    pre = pre_ref[...].astype(F32)
    x = jnp.concatenate([left[0, 0], right[0, 0]], axis=1).astype(F32)
    n, _ = normed_parts(x)
    dh = nt(dpre, w[...])
    dh_ref[0] = dh
    dw = tn(h_ref[...], dpre)
    small = jnp.concatenate(
        [jnp.sum(dh * n, axis=0, keepdims=True), jnp.sum(dh, axis=0, keepdims=True)], axis=0
    )
    conv = jnp.concatenate(
        [jnp.sum(pre * d, axis=0, keepdims=True) for d in (now, one, two)], axis=0
    )

    @pl.when(step == 0)
    def _():
        dw_ref[...] = dw
        small_ref[...] = small
        conv_ref[...] = conv

    @pl.when(step > 0)
    def _():
        dw_ref[...] += dw
        small_ref[...] += small
        conv_ref[...] += conv


def project_back(scalars, mine, recv, left, right, h, pre, w, taps, gain, bias, share, rows):
    blocks, ext, cols = mine.shape
    width = h.shape[1]
    half = width // 2
    extra = len(recv)
    whole = lambda *shape: pl.BlockSpec(shape, lambda t, sc: (0,) * len(shape))
    piece = pl.BlockSpec((1, 1, rows, half), lambda t, sc: (0, t ^ sc[0], 0, 0))
    return pl.pallas_call(
        functools.partial(project_back_kernel, share, rows, extra),
        grid_spec=pltpu.PrefetchScalarGridSpec(
            num_scalar_prefetch=1,
            grid=(blocks,),
            in_specs=[pl.BlockSpec((1, ext, cols), lambda t, sc: (t, 0, 0))]
            + [pl.BlockSpec((1, 1, ext, cols), lambda t, sc: (0, t, 0, 0))] * extra
            + [
                piece,
                piece,
                pl.BlockSpec((rows, width), lambda t, sc: (t * share + sc[1], 0)),
                pl.BlockSpec((rows, cols), lambda t, sc: (t * share + sc[1], 0)),
                whole(width, cols),
                whole(3, cols),
                whole(1, width),
                whole(1, width),
            ],
            out_specs=[
                pl.BlockSpec((1, rows, width), lambda t, sc: (t ^ sc[0], 0, 0)),
                whole(width, cols),
                whole(2, width),
                whole(3, cols),
            ],
            scratch_shapes=[pltpu.VMEM((ext, cols), F32)],
        ),
        out_shape=[
            jax.ShapeDtypeStruct((blocks, rows, width), F32),
            jax.ShapeDtypeStruct((width, cols), F32),
            jax.ShapeDtypeStruct((2, width), F32),
            jax.ShapeDtypeStruct((3, cols), F32),
        ],
        compiler_params=pltpu.CompilerParams(vmem_limit_bytes=VMEM),
        cost_estimate=pl.CostEstimate(
            flops=4 * blocks * rows * width * cols, bytes_accessed=12 * blocks * rows * width, transcendentals=0
        ),
        name="project_back",
    )(scalars, mine, *recv, left, right, h, pre, w, taps, gain, bias)


def per_device(tokens, cotangent, lengths, ln1_gain, ln1_bias, w_qkv, w_conv, w_out, ln2_gain, ln2_bias, w_up, w_down):
    nseq, rows, width = tokens.shape
    half = width // 2
    count = lax.axis_size("ctx")
    parts = lax.axis_size("fsdp")
    rank = lax.axis_index("ctx")
    index = lax.axis_index("fsdp")
    hidden = w_up.shape[1]
    zys = nseq * GROUPS
    share = count // zys
    hp = HEADS // GROUPS
    hd = width // HEADS
    gw = hp * hd
    mine = rank % share
    core = rank % 2
    zy = rank // share
    seq = zy // GROUPS
    group = zy % GROUPS
    bit_b, bit_a, bit_s = share, 2 * share, 4 * share
    share_bits = bits(share)
    positions = rank * rows + jnp.arange(rows, dtype=jnp.int32)
    valid = positions[None, :] < lengths[:, None]
    scalars = jnp.stack([zy, mine, lengths[seq]]).astype(jnp.int32)

    own_seq = at(tokens, seq)
    pair = jnp.stack([own_seq, exch(at(tokens, 1 - seq), "ctx", bit_s)])
    left, right = pair[..., :half], pair[..., half:]
    left = jnp.stack([left, exch(left, "ctx", bit_a)], axis=1)
    right = jnp.stack([right, exch(right, "ctx", bit_b)], axis=1)
    left = jnp.stack([left, exch(left, "ctx", bit_b)], axis=2)
    right = jnp.stack([right, exch(right, "ctx", bit_a)], axis=1)
    left = gather_bits(left.reshape(zys, rows, half), "ctx", share_bits)
    right = gather_bits(right.reshape(zys, rows, half), "ctx", share_bits)

    small = jnp.concatenate([ln1_gain, ln1_bias, ln2_gain, ln2_bias, w_conv.reshape(-1)])
    small = gather_fsdp(small.reshape(1, -1)).reshape(parts, -1).astype(F32)
    own_rows = ln1_gain.shape[0]
    gains = small[:, : 4 * own_rows].reshape(parts, 4, own_rows).transpose(1, 0, 2).reshape(4, 1, width)
    gain_one, bias_one, gain_two, bias_two = gains[0], gains[1], gains[2], gains[3]
    taps = small[:, 4 * own_rows :].reshape(parts, 3, -1).transpose(1, 0, 2).reshape(3, 3, width)
    taps = lax.dynamic_slice_in_dim(taps, group * gw, gw, 2).reshape(3, 3 * gw)
    qkv = lax.dynamic_slice_in_dim(w_qkv.reshape(own_rows, 3, width), group * gw, gw, 2)
    qkv = at(qkv.reshape(2, own_rows // 2, 3 * gw), core)
    qkv = core_pair(gather_fsdp(qkv), core).transpose(1, 0, 2, 3).reshape(width, 3 * gw)
    out_full = gather_fsdp(at(w_out.reshape(2, own_rows // 2, width), core))
    out_full = core_pair(out_full, core).transpose(1, 0, 2, 3).reshape(width, width)
    up_part = lax.dynamic_index_in_dim(
        w_up.reshape(own_rows, parts, 2, hidden // parts // 2), core, 2, keepdims=False
    ).reshape(own_rows, hidden // 2)
    up_part = gather_fsdp(up_part).reshape(width, hidden // 2)
    down_part = at(w_down.reshape(2, hidden // parts // 2, width), core)
    down_part = gather_fsdp(down_part).reshape(hidden // 2, width)

    h_one, pre, q, k, kt, v, vt = project(scalars, left, right, qkv, taps, gain_one, bias_one, share, hp, hd)
    attn_t, o, lse = attend(scalars, q, k, vt, share, rows)
    classes = [[i for i in range(count) if i % share == s] for s in range(share)]
    swap = lambda x: lax.all_to_all(x, "ctx", 0, 0, tiled=True, axis_index_groups=classes)
    attn_t = swap(attn_t).reshape(nseq, width, rows)

    inputs = tokens.astype(F32)
    y_one = inputs + jnp.einsum("sct,cd->std", attn_t, out_full, preferred_element_type=F32)
    normed_two, scale_two = normed_parts(y_one)
    h_two = (normed_two * gain_two + bias_two).astype(BF16).reshape(nseq * rows, width)
    h_pair = jnp.concatenate([h_two, exch(h_two, "ctx", 1)])
    dtop = jnp.where(valid[..., None], cotangent, jnp.zeros_like(cotangent))
    dtop_flat = dtop.reshape(nseq * rows, width)
    dtop_pair = jnp.concatenate([dtop_flat, exch(dtop_flat, "ctx", 1)])
    upper = nn(h_pair, up_part)
    act = jnp.maximum(upper, 0.0)
    r = jnp.square(act).astype(BF16)
    dhidden = nt(dtop_pair, down_part)
    dupper = (dhidden * 2.0 * act).astype(BF16)
    dh_pair = nt(dupper, up_part)
    dh_two = dh_pair[: nseq * rows] + exch(dh_pair[nseq * rows :], "ctx", 1)
    dh_two = dh_two.reshape(nseq, rows, width)
    dy_one = dtop.astype(F32) + norm_back(dh_two, normed_two, scale_two, gain_two)
    small_two = jnp.stack([jnp.sum(dh_two * normed_two, axis=(0, 1)), jnp.sum(dh_two, axis=(0, 1))])
    dy_low = dy_one.astype(BF16)
    dout_t = jnp.einsum("cd,std->sct", out_full, dy_low, preferred_element_type=F32).astype(BF16)
    dout_t = swap(dout_t.reshape(zys, gw, rows))
    y_pair = nn(r, down_part)
    result = y_one + (y_pair[: nseq * rows] + exch(y_pair[nseq * rows :], "ctx", 1)).reshape(nseq, rows, width)
    output = jnp.where(valid[..., None], result, 0.0).astype(BF16)

    grad_down = tn(r, dtop_pair).reshape(parts, hidden // parts // 2, width)
    grad_up = tn(h_pair, dupper).reshape(parts, own_rows, hidden // 2)
    grad_out = jnp.einsum("sct,std->cd", attn_t, dy_low, preferred_element_type=F32)
    grad_out = grad_out.reshape(parts, 2, own_rows // 2, width)
    grad_out = lax.dynamic_index_in_dim(grad_out, core, 1, keepdims=False) + exch(
        lax.dynamic_index_in_dim(grad_out, 1 - core, 1, keepdims=False).astype(BF16), "ctx", 1
    ).astype(F32)

    def reduce_zy(value, b_first):
        rel = flip(value.astype(BF16).reshape(zys, value.shape[0] // zys, value.shape[1]), zy)
        rel = rel.reshape(2, 2, 2, *rel.shape[1:])

        def over_b(x):
            return (x[0].astype(F32) + exch(x[1], "ctx", bit_b).astype(F32)).astype(BF16)

        def over_sa(x):
            total = x[0, 0].astype(F32)
            for s, a in ((0, 1), (1, 0), (1, 1)):
                total = total + exch(x[s, a], "ctx", s * bit_s + a * bit_a).astype(F32)
            return total.astype(BF16)

        if b_first:
            return over_sa(over_b(jnp.moveaxis(rel, 2, 0)))
        return over_b(over_sa(rel))

    def gather_zy(piece, b_first):
        def over_b(x):
            return jnp.stack([x, exch(x, "ctx", bit_b)])

        def over_sa(x):
            return jnp.stack(
                [x] + [exch(x, "ctx", s * bit_s + a * bit_a) for s, a in ((0, 1), (1, 0), (1, 1))]
            )

        if b_first:
            rel = over_sa(over_b(piece))
        else:
            rel = jnp.moveaxis(over_b(over_sa(piece)), 0, 1)
        rel = rel.reshape(zys, *piece.shape)
        return flip(rel, zy).reshape(zys * piece.shape[0], piece.shape[1])

    grad_up = reduce_fsdp(grad_up)
    grad_down = reduce_fsdp(grad_down)
    grad_out = reduce_fsdp(grad_out)
    grad_low = jnp.concatenate([grad_down, grad_out])
    grad_up = gather_zy(reduce_zy(grad_up, True), False)
    grad_low = gather_zy(reduce_zy(grad_low, False), True)
    up_rows = core_pair(grad_up, core).astype(F32)
    up_rows = up_rows.reshape(2, own_rows, parts, hidden // parts // 2).transpose(1, 2, 0, 3)
    w_up_grad = up_rows.reshape(own_rows, hidden)
    low_rows = core_pair(grad_low, core).astype(F32)
    split = hidden // parts // 2
    w_down_grad = low_rows[:, :split].reshape(2 * split, width)
    w_out_grad = low_rows[:, split:].reshape(own_rows, width)

    d_mine, d_send = attend_back(scalars, q, k, kt, v, dout_t, o, lse, share, rows)
    recv = [exch(d_send[s - 1 : s], "ctx", s) for s in range(1, share)]
    dh_rel, dw, small_one, dconv = project_back(
        scalars, d_mine, recv, left, right, h_one, pre, qkv, taps, gain_one, bias_one, share, rows
    )

    def add_over(x, mask):
        return x[0].astype(F32) + exch(x[1].astype(BF16), "ctx", mask).astype(F32)

    dh_rel = dh_rel.reshape(2, 2, 2, rows, width)
    by_a = lambda x: add_over(jnp.moveaxis(x, 1, 0), bit_a)
    d_left, d_right = dh_rel[..., :half], dh_rel[..., half:]
    d_left = by_a(by_a_first := jnp.moveaxis(d_left, 2, 2))
    d_left = add_over(jnp.moveaxis(d_left, 1, 0), bit_b)
    d_right = add_over(jnp.moveaxis(d_right, 2, 0), bit_b)
    d_right = add_over(jnp.moveaxis(d_right, 1, 0), bit_a)
    dh_mine = jnp.concatenate([d_left, d_right], axis=-1)
    dh_other = exch(dh_mine[1].astype(BF16), "ctx", bit_s).astype(F32)
    dh_one = flip(jnp.stack([dh_mine[0], dh_other]), seq)
    normed_one, scale_one = normed_parts(inputs)
    input_grad = dy_one + norm_back(dh_one, normed_one, scale_one, gain_one)

    gains = jnp.concatenate([small_one, small_two * (1.0 / 1.0)]).reshape(4, parts, own_rows)
    gains = gains.transpose(1, 0, 2).reshape(parts, 4 * own_rows)
    convs = lax.dynamic_update_slice_in_dim(
        jnp.zeros((3, 3, width), F32), dconv.reshape(3, 3, gw), group * gw, 2
    )
    convs = convs.reshape(3, parts, 3 * width // parts).transpose(1, 0, 2).reshape(parts, -1)
    tail = jnp.concatenate([gains, convs], axis=1)
    used = tail.shape[1]
    tail_rows = -(-used // (2 * 3 * gw * 8)) * 8
    tail = jnp.pad(tail, ((0, 0), (0, 2 * tail_rows * 3 * gw - used)))
    tail = tail.reshape(parts, 2, tail_rows, 3 * gw)
    block = jnp.concatenate([dw.reshape(parts, 2, own_rows // 2, 3 * gw), tail], axis=2)
    block = lax.dynamic_index_in_dim(block, core, 1, keepdims=False) + exch(
        lax.dynamic_index_in_dim(block, 1 - core, 1, keepdims=False).astype(BF16), "ctx", 1
    ).astype(F32)
    block = reduce_fsdp(block)
    for mask in share_bits[1:] + [bit_s]:
        block = block.astype(BF16)
        block = block.astype(F32) + exch(block, "ctx", mask).astype(F32)
    block = block.astype(BF16)
    cut = block.shape[0] // 2 // 8 * 8
    high, low = block[:cut], block[cut:]
    high = jnp.stack([high, exch(high, "ctx", bit_b)])
    low = jnp.stack([low, exch(low, "ctx", bit_a)])
    high = jnp.stack([high, exch(high, "ctx", bit_a)])
    low = jnp.stack([low, exch(low, "ctx", bit_b)], axis=1)
    rel = jnp.concatenate([high, low], axis=2).reshape(GROUPS, *block.shape)
    full = core_pair(flip(rel, group), core).astype(F32)
    w_qkv_grad = full[:, :, : own_rows // 2].reshape(2, GROUPS, own_rows // 2, 3, gw)
    w_qkv_grad = w_qkv_grad.transpose(0, 2, 3, 1, 4).reshape(own_rows, 3 * width)
    tail = jnp.sum(full[:, :, own_rows // 2 :], axis=1).reshape(-1)[:used]
    gains = tail[: 4 * own_rows].reshape(4, own_rows)
    w_conv_grad = tail[4 * own_rows :].reshape(3, -1)

    return (
        output,
        input_grad,
        gains[0],
        gains[1],
        w_qkv_grad,
        w_conv_grad,
        w_out_grad,
        gains[2],
        gains[3],
        w_up_grad,
        w_down_grad,
    )


def solution(mesh):
    rows = P("fsdp", "ctx", None)
    first = P("fsdp")
    weight = P("fsdp", None)
    second = P(None, "fsdp")
    in_specs = (rows, rows, first, first, first, weight, second, weight, first, first, weight, weight)
    out_specs = (rows, rows, first, first, weight, second, weight, first, first, weight, weight)
    return jax.shard_map(per_device, mesh=mesh, in_specs=in_specs, out_specs=out_specs, check_vma=False)
```

```python
import functools

import jax
import jax.numpy as jnp
from jax import lax
from jax.experimental import pallas as pl
from jax.experimental.pallas import tpu as pltpu
from jax.sharding import PartitionSpec as P

HEADS = 12
GROUPS = 4
EPS = 1e-05
RIM = 16
PIECES = 8
TAIL = 16
MASKED = -1e30
VMEM = 48 * 1024 * 1024
F32 = jnp.float32
BF16 = jnp.bfloat16
FREE = pl.CostEstimate(flops=0, bytes_accessed=0, transcendentals=0)


def exch(value, axis, mask):
    count = lax.axis_size(axis)
    return lax.ppermute(value, axis, [(i, i ^ mask) for i in range(count)])


def bits(count):
    return [1 << b for b in range(count.bit_length() - 1)]


def at(stack, index):
    return lax.dynamic_index_in_dim(stack, index, 0, keepdims=False)


def flip(stack, index):
    return jnp.stack([at(stack, k ^ index) for k in range(stack.shape[0])])


def gather_bits(value, axis, masks):
    held = value[None]
    for mask in masks:
        held = jnp.concatenate([held, exch(held, axis, mask)])
    return held


def gather_fsdp(value):
    count = lax.axis_size("fsdp")
    return flip(gather_bits(value, "fsdp", bits(count)), lax.axis_index("fsdp"))


def gather_list(value, axis, masks):
    held = [value]
    for mask in masks:
        held.append(exch(held[0] if len(held) == 1 else jnp.concatenate(held), axis, mask))
    return held


def after(value, *others):
    return lax.optimization_barrier((value, *others))[0]


class Order:
    def __init__(self):
        self.last = None

    def __call__(self, *values):
        if self.last is not None:
            values = lax.optimization_barrier((*values, self.last))[:-1]
        return values if len(values) > 1 else values[0]

    def mark(self, value):
        self.last = value
        return value


def normed_parts(values):
    centre = values - jnp.mean(values, axis=-1, keepdims=True)
    scale = lax.rsqrt(jnp.mean(centre * centre, axis=-1, keepdims=True) + EPS)
    return centre * scale, scale


def norm_back(grad, normed, scale, gain):
    dnorm = grad * gain
    return scale * (
        dnorm
        - jnp.mean(dnorm, axis=-1, keepdims=True)
        - normed * jnp.mean(dnorm * normed, axis=-1, keepdims=True)
    )


def nn(a, b):
    return lax.dot_general(a, b, (((1,), (0,)), ((), ())), preferred_element_type=F32)


def nt(a, b):
    return lax.dot_general(a, b, (((1,), (1,)), ((), ())), preferred_element_type=F32)


def tn(a, b):
    return lax.dot_general(a, b, (((0,), (0,)), ((), ())), preferred_element_type=F32)


def piece_copies(lists, scratch, sems, index, core, take=None, cols=None):
    copies = []
    cores = len(lists)
    for r, pieces in enumerate(lists):
        k = 0
        for stack in pieces:
            for i in range(stack.shape[0]):
                first, size = take or (0, stack.shape[1])
                part = (core ^ r) if cores == 2 else 0
                start = pl.multiple_of(((index ^ k) * cores + part) * size, size)
                target = scratch.at[pl.ds(start, size)] if cols is None else scratch.at[pl.ds(start, size), cols]
                source = stack.at[i, pl.ds(first, size)]
                copies.append(pltpu.make_async_copy(source, target, sems.at[len(copies)]))
                k += 1
    return copies


def split_lists(refs, counts):
    lists, at_ref = [], 0
    for n in counts:
        lists.append(refs[at_ref : at_ref + n])
        at_ref += n
    return lists, refs[at_ref:]


ANY = pl.BlockSpec(memory_space=pltpu.HBM)


def qkv_part_kernel(groups, gw, sc, w, out):
    group = sc[4]
    for j in range(3):
        picked = w[:, j * groups * gw : j * groups * gw + gw]
        for g in range(1, groups):
            start = (j * groups + g) * gw
            picked = jnp.where(group == g, w[:, start : start + gw], picked)
        out[:, j * gw : (j + 1) * gw] = picked


def qkv_part(scalars, w_qkv, gw):
    rows, cols = w_qkv.shape
    return pl.pallas_call(
        functools.partial(qkv_part_kernel, GROUPS, gw),
        grid_spec=pltpu.PrefetchScalarGridSpec(
            num_scalar_prefetch=1,
            grid=(1,),
            in_specs=[pl.BlockSpec((rows // 2, cols), lambda i, sc: (sc[3], 0))],
            out_specs=pl.BlockSpec((rows // 2, 3 * gw), lambda i, sc: (0, 0)),
        ),
        out_shape=jax.ShapeDtypeStruct((rows // 2, 3 * gw), BF16),
        compiler_params=pltpu.CompilerParams(vmem_limit_bytes=VMEM),
        cost_estimate=FREE,
        name="qkv_part",
    )(scalars, w_qkv)


def up_part_kernel(sc, w, out):
    out[...] = w[...]


def up_part(scalars, w_up, parts):
    rows, cols = w_up.shape
    split = cols // parts // 2
    if split % 128:
        picked = lax.dynamic_index_in_dim(w_up.reshape(rows, parts, 2, split), scalars[3], 2, keepdims=False)
        return picked.reshape(rows, cols // 2)
    return pl.pallas_call(
        up_part_kernel,
        grid_spec=pltpu.PrefetchScalarGridSpec(
            num_scalar_prefetch=1,
            grid=(parts,),
            in_specs=[pl.BlockSpec((rows, split), lambda p, sc: (0, 2 * p + sc[3]))],
            out_specs=pl.BlockSpec((rows, split), lambda p, sc: (0, p)),
        ),
        out_shape=jax.ShapeDtypeStruct((rows, cols // 2), BF16),
        compiler_params=pltpu.CompilerParams(vmem_limit_bytes=VMEM),
        cost_estimate=FREE,
        name="up_part",
    )(scalars, w_up)


def rest_part_kernel(parts, sc, w_up, w_down, w_out, out, sems):
    core = sc[3]
    own, cols = w_up.shape
    split = cols // parts // 2
    copies = []
    for p in range(parts):
        source = w_up.at[:, pl.ds(pl.multiple_of((2 * p + core) * split, split), split)]
        copies.append(pltpu.make_async_copy(source, out.at[0, pl.ds(p * own, own)], sems.at[p]))
    source = w_down.at[pl.ds(pl.multiple_of(core * split, split), split)]
    copies.append(pltpu.make_async_copy(source, out.at[0, pl.ds(parts * own, split)], sems.at[parts]))
    source = w_out.at[pl.ds(pl.multiple_of(core * (own // 2), own // 2), own // 2)]
    copies.append(pltpu.make_async_copy(source, out.at[0, pl.ds(parts * own + split, own // 2)], sems.at[parts + 1]))
    for copy in copies:
        copy.start()
    for copy in copies:
        copy.wait()


def rest_part(scalars, w_up, w_down, w_out, parts):
    own, cols = w_up.shape
    split = cols // parts // 2
    rows = parts * own + split + own // 2
    return pl.pallas_call(
        functools.partial(rest_part_kernel, parts),
        grid_spec=pltpu.PrefetchScalarGridSpec(
            num_scalar_prefetch=1,
            grid=(1,),
            in_specs=[ANY] * 3,
            out_specs=ANY,
            scratch_shapes=[pltpu.SemaphoreType.DMA((parts + 2,))],
        ),
        out_shape=jax.ShapeDtypeStruct((1, rows, split), BF16),
        compiler_params=pltpu.CompilerParams(vmem_limit_bytes=VMEM),
        cost_estimate=FREE,
        name="rest_part",
    )(scalars, w_up, w_down, w_out)


def project_kernel(share, hp, hd, rows, per, shares, counts, sc, *refs):
    (left, right), refs = split_lists(refs, (len(shares), len(shares)))
    taps, gain, bias = refs[:3]
    lists, refs = split_lists(refs[3:], counts)
    h_ref, pre_ref, q_ref, k_ref, kt_ref, v_ref, vt_ref, buf, w, sems = refs
    step = pl.program_id(0)

    @pl.when(step == 0)
    def _():
        copies = piece_copies(lists, w, sems, sc[5], sc[3])
        for copy in copies:
            copy.start()
        for copy in copies:
            copy.wait()

    mine = sc[1]
    length = sc[2]
    gw = hp * hd
    size = per * share * rows
    parts = []
    for z in range(per):
        at_z = z ^ (sc[0] % per)
        pieces = []
        for refs_l, refs_r in zip(left, right):
            pieces += [jnp.concatenate([refs_l[i, at_z], refs_r[i, at_z]], axis=1) for i in range(refs_l.shape[0])]
        for j in range(share):
            picked = pieces[0]
            for k in range(1, share):
                picked = jnp.where((j ^ mine) == k, pieces[k], picked)
            parts.append(picked.astype(F32))
    x = jnp.concatenate(parts, axis=0)
    n, _ = normed_parts(x)
    h = (n * gain[...] + bias[...]).astype(BF16)
    h_ref[...] = h
    pre = nn(h, w[...]).astype(BF16)
    pre_ref[...] = pre

    @pl.when(step == 0)
    def _():
        buf[0:8, :] = jnp.zeros((8, 3 * gw), F32)

    buf[8:, :] = pre.astype(F32)
    conv = (
        taps[0:1, :] * buf[8 : 8 + size, :]
        + taps[1:2, :] * buf[7 : 7 + size, :]
        + taps[2:3, :] * buf[6 : 6 + size, :]
    )
    buf[0:8, :] = buf[size : size + 8, :]
    qs = conv[:, :gw].astype(BF16)
    kf = conv[:, gw : 2 * gw]
    vf = conv[:, 2 * gw :]
    q_own = []
    for z in range(per):
        start = z * share * rows
        picked = qs[start : start + rows]
        for j in range(1, share):
            picked = jnp.where(mine == j, qs[start + j * rows : start + (j + 1) * rows], picked)
        q_own.append(picked)
    q_own = (jnp.concatenate(q_own, axis=0).astype(F32) * 0.125).astype(BF16)
    lane = lax.broadcasted_iota(jnp.int32, (per * rows, hd), 1)
    ones = jnp.where(lane == 0, 1.0, 0.0).astype(BF16)
    lane = lax.broadcasted_iota(jnp.int32, (size, hd), 1)
    pos = step * size + lax.broadcasted_iota(jnp.int32, (size, hd), 0)
    mask = jnp.where((lane == 0) & (pos >= length), MASKED, 0.0).astype(BF16)
    ks = kf.astype(BF16)
    vs = vf.astype(BF16)
    kt = kf.T.astype(BF16)
    vt = vf.T.astype(BF16)
    for h in range(hp):
        cols = slice(h * hd, (h + 1) * hd)
        q_ref[h] = jnp.concatenate([q_own[:, cols], ones], axis=1)
        k_ref[h] = jnp.concatenate([ks[:, cols], mask], axis=1)
        v_ref[h] = vs[:, cols]
        kt_ref[h] = kt[cols]
        vt_ref[h] = vt[cols]


def project(scalars, left, right, w_lists, taps, gain, bias, share, hp, hd):
    counts = [len(pieces) for pieces in w_lists]
    flat = [piece for pieces in w_lists for piece in pieces]
    _, zys, rows, half = left[0].shape
    width = 2 * half
    gw = hp * hd
    per = 2
    total = zys * share * rows
    size = per * share * rows
    shares = [a.shape[0] for a in left]
    body = functools.partial(project_kernel, share, hp, hd, rows, per, shares, counts)
    whole = lambda *shape: pl.BlockSpec(shape, lambda t, sc: (0,) * len(shape))
    pieces = [pl.BlockSpec((n, per, rows, half), lambda t, sc: (0, t ^ (sc[0] // per), 0, 0)) for n in shares]
    return pl.pallas_call(
        body,
        grid_spec=pltpu.PrefetchScalarGridSpec(
            num_scalar_prefetch=1,
            grid=(zys // per,),
            in_specs=pieces * 2 + [whole(3, 3 * gw), whole(1, width), whole(1, width)] + [ANY] * len(flat),
            out_specs=[
                pl.BlockSpec((size, width), lambda t, sc: (t, 0)),
                pl.BlockSpec((size, 3 * gw), lambda t, sc: (t, 0)),
                pl.BlockSpec((hp, per * rows, 2 * hd), lambda t, sc: (0, t, 0)),
                pl.BlockSpec((hp, size, 2 * hd), lambda t, sc: (0, t, 0)),
                pl.BlockSpec((hp, hd, size), lambda t, sc: (0, 0, t)),
                pl.BlockSpec((hp, size, hd), lambda t, sc: (0, t, 0)),
                pl.BlockSpec((hp, hd, size), lambda t, sc: (0, 0, t)),
            ],
            scratch_shapes=[
                pltpu.VMEM((8 + size, 3 * gw), F32),
                pltpu.VMEM((width, 3 * gw), BF16),
                pltpu.SemaphoreType.DMA((2 * PIECES,)),
            ],
        ),
        out_shape=[
            jax.ShapeDtypeStruct((total, width), BF16),
            jax.ShapeDtypeStruct((total, 3 * gw), BF16),
            jax.ShapeDtypeStruct((hp, zys * rows, 2 * hd), BF16),
            jax.ShapeDtypeStruct((hp, total, 2 * hd), BF16),
            jax.ShapeDtypeStruct((hp, hd, total), BF16),
            jax.ShapeDtypeStruct((hp, total, hd), BF16),
            jax.ShapeDtypeStruct((hp, hd, total), BF16),
        ],
        compiler_params=pltpu.CompilerParams(vmem_limit_bytes=VMEM),
        cost_estimate=FREE,
        name="project",
    )(scalars, *left, *right, taps, gain, bias, *flat)


def seen(share, rows, mine, shape):
    key = lax.broadcasted_iota(jnp.int32, shape, 0)
    col = lax.broadcasted_iota(jnp.int32, shape, 1)
    query = jnp.where(col >= rows, share * rows + col - rows, col) + mine * rows
    return key <= query


def attend_kernel(share, rows, sc, q, k, vt, at_ref, o_ref, lse_ref):
    mine = sc[1]
    tile = 2 * rows
    step = share * tile
    hd = vt.shape[1]
    tiles = q.shape[1] // tile
    for t in range(tiles):
        queries = q[0, t * tile : (t + 1) * tile, :]
        top = jnp.full((1, tile), MASKED, F32)
        total = jnp.zeros((1, tile), F32)
        accum = jnp.zeros((hd, tile), F32)
        for j in [t] + list(range(t)):
            scores = nt(k[0, j * step : (j + 1) * step, :], queries)
            if j == t:
                scores = jnp.where(seen(share, rows, mine, scores.shape), scores, MASKED)
            higher = jnp.maximum(top, jnp.max(scores, axis=0, keepdims=True))
            probs = jnp.exp(scores - higher)
            factor = jnp.exp(top - higher)
            total = total * factor + jnp.sum(probs, axis=0, keepdims=True)
            accum = accum * factor + nn(vt[0, :, j * step : (j + 1) * step], probs.astype(BF16))
            top = higher
        out = accum / total
        o_ref[0, :, t * tile : (t + 1) * tile] = out
        lse_ref[0, :, t * tile : (t + 1) * tile] = top + jnp.log(total)
        low = out.astype(BF16)
        at_ref[2 * t] = low[:, :rows]
        at_ref[2 * t + 1] = low[:, rows:]


def attend(scalars, q, k, vt, share, rows):
    hp, own, wide = q.shape
    total = k.shape[1]
    hd = vt.shape[1]
    head = lambda *shape: pl.BlockSpec((1, *shape), lambda h, sc: (h, 0, 0))
    return pl.pallas_call(
        functools.partial(attend_kernel, share, rows),
        grid_spec=pltpu.PrefetchScalarGridSpec(
            num_scalar_prefetch=1,
            grid=(hp,),
            in_specs=[head(own, wide), head(total, wide), head(hd, total)],
            out_specs=[
                pl.BlockSpec((own // rows, hd, rows), lambda h, sc: (0, h, 0)),
                head(hd, own),
                head(1, own),
            ],
        ),
        out_shape=[
            jax.ShapeDtypeStruct((own // rows, hp * hd, rows), BF16),
            jax.ShapeDtypeStruct((hp, hd, own), F32),
            jax.ShapeDtypeStruct((hp, 1, own), F32),
        ],
        compiler_params=pltpu.CompilerParams(vmem_limit_bytes=VMEM),
        cost_estimate=FREE,
        name="attend",
    )(scalars, q, k, vt)


def attend_back_kernel(share, rows, sc, q, k, kt, v, dot_ref, o, lse, mine_ref, send_ref, dq_acc, dk_acc, dv_acc):
    mine = sc[1]
    own = q.shape[1]
    hd = v.shape[2]
    tile = 2 * rows
    step = share * tile
    tiles = own // tile
    total = tiles * step
    dq_acc[...] = jnp.zeros(dq_acc.shape, F32)
    dk_acc[total:, :] = jnp.zeros((RIM, hd), F32)
    dv_acc[total:, :] = jnp.zeros((RIM, hd), F32)
    for t in reversed(range(tiles)):
        queries = q[0, t * tile : (t + 1) * tile, :]
        douts = jnp.concatenate([dot_ref[2 * t], dot_ref[2 * t + 1]], axis=1)
        outs = o[0, :, t * tile : (t + 1) * tile]
        logs = lse[0, :, t * tile : (t + 1) * tile]
        inner = jnp.sum(outs * douts.astype(F32), axis=0, keepdims=True)
        dqt = jnp.zeros((hd, tile), F32)
        for j in reversed(range(t + 1)):
            at_j = slice(j * step, (j + 1) * step)
            probs = jnp.exp(nt(k[0, at_j, :], queries) - logs)
            if j == t:
                probs = jnp.where(seen(share, rows, mine, probs.shape), probs, 0.0)
            dv = nt(probs.astype(BF16), douts)
            dprobs = nn(v[0, at_j, :], douts)
            dscores = (probs * (dprobs - inner)).astype(BF16)
            dk = nn(dscores, queries)[:, :hd]
            if t == tiles - 1:
                dv_acc[at_j, :] = dv
                dk_acc[at_j, :] = dk
            else:
                dv_acc[at_j, :] += dv
                dk_acc[at_j, :] += dk
            dqt += nn(kt[0, :, at_j], dscores)
        dq = (dqt * 0.125).T
        for b in (2 * t, 2 * t + 1):
            at_b = pl.ds(pl.multiple_of((b * share + mine) * rows, rows), rows)
            dq_acc[at_b, :] = dq[(b % 2) * rows : (b % 2 + 1) * rows]
    for b in range(own // rows):
        for r in range(share):
            start = (b * share + (mine ^ r)) * rows
            rows_i = pl.ds(pl.multiple_of(start, rows), rows + RIM)
            block = jnp.concatenate([acc[rows_i, :] for acc in (dq_acc, dk_acc, dv_acc)], axis=1)
            if r == 0:
                mine_ref[b] = block
            else:
                send_ref[r - 1, b] = block.astype(BF16)


def attend_back(scalars, head, q, k, kt, v, dout_t, o, lse, share, rows):
    hp, own, wide = q.shape
    total = k.shape[1]
    hd = v.shape[2]
    blocks = own // rows
    whole = lambda a: pl.BlockSpec(a.shape, lambda i, sc: (0,) * a.ndim)
    one = lambda a: pl.BlockSpec((1, *a.shape[1:]), lambda i, sc: (head, 0, 0))
    out_shape = [
        jax.ShapeDtypeStruct((blocks, rows + RIM, 3 * hd), F32),
        jax.ShapeDtypeStruct((share - 1, blocks, rows + RIM, 3 * hd), BF16),
    ]
    return pl.pallas_call(
        functools.partial(attend_back_kernel, share, rows),
        grid_spec=pltpu.PrefetchScalarGridSpec(
            num_scalar_prefetch=1,
            grid=(1,),
            in_specs=[one(q), one(k), one(kt), one(v)]
            + [pl.BlockSpec((blocks, hd, rows), lambda i, sc: (0, head, 0)), one(o), one(lse)],
            out_specs=[whole(a) for a in out_shape],
            scratch_shapes=[pltpu.VMEM((total + RIM, hd), F32)] * 3,
        ),
        out_shape=out_shape,
        compiler_params=pltpu.CompilerParams(vmem_limit_bytes=VMEM),
        cost_estimate=FREE,
        name="attend_back",
    )(scalars, q, k, kt, v, dout_t, o, lse)


def project_back_kernel(share, rows, heads, parts, counts, sc, *refs):
    (kept, recv), refs = split_lists(refs, (heads, heads * (share - 1)))
    left, right, h_ref, pre_ref, taps, small_two = refs[:6]
    lists, refs = split_lists(refs[6:], counts)
    left_keep, left_send, right_keep, right_send, dw_keep, dw_send, buf, w, dw_acc, small_acc, conv_acc, sems = refs
    step = pl.program_id(0)
    steps = pl.num_programs(0)
    width = w.shape[0]
    half = width // 2

    @pl.when(step == 0)
    def _():
        copies = piece_copies(lists, w, sems, sc[5], sc[3])
        for copy in copies:
            copy.start()
        dw_acc[...] = jnp.zeros(dw_acc.shape, F32)
        small_acc[...] = jnp.zeros(small_acc.shape, F32)
        conv_acc[...] = jnp.zeros(conv_acc.shape, F32)
        for copy in copies:
            copy.wait()

    hd = kept[0].shape[2] // 3
    per = kept[0].shape[0]
    now, one, two, x = [], [], [], []
    for z in range(per):
        for i in range(heads):
            total = kept[i][z]
            for r in recv[i * (share - 1) : (i + 1) * (share - 1)]:
                total = total + r[0, z].astype(F32)
            for j in range(3):
                start = (j * heads + i) * hd
                buf[z, :, start : start + hd] = total[:, j * hd : (j + 1) * hd]
        now.append(buf[z, 0:rows, :])
        one.append(buf[z, 1 : rows + 1, :])
        two.append(buf[z, 2 : rows + 2, :])
        at_z = z ^ (sc[0] % per)
        x.append(jnp.concatenate([left[0, at_z], right[0, at_z]], axis=1))
    now, one, two, x = (jnp.concatenate(v, axis=0) for v in (now, one, two, x))
    dpre = (taps[0:1, :] * now + taps[1:2, :] * one + taps[2:3, :] * two).astype(BF16)
    pre = jnp.concatenate([pre_ref[z, 0] for z in range(per)], axis=0).astype(F32)
    n, _ = normed_parts(x.astype(F32))
    dh = nt(dpre, w[...])
    for z in range(per):
        k = (per * step + z) ^ sc[0]
        bit_s, bit_a, bit_b = k // 4, k // 2 % 2, k % 2
        dh_z = dh[z * rows : (z + 1) * rows]
        to_left, to_right = 2 * bit_b + bit_s, 2 * bit_a + bit_s

        @pl.when(bit_a == 0)
        def _(dh_z=dh_z, to_left=to_left):
            left_keep[to_left] = dh_z[:, :half]

        @pl.when(bit_a == 1)
        def _(dh_z=dh_z, to_left=to_left):
            left_send[to_left] = dh_z[:, :half].astype(BF16)

        @pl.when(bit_b == 0)
        def _(dh_z=dh_z, to_right=to_right):
            right_keep[to_right] = dh_z[:, half:]

        @pl.when(bit_b == 1)
        def _(dh_z=dh_z, to_right=to_right):
            right_send[to_right] = dh_z[:, half:].astype(BF16)

    h = jnp.concatenate([h_ref[z, 0] for z in range(per)], axis=0)
    dw_acc[...] += tn(h, dpre)
    small_acc[0:1, :] += jnp.sum(dh * n, axis=0, keepdims=True)
    small_acc[1:2, :] += jnp.sum(dh, axis=0, keepdims=True)
    conv_acc[0:3, :] += jnp.concatenate([jnp.sum(pre * d, axis=0, keepdims=True) for d in (now, one, two)], axis=0)

    @pl.when(step == steps - 1)
    def _():
        core = sc[3]
        own = width // parts
        high = own // 2
        cols = dw_acc.shape[1]
        small_acc[2:4, :] = small_two[...]
        for p in range(parts):
            gains = small_acc[0:4, p * own : (p + 1) * own]
            gains = jnp.concatenate([gains, jnp.zeros((4, cols - own), F32)], axis=1)
            tail = jnp.concatenate([gains, conv_acc[0:3, :], jnp.zeros((TAIL - 7, cols), F32)], axis=0)
            keep = pl.ds(pl.multiple_of((2 * p + core) * high, high), high)
            send = pl.ds(pl.multiple_of((2 * p + 1 - core) * high, high), high)
            dw_keep[p, 0:high, :] = dw_acc[keep, :]
            dw_keep[p, high : high + TAIL, :] = tail
            dw_send[p, 0:high, :] = dw_acc[send, :].astype(BF16)
            dw_send[p, high : high + TAIL, :] = tail.astype(BF16)


def project_back(scalars, mine, recv, left, right, h, pre, taps, small_two, w_lists, share, rows, parts):
    counts = [len(pieces) for pieces in w_lists]
    flat = [piece for pieces in w_lists for piece in pieces]
    blocks, ext, thin = mine[0].shape
    heads = len(mine)
    cols = heads * thin
    width = h.shape[1]
    half = width // 2
    high = width // parts // 2
    whole = lambda *shape: pl.BlockSpec(shape, lambda t, sc: (0,) * len(shape))
    per = blocks // 2
    piece = pl.BlockSpec((1, per, rows, half), lambda t, sc: (0, t ^ (sc[0] // per), 0, 0))
    by_block = lambda a: a.reshape(blocks, share, rows, a.shape[1])
    out_shape = [
        jax.ShapeDtypeStruct((blocks // 2, rows, half), F32),
        jax.ShapeDtypeStruct((blocks // 2, rows, half), BF16),
        jax.ShapeDtypeStruct((blocks // 2, rows, half), F32),
        jax.ShapeDtypeStruct((blocks // 2, rows, half), BF16),
        jax.ShapeDtypeStruct((parts, high + TAIL, cols), F32),
        jax.ShapeDtypeStruct((parts, high + TAIL, cols), BF16),
    ]
    return pl.pallas_call(
        functools.partial(project_back_kernel, share, rows, heads, parts, counts),
        grid_spec=pltpu.PrefetchScalarGridSpec(
            num_scalar_prefetch=1,
            grid=(blocks // per,),
            in_specs=[pl.BlockSpec((per, ext, thin), lambda t, sc: (t, 0, 0))] * heads
            + [pl.BlockSpec((1, per, ext, thin), lambda t, sc: (0, t, 0, 0))] * len(recv)
            + [
                piece,
                piece,
                pl.BlockSpec((per, 1, rows, width), lambda t, sc: (t, sc[1], 0, 0)),
                pl.BlockSpec((per, 1, rows, cols), lambda t, sc: (t, sc[1], 0, 0)),
                whole(3, cols),
                whole(2, width),
            ]
            + [ANY] * len(flat),
            out_specs=[whole(*o.shape) for o in out_shape],
            scratch_shapes=[
                pltpu.VMEM((per, ext, cols), F32),
                pltpu.VMEM((width, cols), BF16),
                pltpu.VMEM((width, cols), F32),
                pltpu.VMEM((8, width), F32),
                pltpu.VMEM((8, cols), F32),
                pltpu.SemaphoreType.DMA((2 * PIECES,)),
            ],
        ),
        out_shape=out_shape,
        compiler_params=pltpu.CompilerParams(vmem_limit_bytes=VMEM),
        cost_estimate=FREE,
        name="project_back",
    )(scalars, *mine, *recv, left, right, by_block(h), by_block(pre), taps, small_two, *flat)


def mix_kernel(counts, sc, attn, tokens, gain, bias, *refs):
    lists, refs = split_lists(refs, counts)
    y_ref, h_ref, w, sems = refs
    copies = piece_copies(lists, w, sems, sc[5], sc[3])
    for copy in copies:
        copy.start()
    for copy in copies:
        copy.wait()
    nseq, rows, width = tokens.shape
    parts = h_ref.shape[0]
    own = width // parts
    for i in range(nseq):
        y = tokens[i].astype(F32) + tn(attn[i], w[...])
        y_ref[i] = y
        n, _ = normed_parts(y)
        h = (n * gain[...] + bias[...]).astype(BF16)
        for p in range(parts):
            h_ref[p, i * rows : (i + 1) * rows, :] = h[:, p * own : (p + 1) * own]


def mix(scalars, attn, tokens, gain, bias, w_lists, parts):
    counts = [len(pieces) for pieces in w_lists]
    flat = [piece for pieces in w_lists for piece in pieces]
    nseq, rows, width = tokens.shape
    whole = lambda a: pl.BlockSpec(a.shape, lambda i, sc: (0,) * a.ndim)
    out_shape = [
        jax.ShapeDtypeStruct((nseq, rows, width), F32),
        jax.ShapeDtypeStruct((parts, nseq * rows, width // parts), BF16),
    ]
    args = (attn, tokens, gain, bias)
    return pl.pallas_call(
        functools.partial(mix_kernel, counts),
        grid_spec=pltpu.PrefetchScalarGridSpec(
            num_scalar_prefetch=1,
            grid=(1,),
            in_specs=[whole(a) for a in args] + [ANY] * len(flat),
            out_specs=[whole(a) for a in out_shape],
            scratch_shapes=[pltpu.VMEM((width, width), BF16), pltpu.SemaphoreType.DMA((2 * PIECES,))],
        ),
        out_shape=out_shape,
        compiler_params=pltpu.CompilerParams(vmem_limit_bytes=VMEM),
        cost_estimate=FREE,
        name="mix",
    )(scalars, *args, *flat)


def feed_kernel(counts, merged, sc, h_own, h_other, d_own, d_other, *refs):
    (ups, downs), refs = split_lists(refs, counts)
    r_ref, du_ref, dh_keep, dh_send, y_keep, y_send, up, down, sems = refs
    parts, rows, own = h_own.shape
    split = r_ref.shape[2]
    copies, later = [], []
    if merged:
        for p in range(parts):
            take = (p * own, own)
            cols = pl.ds(p * split, split)
            copies += piece_copies([ups], up, sems.at[0, p], sc[5], 0, take, cols)
        later += piece_copies([ups], down, sems.at[1, 0], sc[5], 0, (parts * own, split))
    else:
        copies += piece_copies([ups], up, sems.at[0, 0], sc[5], 0)
        later += piece_copies([downs], down, sems.at[1, 0], sc[5], 0)
    for copy in copies + later:
        copy.start()
    for copy in copies:
        copy.wait()
    h = jnp.concatenate(
        [jnp.concatenate([ref[p] for p in range(parts)], axis=1) for ref in (h_own, h_other)], axis=0
    )
    d = jnp.concatenate([d_own[...], d_other[...]], axis=0)
    dh = None
    y = None
    for p in range(parts):
        cols = slice(p * split, (p + 1) * split)
        act = jnp.maximum(nn(h, up[:, cols]), 0.0)
        r = jnp.square(act).astype(BF16)
        r_ref[p] = r
        if p == 0:
            for copy in later:
                copy.wait()
        dr = nt(d, down[cols, :])
        du = (dr * 2.0 * act).astype(BF16)
        du_ref[:, cols] = du
        term = nt(du, up[:, cols])
        dh = term if dh is None else dh + term
        term = nn(r, down[cols, :])
        y = term if y is None else y + term
    dh_keep[...] = dh[:rows]
    dh_send[...] = dh[rows:].astype(BF16)
    y_keep[...] = y[:rows]
    y_send[...] = y[rows:].astype(BF16)


def feed(scalars, h_own, h_other, d_own, d_other, ups, downs, split):
    parts, rows, own = h_own.shape
    width = parts * own
    cols = split * parts
    whole = lambda a: pl.BlockSpec(a.shape, lambda i, sc: (0,) * a.ndim)
    out_shape = [
        jax.ShapeDtypeStruct((parts, 2 * rows, split), BF16),
        jax.ShapeDtypeStruct((2 * rows, cols), BF16),
        jax.ShapeDtypeStruct((rows, width), F32),
        jax.ShapeDtypeStruct((rows, width), BF16),
        jax.ShapeDtypeStruct((rows, width), F32),
        jax.ShapeDtypeStruct((rows, width), BF16),
    ]
    args = (h_own, h_other, d_own, d_other)
    return pl.pallas_call(
        functools.partial(feed_kernel, (len(ups), len(downs)), not downs),
        grid_spec=pltpu.PrefetchScalarGridSpec(
            num_scalar_prefetch=1,
            grid=(1,),
            in_specs=[whole(a) for a in args] + [ANY] * (len(ups) + len(downs)),
            out_specs=[whole(a) for a in out_shape],
            scratch_shapes=[
                pltpu.VMEM((width, cols), BF16),
                pltpu.VMEM((cols, width), BF16),
                pltpu.SemaphoreType.DMA((2, parts, PIECES)),
            ],
        ),
        out_shape=out_shape,
        compiler_params=pltpu.CompilerParams(vmem_limit_bytes=VMEM),
        cost_estimate=FREE,
        name="feed",
    )(scalars, *args, *ups, *downs)


def mix_back_kernel(counts, sc, dh_own, dh_other, y, dtop, gain, *refs):
    lists, refs = split_lists(refs, counts)
    dy_ref, low_ref, dout_ref, small_ref, w, sems = refs
    copies = piece_copies(lists, w, sems, sc[5], sc[3])
    for copy in copies:
        copy.start()
    for copy in copies:
        copy.wait()
    nseq, rows, width = y.shape
    sums = None
    for i in range(nseq):
        at_i = slice(i * rows, (i + 1) * rows)
        dh = dh_own[at_i, :] + dh_other[at_i, :].astype(F32)
        n, scale = normed_parts(y[i])
        dy = dtop[at_i, :].astype(F32) + norm_back(dh, n, scale, gain[...])
        dy_ref[i] = dy
        low = dy.astype(BF16)
        low_ref[i] = low
        dout_ref[i] = nt(w[...], low).astype(BF16)
        term = jnp.concatenate([jnp.sum(dh * n, axis=0, keepdims=True), jnp.sum(dh, axis=0, keepdims=True)], axis=0)
        sums = term if sums is None else sums + term
    small_ref[...] = sums


def mix_back(scalars, dh_own, dh_other, y, dtop, gain, w_lists):
    counts = [len(pieces) for pieces in w_lists]
    flat = [piece for pieces in w_lists for piece in pieces]
    nseq, rows, width = y.shape
    whole = lambda a: pl.BlockSpec(a.shape, lambda i, sc: (0,) * a.ndim)
    out_shape = [
        jax.ShapeDtypeStruct((nseq, rows, width), F32),
        jax.ShapeDtypeStruct((nseq, rows, width), BF16),
        jax.ShapeDtypeStruct((nseq, width, rows), BF16),
        jax.ShapeDtypeStruct((2, width), F32),
    ]
    args = (dh_own, dh_other, y, dtop, gain)
    return pl.pallas_call(
        functools.partial(mix_back_kernel, counts),
        grid_spec=pltpu.PrefetchScalarGridSpec(
            num_scalar_prefetch=1,
            grid=(1,),
            in_specs=[whole(a) for a in args] + [ANY] * len(flat),
            out_specs=[whole(a) for a in out_shape],
            scratch_shapes=[pltpu.VMEM((width, width), BF16), pltpu.SemaphoreType.DMA((2 * PIECES,))],
        ),
        out_shape=out_shape,
        compiler_params=pltpu.CompilerParams(vmem_limit_bytes=VMEM),
        cost_estimate=FREE,
        name="mix_back",
    )(scalars, *args, *flat)


def whole_call(body, scalars, args, out_shape, name, scratch=()):
    whole = lambda a: pl.BlockSpec(a.shape, lambda i, sc: (0,) * len(a.shape))
    return pl.pallas_call(
        body,
        grid_spec=pltpu.PrefetchScalarGridSpec(
            num_scalar_prefetch=1,
            grid=(1,),
            in_specs=[whole(a) for a in args],
            out_specs=[whole(a) for a in out_shape],
            scratch_shapes=list(scratch),
        ),
        out_shape=out_shape,
        compiler_params=pltpu.CompilerParams(vmem_limit_bytes=VMEM),
        cost_estimate=FREE,
        name=name,
    )(scalars, *args)


def fold(scalars, keep, got, which):
    def body(sc, keep_ref, got_ref, keep_out, send_out):
        bit = 0 if which is None else sc[which]
        for i in range(keep_ref.shape[0]):
            keep_out[i] = keep_ref[i, bit].astype(F32) + got_ref[i, bit].astype(F32)
            send_out[i] = (keep_ref[i, 1 - bit].astype(F32) + got_ref[i, 1 - bit].astype(F32)).astype(BF16)

    shape = (keep.shape[0], *keep.shape[2:])
    out_shape = [jax.ShapeDtypeStruct(shape, F32), jax.ShapeDtypeStruct(shape, BF16)]
    return whole_call(body, scalars, (keep, got.reshape(keep.shape)), out_shape, "fold")


def fold_halves(scalars, left, left_got, right, right_got):
    rows, half = left.shape[2:]

    def body(sc, lk, lg, rk, rg, left_out, right_out, send_out):
        left_out[0] = lk[0, 0] + lg[0, 0].astype(F32)
        right_out[0] = rk[0, 0] + rg[0, 0].astype(F32)
        send_out[0, :, :half] = (lk[0, 1] + lg[0, 1].astype(F32)).astype(BF16)
        send_out[0, :, half:] = (rk[0, 1] + rg[0, 1].astype(F32)).astype(BF16)

    one = jax.ShapeDtypeStruct((1, rows, half), F32)
    out_shape = [one, one, jax.ShapeDtypeStruct((1, rows, 2 * half), BF16)]
    args = (left, left_got.reshape(left.shape), right, right_got.reshape(right.shape))
    return whole_call(body, scalars, args, out_shape, "fold_halves")


def join(scalars, keep, got):
    def body(sc, keep_ref, got_ref, out):
        out[...] = (keep_ref[...].astype(F32) + got_ref[...].astype(F32)).astype(BF16)

    out_shape = [jax.ShapeDtypeStruct(keep.shape, BF16)]
    return whole_call(body, scalars, (keep, got.reshape(keep.shape)), out_shape, "join")[0]


def append(scalars, held, got):
    def body(sc, held_ref, got_ref, out):
        count = held_ref.shape[0]
        out[0:count] = held_ref[...]
        out[count : 2 * count] = got_ref[...]

    out_shape = [jax.ShapeDtypeStruct((2 * held.shape[0], *held.shape[1:]), held.dtype)]
    return whole_call(body, scalars, (held, got), out_shape, "append")[0]


def merge_low(scalars, down, down_got, out, out_got, which):
    zys, lows, width = down.shape
    outs = out.shape[1]
    fill = -outs % 16

    def body(sc, down_ref, down_got_ref, out_ref, out_got_ref, keep_out, send_out):
        for i in range(zys // 2):
            for target, bit in ((keep_out, sc[which]), (send_out, 1 - sc[which])):
                t = 2 * i + bit
                first = down_ref[t].astype(F32) + down_got_ref[t].astype(F32)
                second = out_ref[t].astype(F32) + out_got_ref[t].astype(F32)
                rows = [first, second] + ([jnp.zeros((fill, width), F32)] if fill else [])
                target[i] = jnp.concatenate(rows, axis=0).astype(target.dtype)

    shape = (zys // 2, lows + outs + fill, width)
    out_shape = [jax.ShapeDtypeStruct(shape, F32), jax.ShapeDtypeStruct(shape, BF16)]
    args = (down, down_got.reshape(down.shape), out, out_got.reshape(out.shape))
    return whole_call(body, scalars, args, out_shape, "merge_low")


def first_norm_back(scalars, tokens, dy, gain, parts):
    nseq, rows, width = tokens.shape

    def body(sc, tokens_ref, dy_ref, gain_ref, lk, rk, got, out):
        seq = sc[6]
        for i in range(nseq):
            here = seq == i
            dh = jnp.where(here, jnp.concatenate([lk[0], rk[0]], axis=1), got[0].astype(F32))
            n, scale = normed_parts(tokens_ref[i].astype(F32))
            out[i] = dy_ref[i] + norm_back(dh, n, scale, gain_ref[...])

    out_shape = [jax.ShapeDtypeStruct(tokens.shape, F32)]
    return whole_call(body, scalars, (tokens, dy, gain, *parts), out_shape, "first_norm_back")[0]


def piece_of(places):
    def block(t, sc):
        d = t ^ sc[0]
        return (d % 2 * 2 ** places[0] + d // 2 % 2 * 2 ** places[1] + d // 4 % 2 * 2 ** places[2], 0, 0)

    return block


def up_rows_kernel(parts, sc, own_ref, other_ref, out_ref):
    first = sc[3] == 0
    own, other = own_ref[0].astype(F32), other_ref[0].astype(F32)
    split = own.shape[1] // parts
    for p in range(parts):
        cols = slice(p * split, (p + 1) * split)
        out_ref[0, :, 2 * p * split : (2 * p + 1) * split] = jnp.where(first, own[:, cols], other[:, cols])
        out_ref[0, :, (2 * p + 1) * split : (2 * p + 2) * split] = jnp.where(first, other[:, cols], own[:, cols])


def up_rows(scalars, own, other, parts):
    pieces, high, wide = own.shape
    return pl.pallas_call(
        functools.partial(up_rows_kernel, parts),
        grid_spec=pltpu.PrefetchScalarGridSpec(
            num_scalar_prefetch=1,
            grid=(pieces,),
            in_specs=[pl.BlockSpec((1, high, wide), piece_of((2, 1, 0)))] * 2,
            out_specs=pl.BlockSpec((1, high, 2 * wide), lambda t, sc: (t, 0, 0)),
        ),
        out_shape=jax.ShapeDtypeStruct((pieces, high, 2 * wide), F32),
        compiler_params=pltpu.CompilerParams(vmem_limit_bytes=VMEM),
        cost_estimate=FREE,
        name="up_rows",
    )(scalars, own, other)


def low_rows_kernel(lows, outs, sc, own_ref, other_ref, down_ref, out_ref):
    first = sc[3] == 0
    own, other = own_ref[0].astype(F32), other_ref[0].astype(F32)
    for c, value in enumerate((jnp.where(first, own, other), jnp.where(first, other, own))):
        down_ref[c, 0] = value[:lows]
        out_ref[c, 0] = value[lows : lows + outs]


def low_rows(scalars, own, other, lows, outs):
    pieces, low, width = own.shape
    return pl.pallas_call(
        functools.partial(low_rows_kernel, lows, outs),
        grid_spec=pltpu.PrefetchScalarGridSpec(
            num_scalar_prefetch=1,
            grid=(pieces,),
            in_specs=[pl.BlockSpec((1, low, width), piece_of((1, 2, 0)))] * 2,
            out_specs=[
                pl.BlockSpec((2, 1, lows, width), lambda t, sc: (0, t, 0, 0)),
                pl.BlockSpec((2, 1, outs, width), lambda t, sc: (0, t, 0, 0)),
            ],
        ),
        out_shape=[
            jax.ShapeDtypeStruct((2, pieces, lows, width), F32),
            jax.ShapeDtypeStruct((2, pieces, outs, width), F32),
        ],
        compiler_params=pltpu.CompilerParams(vmem_limit_bytes=VMEM),
        cost_estimate=FREE,
        name="low_rows",
    )(scalars, own, other)


def qkv_rows_kernel(groups, high, own, gw, sc, own_ref, other_ref, out_ref, gain_ref, conv_ref):
    core = sc[3]
    swapped = [(g ^ sc[4]) % 2 * 2 + (g ^ sc[4]) // 2 for g in range(groups)]
    convs = []
    gains = None
    for k in swapped:
        tail = own_ref[k].astype(F32)[high:]
        gains = tail[0:4, :own] if gains is None else gains + tail[0:4, :own]
        convs.append(tail[4:7, :])
    gain_ref[...] = gains
    for j in range(3):
        cols = slice(j * gw, (j + 1) * gw)
        conv_ref[:, j * groups * gw : (j + 1) * groups * gw] = jnp.concatenate([c[:, cols] for c in convs], axis=1)
    for c in range(2):
        pieces = [jnp.where(core == c, own_ref[k], other_ref[k]).astype(F32) for k in swapped]
        for j in range(3):
            cols = slice(j * gw, (j + 1) * gw)
            out = slice(j * groups * gw, (j + 1) * groups * gw)
            out_ref[c, :, out] = jnp.concatenate([p[:high, cols] for p in pieces], axis=1)


def qkv_rows(scalars, args, high):
    groups, _, cols = args[0].shape
    own = 2 * high
    shapes = [(2, high, groups * cols), (4, own), (3, groups * cols)]
    out_shape = [jax.ShapeDtypeStruct(shape, F32) for shape in shapes]
    return whole_call(
        functools.partial(qkv_rows_kernel, groups, high, own, cols // 3), scalars, args, out_shape, "qkv_rows"
    )


def per_device(tokens, cotangent, lengths, ln1_gain, ln1_bias, w_qkv, w_conv, w_out, ln2_gain, ln2_bias, w_up, w_down):
    nseq, rows, width = tokens.shape
    half = width // 2
    count = lax.axis_size("ctx")
    parts = lax.axis_size("fsdp")
    rank = lax.axis_index("ctx")
    index = lax.axis_index("fsdp")
    hidden = w_up.shape[1]
    zys = nseq * GROUPS
    share = count // zys
    hp = HEADS // GROUPS
    hd = width // HEADS
    gw = hp * hd
    mine = rank % share
    core = rank % 2
    zy = rank // share
    seq = zy // GROUPS
    group = zy % GROUPS
    bit_b, bit_a, bit_s = share, 2 * share, 4 * share
    share_bits = bits(share)
    positions = rank * rows + jnp.arange(rows, dtype=jnp.int32)
    valid = positions[None, :] < lengths[:, None]
    high_bits = [index // mask % 2 for mask in reversed(bits(parts))]
    scalars = [zy, mine, lengths[seq], core, group, index, seq, zy // 2 % 2, zy % 2] + high_bits
    scalars = jnp.stack(scalars).astype(jnp.int32)
    at_s, at_a, at_b, at_x = 6, 7, 8, 9

    own_seq, far_seq = at(tokens, seq), at(tokens, 1 - seq)
    w_qkv, w_conv = lax.optimization_barrier((w_qkv, w_conv, far_seq))[:2]
    pair = jnp.stack([own_seq, exch(far_seq, "ctx", bit_s)])
    left, right = pair[..., :half], pair[..., half:]
    w_up, w_down, w_out = lax.optimization_barrier((w_up, w_down, w_out, left, right))[:3]
    left = jnp.stack([left, exch(left, "ctx", bit_a)], axis=1)
    right = jnp.stack([right, exch(right, "ctx", bit_b)], axis=1)
    left = jnp.stack([left, exch(left, "ctx", bit_b)], axis=2)
    right = jnp.stack([right, exch(right, "ctx", bit_a)], axis=1)
    left = gather_list(left.reshape(1, zys, rows, half), "ctx", share_bits)
    right = gather_list(right.reshape(1, zys, rows, half), "ctx", share_bits)

    small = jnp.concatenate([ln1_gain, ln1_bias, ln2_gain, ln2_bias, w_conv.reshape(-1)])
    small = gather_fsdp(small.reshape(1, -1)).reshape(parts, -1).astype(F32)
    own_rows = ln1_gain.shape[0]
    gains = small[:, : 4 * own_rows].reshape(parts, 4, own_rows).transpose(1, 0, 2).reshape(4, 1, width)
    gain_one, bias_one, gain_two, bias_two = gains[0], gains[1], gains[2], gains[3]
    taps = small[:, 4 * own_rows :].reshape(parts, 3, -1).transpose(1, 0, 2).reshape(3, 3, width)
    taps = lax.dynamic_slice_in_dim(taps, group * gw, gw, 2).reshape(3, 3 * gw)
    fsdp_bits = bits(parts)
    split = hidden // parts // 2
    both_cores = lambda pieces: [pieces, [exch(piece, "ctx", 1) for piece in pieces]]
    qkv = both_cores(gather_list(qkv_part(scalars, w_qkv, gw)[None], "fsdp", fsdp_bits))
    if split == width:
        ups = gather_list(rest_part(scalars, w_up, w_down, w_out, parts), "fsdp", fsdp_bits)
        downs = []
        out_w = both_cores([rest[:, parts * own_rows + split :] for rest in ups])
    else:
        out_w = both_cores(gather_list(at(w_out.reshape(2, own_rows // 2, width), core)[None], "fsdp", fsdp_bits))
        ups = gather_list(up_part(scalars, w_up, parts)[None], "fsdp", fsdp_bits)
        downs = gather_list(at(w_down.reshape(2, split, width), core)[None], "fsdp", fsdp_bits)

    h_one, pre, q, k, kt, v, vt = project(scalars, left, right, qkv, taps, gain_one, bias_one, share, hp, hd)
    attn_t, o, lse = attend(scalars, q, k, vt, share, rows)
    classes = [[i for i in range(count) if i % share == s] for s in range(share)]
    swap = lambda x: lax.all_to_all(x, "ctx", 0, 0, tiled=True, axis_index_groups=classes)
    attn_t = swap(attn_t).reshape(nseq, width, rows)

    order = Order()
    dtop = jnp.where(valid[..., None], cotangent, jnp.zeros_like(cotangent)).reshape(nseq * rows, width)
    dtop_other = exch(dtop, "ctx", 1)
    y_one, h_two = mix(scalars, attn_t, tokens, gain_two, bias_two, out_w, parts)
    h_other = exch(h_two, "ctx", 1)
    r, dupper, dh_keep, dh_send, y_keep, y_send = feed(
        scalars, h_two, h_other, dtop, dtop_other, ups, downs, split
    )
    dh_other = exch(dh_send, "ctx", 1)
    h_pair = jnp.concatenate([h_two, h_other], axis=1)
    dtop_pair = jnp.concatenate([dtop, dtop_other])

    near_base = index // (parts // 2) * (parts // 2)

    def near(term):
        return jnp.stack([term(near_base + p) for p in range(parts // 2)])

    def fsdp_start(term):
        far = [term(parts // 2 - near_base + p) for p in range(parts // 2)]
        return exch(jnp.stack(far).astype(BF16), "fsdp", parts // 2)

    def fsdp_more(keep, got):
        for i, mask in enumerate(reversed(fsdp_bits[:-1])):
            keep, send = fold(scalars, keep.reshape(1, 2, mask, *keep.shape[1:]), got, at_x + 1 + i)
            keep, got = keep[0], exch(send[0], "fsdp", mask)
        return keep, got

    down_term = lambda p: tn(at(r, p), dtop_pair)
    down_got = fsdp_start(down_term)
    dh_keep, dh_other = order(dh_keep, dh_other)
    dy_one, dy_low, dout_t, small_two = mix_back(scalars, dh_keep, dh_other, y_one, dtop, gain_two, out_w)
    order.mark(dout_t)
    r, dupper, y_keep, y_send, h_pair = order(r, dupper, y_keep, y_send, h_pair)
    dout_t = swap(dout_t.reshape(zys, gw, rows))

    def cut(held, axis, bit):
        keep = lax.dynamic_slice_in_dim(held, bit, 1, axis)
        send = lax.dynamic_slice_in_dim(held, 1 - bit, 1, axis)
        return keep, send.astype(BF16)

    zy_bits = {"s": (0, bit_s, zy // 4), "a": (1, bit_a, zy // 2 % 2), "b": (2, bit_b, zy % 2)}
    grad_out = jnp.einsum("sct,std->cd", attn_t, dy_low, preferred_element_type=F32)
    grad_out = grad_out.reshape(parts, 2, own_rows // 2, width)
    grad_out = lax.dynamic_index_in_dim(grad_out, core, 1, keepdims=False) + exch(
        lax.dynamic_index_in_dim(grad_out, 1 - core, 1, keepdims=False).astype(BF16), "ctx", 1
    ).astype(F32)
    out_got = fsdp_start(lambda p: at(grad_out, p))
    out_keep = near(lambda p: at(grad_out, p))
    grad_up = jnp.einsum("pnk,nf->pkf", h_pair, dupper, preferred_element_type=F32)
    grad_up = grad_up.reshape(parts, 2, 2, 2, own_rows // zys, hidden // 2)
    up_keep, up_send = cut(grad_up, 2, zy_bits["a"][2])
    down_keep = near(down_term)
    result = y_one + (y_keep + exch(y_send, "ctx", 1).astype(F32)).reshape(nseq, rows, width)
    output = jnp.where(valid[..., None], result, 0.0).astype(BF16)

    dout_t, up_keep, up_send, down_keep, out_keep, output = lax.optimization_barrier(
        (dout_t, up_keep, up_send, down_keep, out_keep, output)
    )
    up_got = exch(up_send, "ctx", bit_a)
    lows = down_keep.shape[1] // zys
    outs = out_keep.shape[1] // zys
    d_mine, recv = [], []
    for h in range(hp):
        dout_t = order(dout_t)
        kept, sent = attend_back(scalars, h, q, k, kt, v, dout_t, o, lse, share, rows)
        order.mark(kept)
        d_mine.append(kept)
        recv += [exch(sent[x - 1 : x], "ctx", x) for x in range(1, share)]
        if h == 0:
            down_keep, out_keep = order(down_keep, out_keep)
            down_keep, down_got = fsdp_more(down_keep, down_got)
            out_keep, out_got = fsdp_more(out_keep, out_got)
            low_keep, low_send = merge_low(
                scalars,
                down_keep.reshape(zys, lows, width),
                down_got,
                out_keep.reshape(zys, outs, width),
                out_got,
                at_b,
            )
            order.mark(low_send)
            low_got = exch(low_send, "ctx", bit_b)
    low_rest = low_keep.shape[1:]
    high = own_rows // zys
    low_keep, low_send = fold(scalars, order(low_keep).reshape(2, 2, *low_rest), low_got, at_a)
    order.mark(low_send)
    low_got = exch(low_send, "ctx", bit_a)
    up_keep = order(up_keep).reshape(1, 2, parts // 2 * 4 * high, hidden // 2)
    up_keep, up_send = fold(scalars, up_keep, up_got, at_x)
    order.mark(up_send)
    up_got = exch(up_send, "fsdp", parts // 2)
    d_last = order(d_mine[-1])
    left_keep, left_send, right_keep, right_send, dw_keep, dw_send = project_back(
        scalars, d_mine[:-1] + [d_last], recv, left[0], right[0], h_one, pre, taps, small_two, qkv, share, rows, parts
    )
    order.mark(dw_send)

    def folded(keep, got, which, shape):
        keep, send = fold(scalars, order(keep).reshape(shape), got, which)
        order.mark(send)
        return keep, send

    def appended(held, got):
        return order.mark(append(scalars, order(held), got))

    left_got = exch(left_send, "ctx", bit_a)
    right_got = exch(right_send, "ctx", bit_b)
    dw_got = exch(dw_send, "ctx", 1)
    up_rest = (high, hidden // 2)
    low_keep, low_send = folded(low_keep, low_got, at_s, (1, 2, *low_rest))
    low_got = exch(low_send, "ctx", bit_s)
    up_keep, up_got = fsdp_more(up_keep.reshape(parts // 2, 2, 2, *up_rest), up_got)
    up_keep, up_send = folded(up_keep, up_got, at_b, (2, 2, *up_rest))
    up_got = exch(up_send, "ctx", bit_b)
    dw_rest = dw_keep.shape[1:]
    right_keep, right_send = folded(right_keep, right_got, None, (1, 2, 2, rows, half))
    right_got = exch(right_send, "ctx", bit_a)
    left_keep, left_send = folded(left_keep, left_got, None, (1, 2, 2, rows, half))
    left_got = exch(left_send, "ctx", bit_b)
    dw_keep, dw_send = folded(dw_keep, dw_got, at_x, (1, 2, parts // 2, *dw_rest))
    dw_keep, dw_got = fsdp_more(dw_keep[0], exch(dw_send[0], "fsdp", parts // 2))
    low = order.mark(join(scalars, order(low_keep), low_got))
    low_got = exch(low, "ctx", bit_s)
    up_keep, up_send = folded(up_keep, up_got, at_s, (1, 2, *up_rest))
    up_got = exch(up_send, "ctx", bit_s)
    block = order.mark(join(scalars, order(dw_keep).reshape(dw_rest), dw_got))
    dw_got = exch(block, "ctx", bit_s)
    left_keep, right_keep = order(left_keep, right_keep)
    left_keep, right_keep, dh_send = fold_halves(scalars, left_keep, left_got, right_keep, right_got)
    order.mark(dh_send)
    dh_got = exch(dh_send, "ctx", bit_s)
    low = appended(low, low_got)
    low_got = exch(low, "ctx", bit_b)
    up = order.mark(join(scalars, order(up_keep), up_got))
    up_got = exch(up, "ctx", bit_s)
    block = join(scalars, order(block), dw_got)
    for mask in share_bits[1:]:
        block = join(scalars, block, exch(block, "ctx", mask))
    block = order.mark(block[None])
    dw_got = exch(block, "ctx", bit_a)
    low = appended(low, low_got)
    low_got = exch(low, "ctx", bit_a)
    dy_one = order(dy_one)
    input_grad = order.mark(first_norm_back(scalars, tokens, dy_one, gain_one, (left_keep, right_keep, dh_got)))
    block = appended(block, dw_got)
    dw_got = exch(block, "ctx", bit_b)
    up = appended(up, up_got)
    up_got = exch(up, "ctx", bit_a)
    block = appended(block, dw_got)
    block_other = exch(block, "ctx", 1)
    up = appended(up, up_got)
    up_got = exch(up, "ctx", bit_b)
    low = appended(low, low_got)
    low_other = exch(low, "ctx", 1)
    block = order(block)
    w_qkv_grad, gains, convs = qkv_rows(scalars, (block, block_other), own_rows // 2)
    w_qkv_grad = order.mark(w_qkv_grad.reshape(own_rows, 3 * width))
    share_cols = 3 * width // parts
    w_conv_grad = lax.dynamic_slice_in_dim(convs, index * share_cols, share_cols, 1)
    w_down_grad, w_out_grad = low_rows(scalars, order(low), low_other, lows, outs)
    w_down_grad = order.mark(w_down_grad.reshape(hidden // parts, width))
    w_out_grad = w_out_grad.reshape(own_rows, width)
    up = appended(up, up_got)
    w_up_grad = up_rows(scalars, up, exch(up, "ctx", 1), parts).reshape(own_rows, hidden)

    return (
        output,
        input_grad,
        gains[0],
        gains[1],
        w_qkv_grad,
        w_conv_grad,
        w_out_grad,
        gains[2],
        gains[3],
        w_up_grad,
        w_down_grad,
    )


def solution(mesh):
    rows = P("fsdp", "ctx", None)
    first = P("fsdp")
    weight = P("fsdp", None)
    second = P(None, "fsdp")
    in_specs = (rows, rows, first, first, first, weight, second, weight, first, first, weight, weight)
    out_specs = (rows, rows, first, first, weight, second, weight, first, first, weight, weight)
    return jax.shard_map(per_device, mesh=mesh, in_specs=in_specs, out_specs=out_specs, check_vma=False)
```

```python
import functools

import jax
import jax.numpy as jnp
from jax import lax
from jax.experimental import pallas as pl
from jax.experimental.pallas import tpu as pltpu
from jax.sharding import PartitionSpec as P

HEADS = 12
GROUPS = 4
EPS = 1e-05
RIM = 16
PIECES = 8
TAIL = 16
MASKED = -1e30
MIB = 1024 * 1024
F32 = jnp.float32
BF16 = jnp.bfloat16
LINE = (
    "head 0",
    "low b",
    "head 1",
    "head 2",
    "up x",
    "low a",
    "back",
    "low s",
    "up b",
    "qkv x",
    "low sum",
    "up s",
    "right a",
    "low gather b",
    "qkv s",
    "left b",
    "up sum",
    "up gather a",
    "input s",
    "low gather a",
    "qkv a",
    "up gather b",
    "qkv gather b",
    "up core",
    "low core",
    "low end",
    "input end",
    "qkv core",
    "up end",
    "qkv end",
)
FREE = pl.CostEstimate(flops=0, bytes_accessed=0, transcendentals=0)


def exch(value, axis, mask):
    count = lax.axis_size(axis)
    return lax.ppermute(value, axis, [(i, i ^ mask) for i in range(count)])


def bits(count):
    return [1 << b for b in range(count.bit_length() - 1)]


def at(stack, index):
    return lax.dynamic_index_in_dim(stack, index, 0, keepdims=False)


def flip(stack, index):
    return jnp.stack([at(stack, k ^ index) for k in range(stack.shape[0])])


def gather_bits(value, axis, masks):
    held = value[None]
    for mask in masks:
        held = jnp.concatenate([held, exch(held, axis, mask)])
    return held


def gather_fsdp(value):
    count = lax.axis_size("fsdp")
    return flip(gather_bits(value, "fsdp", bits(count)), lax.axis_index("fsdp"))


def gather_list(value, axis, masks):
    held = [value]
    for mask in masks:
        held.append(exch(held[0] if len(held) == 1 else jnp.concatenate(held), axis, mask))
    return held


def after(value, *others):
    return lax.optimization_barrier((value, *others))[0]


class Order:
    def __init__(self):
        self.last = None

    def __call__(self, *values):
        if self.last is not None:
            values = lax.optimization_barrier((*values, self.last))[:-1]
        return values if len(values) > 1 else values[0]

    def mark(self, value):
        self.last = value
        return value


def normed_parts(values):
    centre = values - jnp.mean(values, axis=-1, keepdims=True)
    scale = lax.rsqrt(jnp.mean(centre * centre, axis=-1, keepdims=True) + EPS)
    return centre * scale, scale


def norm_back(grad, normed, scale, gain):
    dnorm = grad * gain
    return scale * (
        dnorm
        - jnp.mean(dnorm, axis=-1, keepdims=True)
        - normed * jnp.mean(dnorm * normed, axis=-1, keepdims=True)
    )


def nn(a, b):
    return lax.dot_general(a, b, (((1,), (0,)), ((), ())), preferred_element_type=F32)


def nt(a, b):
    return lax.dot_general(a, b, (((1,), (1,)), ((), ())), preferred_element_type=F32)


def tn(a, b):
    return lax.dot_general(a, b, (((0,), (0,)), ((), ())), preferred_element_type=F32)


def piece_copies(lists, scratch, sems, index, core, take=None, cols=None, rows=None):
    copies = []
    cores = len(lists)
    for r, pieces in enumerate(lists):
        k = 0
        for stack in pieces:
            for i in range(stack.shape[0]):
                first, size = take or (0, stack.shape[1])
                if rows is not None:
                    first, size = stack.shape[1] - rows, rows
                part = (core ^ r) if cores == 2 else 0
                start = pl.multiple_of(((index ^ k) * cores + part) * size, size)
                target = scratch.at[pl.ds(start, size)] if cols is None else scratch.at[pl.ds(start, size), cols]
                source = stack.at[i, pl.ds(first, size)]
                copies.append(pltpu.make_async_copy(source, target, sems.at[len(copies)]))
                k += 1
    return copies


def split_lists(refs, counts):
    lists, at_ref = [], 0
    for n in counts:
        lists.append(refs[at_ref : at_ref + n])
        at_ref += n
    return lists, refs[at_ref:]


ANY = pl.BlockSpec(memory_space=pl.ANY)


def qkv_part_kernel(groups, gw, sc, w, out):
    group = sc[4]
    for j in range(3):
        picked = w[:, j * groups * gw : j * groups * gw + gw]
        for g in range(1, groups):
            start = (j * groups + g) * gw
            picked = jnp.where(group == g, w[:, start : start + gw], picked)
        out[:, j * gw : (j + 1) * gw] = picked


def qkv_part(scalars, w_qkv, gw):
    rows, cols = w_qkv.shape
    return pl.pallas_call(
        functools.partial(qkv_part_kernel, GROUPS, gw),
        grid_spec=pltpu.PrefetchScalarGridSpec(
            num_scalar_prefetch=1,
            grid=(1,),
            in_specs=[pl.BlockSpec((rows // 2, cols), lambda i, sc: (sc[3], 0))],
            out_specs=pl.BlockSpec((rows // 2, 3 * gw), lambda i, sc: (0, 0)),
        ),
        out_shape=jax.ShapeDtypeStruct((rows // 2, 3 * gw), BF16),
        compiler_params=pltpu.CompilerParams(vmem_limit_bytes=8 * MIB),
        cost_estimate=FREE,
        name="qkv_part",
    )(scalars, w_qkv)


def up_part_kernel(sc, w, out):
    out[...] = w[...]


def up_part(scalars, w_up, parts):
    rows, cols = w_up.shape
    split = cols // parts // 2
    if split % 128:
        picked = lax.dynamic_index_in_dim(w_up.reshape(rows, parts, 2, split), scalars[3], 2, keepdims=False)
        return picked.reshape(rows, cols // 2)
    return pl.pallas_call(
        up_part_kernel,
        grid_spec=pltpu.PrefetchScalarGridSpec(
            num_scalar_prefetch=1,
            grid=(parts,),
            in_specs=[pl.BlockSpec((rows, split), lambda p, sc: (0, 2 * p + sc[3]))],
            out_specs=pl.BlockSpec((rows, split), lambda p, sc: (0, p)),
        ),
        out_shape=jax.ShapeDtypeStruct((rows, cols // 2), BF16),
        compiler_params=pltpu.CompilerParams(vmem_limit_bytes=8 * MIB),
        cost_estimate=FREE,
        name="up_part",
    )(scalars, w_up)


def rest_part_kernel(parts, sc, w_up, w_down, w_out, out, sems):
    core = sc[3]
    own, cols = w_up.shape
    split = cols // parts // 2
    copies = []
    for p in range(parts):
        source = w_up.at[:, pl.ds(pl.multiple_of((2 * p + core) * split, split), split)]
        copies.append(pltpu.make_async_copy(source, out.at[0, pl.ds(p * own, own)], sems.at[p]))
    source = w_down.at[pl.ds(pl.multiple_of(core * split, split), split)]
    copies.append(pltpu.make_async_copy(source, out.at[0, pl.ds(parts * own, split)], sems.at[parts]))
    source = w_out.at[pl.ds(pl.multiple_of(core * (own // 2), own // 2), own // 2)]
    copies.append(pltpu.make_async_copy(source, out.at[0, pl.ds(parts * own + split, own // 2)], sems.at[parts + 1]))
    for copy in copies:
        copy.start()
    for copy in copies:
        copy.wait()


def rest_part(scalars, w_up, w_down, w_out, parts):
    own, cols = w_up.shape
    split = cols // parts // 2
    rows = parts * own + split + own // 2
    return pl.pallas_call(
        functools.partial(rest_part_kernel, parts),
        grid_spec=pltpu.PrefetchScalarGridSpec(
            num_scalar_prefetch=1,
            grid=(1,),
            in_specs=[ANY] * 3,
            out_specs=ANY,
            scratch_shapes=[pltpu.SemaphoreType.DMA((parts + 2,))],
        ),
        out_shape=jax.ShapeDtypeStruct((1, rows, split), BF16),
        compiler_params=pltpu.CompilerParams(vmem_limit_bytes=2 * MIB),
        cost_estimate=FREE,
        name="rest_part",
    )(scalars, w_up, w_down, w_out)


def attention_kernel(share, hp, hd, rows, per, last, shares, counts, sc, *refs):
    (left, right), refs = split_lists(refs, (len(shares), len(shares)))
    taps, gain, bias = refs[:3]
    lists, refs = split_lists(refs[3:], counts)
    h_ref, pre_ref, at_ref, o_ref, lse_ref = refs[:5]
    kept = refs[5:9]
    buf, w, sems, save_sems, q_ref, k_ref, kt_ref, v_ref, vt_ref = refs[9:]
    step = pl.program_id(0)
    saves = [
        pltpu.make_async_copy(source, target, save_sems.at[i])
        for i, (source, target) in enumerate(zip((q_ref, k_ref, kt_ref, v_ref), kept))
    ]

    @pl.when(step <= last)
    def _():
        project_step(share, hp, hd, rows, per, sc, left, right, taps, gain, bias, lists, h_ref, pre_ref, q_ref, k_ref,
                     kt_ref, v_ref, vt_ref, buf, w, sems)

    @pl.when(step == last + 1)
    def _():
        for copy in saves:
            copy.start()

    @pl.when(step > last)
    def _():
        attend_step(share, rows, sc, step - last - 1, q_ref, k_ref, vt_ref, at_ref, o_ref, lse_ref)

    @pl.when(step == last + hp)
    def _():
        for copy in saves:
            copy.wait()


def project_step(share, hp, hd, rows, per, sc, left, right, taps, gain, bias, lists, h_ref, pre_ref, q_ref, k_ref,
                 kt_ref, v_ref, vt_ref, buf, w, sems):
    step = pl.program_id(0)

    @pl.when(step == 0)
    def _():
        copies = piece_copies(lists, w, sems, sc[5], sc[3])
        for copy in copies:
            copy.start()
        for copy in copies:
            copy.wait()

    mine = sc[1]
    length = sc[2]
    gw = hp * hd
    size = per * share * rows
    parts = []
    for z in range(per):
        at_z = z ^ (sc[0] % per)
        pieces = []
        for refs_l, refs_r in zip(left, right):
            pieces += [jnp.concatenate([refs_l[i, at_z], refs_r[i, at_z]], axis=1) for i in range(refs_l.shape[0])]
        for j in range(share):
            picked = pieces[0]
            for k in range(1, share):
                picked = jnp.where((j ^ mine) == k, pieces[k], picked)
            parts.append(picked.astype(F32))
    x = jnp.concatenate(parts, axis=0)
    n, _ = normed_parts(x)
    h = (n * gain[...] + bias[...]).astype(BF16)
    h_ref[...] = h
    pre = nn(h, w[...]).astype(BF16)
    pre_ref[...] = pre

    @pl.when(step == 0)
    def _():
        buf[0:8, :] = jnp.zeros((8, 3 * gw), F32)

    buf[8:, :] = pre.astype(F32)
    conv = (
        taps[0:1, :] * buf[8 : 8 + size, :]
        + taps[1:2, :] * buf[7 : 7 + size, :]
        + taps[2:3, :] * buf[6 : 6 + size, :]
    )
    buf[0:8, :] = buf[size : size + 8, :]
    qs = conv[:, :gw].astype(BF16)
    kf = conv[:, gw : 2 * gw]
    vf = conv[:, 2 * gw :]
    q_own = []
    for z in range(per):
        start = z * share * rows
        picked = qs[start : start + rows]
        for j in range(1, share):
            picked = jnp.where(mine == j, qs[start + j * rows : start + (j + 1) * rows], picked)
        q_own.append(picked)
    q_own = (jnp.concatenate(q_own, axis=0).astype(F32) * 0.125).astype(BF16)
    lane = lax.broadcasted_iota(jnp.int32, (per * rows, hd), 1)
    ones = jnp.where(lane == 0, 1.0, 0.0).astype(BF16)
    lane = lax.broadcasted_iota(jnp.int32, (size, hd), 1)
    pos = step * size + lax.broadcasted_iota(jnp.int32, (size, hd), 0)
    mask = jnp.where((lane == 0) & (pos >= length), MASKED, 0.0).astype(BF16)
    ks = kf.astype(BF16)
    vs = vf.astype(BF16)
    kt = kf.T.astype(BF16)
    vt = vf.T.astype(BF16)
    own = pl.ds(pl.multiple_of(step * per * rows, per * rows), per * rows)
    every = pl.ds(pl.multiple_of(step * size, size), size)
    for h in range(hp):
        cols = slice(h * hd, (h + 1) * hd)
        q_ref[h, own, :] = jnp.concatenate([q_own[:, cols], ones], axis=1)
        k_ref[h, every, :] = jnp.concatenate([ks[:, cols], mask], axis=1)
        v_ref[h, every, :] = vs[:, cols]
        kt_ref[h, :, every] = kt[cols]
        vt_ref[h, :, every] = vt[cols]


def attention(scalars, left, right, w_lists, taps, gain, bias, share, hp, hd):
    counts = [len(pieces) for pieces in w_lists]
    flat = [piece for pieces in w_lists for piece in pieces]
    _, zys, rows, half = left[0].shape
    width = 2 * half
    gw = hp * hd
    per = 2
    last = zys // per - 1
    total = zys * share * rows
    own = zys * rows
    size = per * share * rows
    shares = [a.shape[0] for a in left]
    body = functools.partial(attention_kernel, share, hp, hd, rows, per, last, shares, counts)
    whole = lambda *shape: pl.BlockSpec(shape, lambda t, sc: (0,) * len(shape))
    block = lambda t: jnp.minimum(t, last)
    head = lambda t: jnp.maximum(t - last - 1, 0)
    pieces = [pl.BlockSpec((n, per, rows, half), lambda t, sc: (0, block(t) ^ (sc[0] // per), 0, 0)) for n in shares]
    kept = [(hp, own, 2 * hd), (hp, total, 2 * hd), (hp, hd, total), (hp, total, hd)]
    return pl.pallas_call(
        body,
        grid_spec=pltpu.PrefetchScalarGridSpec(
            num_scalar_prefetch=1,
            grid=(last + 1 + hp,),
            in_specs=pieces * 2 + [whole(3, 3 * gw), whole(1, width), whole(1, width)] + [ANY] * len(flat),
            out_specs=[
                pl.BlockSpec((size, width), lambda t, sc: (block(t), 0)),
                pl.BlockSpec((size, 3 * gw), lambda t, sc: (block(t), 0)),
                pl.BlockSpec((zys, hd, rows), lambda t, sc: (0, head(t), 0)),
                pl.BlockSpec((1, hd, own), lambda t, sc: (head(t), 0, 0)),
                pl.BlockSpec((1, 1, own), lambda t, sc: (head(t), 0, 0)),
            ]
            + [ANY] * 4,
            scratch_shapes=[
                pltpu.VMEM((8 + size, 3 * gw), F32),
                pltpu.VMEM((width, 3 * gw), BF16),
                pltpu.SemaphoreType.DMA((2 * PIECES,)),
                pltpu.SemaphoreType.DMA((4,)),
            ]
            + [pltpu.VMEM(shape, BF16) for shape in kept + [(hp, hd, total)]],
        ),
        out_shape=[
            pltpu.HBM((total, width), BF16),
            pltpu.HBM((total, 3 * gw), BF16),
            jax.ShapeDtypeStruct((zys, gw, rows), BF16),
            pltpu.HBM((hp, hd, own), F32),
            jax.ShapeDtypeStruct((hp, 1, own), F32),
        ]
        + [pltpu.HBM(shape, BF16) for shape in kept],
        compiler_params=pltpu.CompilerParams(vmem_limit_bytes=32 * MIB),
        cost_estimate=FREE,
        name="attention",
    )(scalars, *left, *right, taps, gain, bias, *flat)


def seen(share, rows, mine, shape):
    key = lax.broadcasted_iota(jnp.int32, shape, 0)
    col = lax.broadcasted_iota(jnp.int32, shape, 1)
    query = jnp.where(col >= rows, share * rows + col - rows, col) + mine * rows
    return key <= query


def head_copies(sources, targets, sems, head, slot):
    return [
        pltpu.make_async_copy(source.at[pl.ds(head, 1)], target.at[pl.ds(slot, 1)], sems.at[i, slot])
        for i, (source, target) in enumerate(zip(sources, targets))
    ]


def attend_step(share, rows, sc, head, q_all, k_all, vt_all, at_ref, o_ref, lse_ref):
    mine = sc[1]
    q, k, vt = (buf.at[pl.ds(head, 1)] for buf in (q_all, k_all, vt_all))
    tile = 2 * rows
    step = share * tile
    hd = vt.shape[1]
    tiles = q.shape[1] // tile
    for t in range(tiles):
        queries = q[0, t * tile : (t + 1) * tile, :]
        top = jnp.full((1, tile), MASKED, F32)
        total = jnp.zeros((1, tile), F32)
        accum = jnp.zeros((hd, tile), F32)
        for j in [t] + list(range(t)):
            scores = nt(k[0, j * step : (j + 1) * step, :], queries)
            if j == t:
                scores = jnp.where(seen(share, rows, mine, scores.shape), scores, MASKED)
            higher = jnp.maximum(top, jnp.max(scores, axis=0, keepdims=True))
            probs = jnp.exp(scores - higher)
            factor = jnp.exp(top - higher)
            total = total * factor + jnp.sum(probs, axis=0, keepdims=True)
            accum = accum * factor + nn(vt[0, :, j * step : (j + 1) * step], probs.astype(BF16))
            top = higher
        out = accum / total
        o_ref[0, :, t * tile : (t + 1) * tile] = out
        lse_ref[0, :, t * tile : (t + 1) * tile] = top + jnp.log(total)
        low = out.astype(BF16)
        at_ref[2 * t] = low[:, :rows]
        at_ref[2 * t + 1] = low[:, rows:]


def attend_back_kernel(share, rows, head, sc, q_all, k_all, kt_all, v_all, o_all, dot_ref, lse, mine_ref, send_ref,
                       dq_acc, dk_acc, dv_acc, q, k, kt, v, o, sems):
    mine = sc[1]
    copies = head_copies((q_all, k_all, kt_all, v_all, o_all), (q, k, kt, v, o), sems, head, 0)
    for copy in copies:
        copy.start()
    own = q.shape[1]
    hd = v.shape[2]
    tile = 2 * rows
    step = share * tile
    tiles = own // tile
    total = tiles * step
    dq_acc[...] = jnp.zeros(dq_acc.shape, F32)
    dk_acc[total:, :] = jnp.zeros((RIM, hd), F32)
    dv_acc[total:, :] = jnp.zeros((RIM, hd), F32)
    for copy in copies:
        copy.wait()
    for t in reversed(range(tiles)):
        queries = q[0, t * tile : (t + 1) * tile, :]
        douts = jnp.concatenate([dot_ref[2 * t], dot_ref[2 * t + 1]], axis=1)
        outs = o[0, :, t * tile : (t + 1) * tile]
        logs = lse[0, :, t * tile : (t + 1) * tile]
        inner = jnp.sum(outs * douts.astype(F32), axis=0, keepdims=True)
        dqt = jnp.zeros((hd, tile), F32)
        for j in reversed(range(t + 1)):
            at_j = slice(j * step, (j + 1) * step)
            probs = jnp.exp(nt(k[0, at_j, :], queries) - logs)
            if j == t:
                probs = jnp.where(seen(share, rows, mine, probs.shape), probs, 0.0)
            dv = nt(probs.astype(BF16), douts)
            dprobs = nn(v[0, at_j, :], douts)
            dscores = (probs * (dprobs - inner)).astype(BF16)
            dk = nn(dscores, queries)[:, :hd]
            if t == tiles - 1:
                dv_acc[at_j, :] = dv
                dk_acc[at_j, :] = dk
            else:
                dv_acc[at_j, :] += dv
                dk_acc[at_j, :] += dk
            dqt += nn(kt[0, :, at_j], dscores)
        dq = (dqt * 0.125).T
        for b in (2 * t, 2 * t + 1):
            at_b = pl.ds(pl.multiple_of((b * share + mine) * rows, rows), rows)
            dq_acc[at_b, :] = dq[(b % 2) * rows : (b % 2 + 1) * rows]
    for b in range(own // rows):
        for r in range(share):
            start = (b * share + (mine ^ r)) * rows
            rows_i = pl.ds(pl.multiple_of(start, rows), rows + RIM)
            block = jnp.concatenate([acc[rows_i, :] for acc in (dq_acc, dk_acc, dv_acc)], axis=1)
            if r == 0:
                mine_ref[b] = block
            else:
                send_ref[r - 1, b] = block.astype(BF16)


def attend_back(scalars, head, q, k, kt, v, dout_t, o, lse, share, rows):
    hp, own, wide = q.shape
    total = k.shape[1]
    hd = v.shape[2]
    blocks = own // rows
    whole = lambda a: pl.BlockSpec(a.shape, lambda i, sc: (0,) * len(a.shape))
    one = lambda a: pl.BlockSpec((1, *a.shape[1:]), lambda i, sc: (head, 0, 0))
    out_shape = [
        pltpu.HBM((blocks, rows + RIM, 3 * hd), F32),
        jax.ShapeDtypeStruct((share - 1, blocks, rows + RIM, 3 * hd), BF16),
    ]
    return pl.pallas_call(
        functools.partial(attend_back_kernel, share, rows, head),
        grid_spec=pltpu.PrefetchScalarGridSpec(
            num_scalar_prefetch=1,
            grid=(1,),
            in_specs=[ANY] * 5 + [pl.BlockSpec((blocks, hd, rows), lambda i, sc: (0, head, 0)), one(lse)],
            out_specs=[whole(a) for a in out_shape],
            scratch_shapes=[pltpu.VMEM((total + RIM, hd), F32)] * 3
            + [pltpu.VMEM((1, *a.shape[1:]), a.dtype) for a in (q, k, kt, v, o)]
            + [pltpu.SemaphoreType.DMA((5, 1))],
        ),
        out_shape=out_shape,
        compiler_params=pltpu.CompilerParams(vmem_limit_bytes=16 * MIB),
        cost_estimate=FREE,
        name="attend_back",
    )(scalars, q, k, kt, v, o, dout_t, lse)


def project_back_kernel(share, rows, heads, parts, counts, sc, *refs):
    (kept, recv), refs = split_lists(refs, (heads, heads * (share - 1)))
    left, right, h_ref, pre_ref, taps, small_two = refs[:6]
    lists, refs = split_lists(refs[6:], counts)
    left_keep, left_send, right_keep, right_send, dw_keep, dw_send, buf, w, dw_acc, small_acc, conv_acc, sems = refs
    step = pl.program_id(0)
    steps = pl.num_programs(0)
    width = w.shape[0]
    half = width // 2

    @pl.when(step == 0)
    def _():
        copies = piece_copies(lists, w, sems, sc[5], sc[3])
        for copy in copies:
            copy.start()
        dw_acc[...] = jnp.zeros(dw_acc.shape, F32)
        small_acc[...] = jnp.zeros(small_acc.shape, F32)
        conv_acc[...] = jnp.zeros(conv_acc.shape, F32)
        for copy in copies:
            copy.wait()

    hd = kept[0].shape[2] // 3
    per = kept[0].shape[0]
    now, one, two, x = [], [], [], []
    for z in range(per):
        for i in range(heads):
            total = kept[i][z]
            for r in recv[i * (share - 1) : (i + 1) * (share - 1)]:
                total = total + r[0, z].astype(F32)
            for j in range(3):
                start = (j * heads + i) * hd
                buf[z, :, start : start + hd] = total[:, j * hd : (j + 1) * hd]
        now.append(buf[z, 0:rows, :])
        one.append(buf[z, 1 : rows + 1, :])
        two.append(buf[z, 2 : rows + 2, :])
        at_z = z ^ (sc[0] % per)
        x.append(jnp.concatenate([left[0, at_z], right[0, at_z]], axis=1))
    now, one, two, x = (jnp.concatenate(v, axis=0) for v in (now, one, two, x))
    dpre = (taps[0:1, :] * now + taps[1:2, :] * one + taps[2:3, :] * two).astype(BF16)
    pre = jnp.concatenate([pre_ref[z, 0] for z in range(per)], axis=0).astype(F32)
    n, _ = normed_parts(x.astype(F32))
    dh = nt(dpre, w[...])
    for z in range(per):
        k = (per * step + z) ^ sc[0]
        bit_s, bit_a, bit_b = k // 4, k // 2 % 2, k % 2
        dh_z = dh[z * rows : (z + 1) * rows]
        to_left, to_right = 2 * bit_b + bit_s, 2 * bit_a + bit_s

        @pl.when(bit_a == 0)
        def _(dh_z=dh_z, to_left=to_left):
            left_keep[to_left] = dh_z[:, :half]

        @pl.when(bit_a == 1)
        def _(dh_z=dh_z, to_left=to_left):
            left_send[to_left] = dh_z[:, :half].astype(BF16)

        @pl.when(bit_b == 0)
        def _(dh_z=dh_z, to_right=to_right):
            right_keep[to_right] = dh_z[:, half:]

        @pl.when(bit_b == 1)
        def _(dh_z=dh_z, to_right=to_right):
            right_send[to_right] = dh_z[:, half:].astype(BF16)

    h = jnp.concatenate([h_ref[z, 0] for z in range(per)], axis=0)
    dw_acc[...] += tn(h, dpre)
    small_acc[0:1, :] += jnp.sum(dh * n, axis=0, keepdims=True)
    small_acc[1:2, :] += jnp.sum(dh, axis=0, keepdims=True)
    conv_acc[0:3, :] += jnp.concatenate([jnp.sum(pre * d, axis=0, keepdims=True) for d in (now, one, two)], axis=0)

    @pl.when(step == steps - 1)
    def _():
        core = sc[3]
        own = width // parts
        high = own // 2
        cols = dw_acc.shape[1]
        small_acc[2:4, :] = small_two[...]
        for p in range(parts):
            gains = small_acc[0:4, p * own : (p + 1) * own]
            gains = jnp.concatenate([gains, jnp.zeros((4, cols - own), F32)], axis=1)
            tail = jnp.concatenate([gains, conv_acc[0:3, :], jnp.zeros((TAIL - 7, cols), F32)], axis=0)
            keep = pl.ds(pl.multiple_of((2 * p + core) * high, high), high)
            send = pl.ds(pl.multiple_of((2 * p + 1 - core) * high, high), high)
            dw_keep[p, 0:high, :] = dw_acc[keep, :]
            dw_keep[p, high : high + TAIL, :] = tail
            dw_send[p, 0:high, :] = dw_acc[send, :].astype(BF16)
            dw_send[p, high : high + TAIL, :] = tail.astype(BF16)


def project_back(scalars, mine, recv, left, right, h, pre, taps, small_two, w_lists, share, rows, parts):
    counts = [len(pieces) for pieces in w_lists]
    flat = [piece for pieces in w_lists for piece in pieces]
    blocks, ext, thin = mine[0].shape
    heads = len(mine)
    cols = heads * thin
    width = h.shape[1]
    half = width // 2
    high = width // parts // 2
    whole = lambda *shape: pl.BlockSpec(shape, lambda t, sc: (0,) * len(shape))
    per = blocks // 2
    piece = pl.BlockSpec((1, per, rows, half), lambda t, sc: (0, t ^ (sc[0] // per), 0, 0))
    by_block = lambda a: a.reshape(blocks, share, rows, a.shape[1])
    out_shape = [
        jax.ShapeDtypeStruct((blocks // 2, rows, half), F32),
        jax.ShapeDtypeStruct((blocks // 2, rows, half), BF16),
        jax.ShapeDtypeStruct((blocks // 2, rows, half), F32),
        jax.ShapeDtypeStruct((blocks // 2, rows, half), BF16),
        jax.ShapeDtypeStruct((parts, high + TAIL, cols), F32),
        jax.ShapeDtypeStruct((parts, high + TAIL, cols), BF16),
    ]
    return pl.pallas_call(
        functools.partial(project_back_kernel, share, rows, heads, parts, counts),
        grid_spec=pltpu.PrefetchScalarGridSpec(
            num_scalar_prefetch=1,
            grid=(blocks // per,),
            in_specs=[pl.BlockSpec((per, ext, thin), lambda t, sc: (t, 0, 0))] * heads
            + [pl.BlockSpec((1, per, ext, thin), lambda t, sc: (0, t, 0, 0))] * len(recv)
            + [
                piece,
                piece,
                pl.BlockSpec((per, 1, rows, width), lambda t, sc: (t, sc[1], 0, 0)),
                pl.BlockSpec((per, 1, rows, cols), lambda t, sc: (t, sc[1], 0, 0)),
                whole(3, cols),
                whole(2, width),
            ]
            + [ANY] * len(flat),
            out_specs=[whole(*o.shape) for o in out_shape],
            scratch_shapes=[
                pltpu.VMEM((per, ext, cols), F32),
                pltpu.VMEM((width, cols), BF16),
                pltpu.VMEM((width, cols), F32),
                pltpu.VMEM((8, width), F32),
                pltpu.VMEM((8, cols), F32),
                pltpu.SemaphoreType.DMA((2 * PIECES,)),
            ],
        ),
        out_shape=out_shape,
        compiler_params=pltpu.CompilerParams(vmem_limit_bytes=28 * MIB),
        cost_estimate=FREE,
        name="project_back",
    )(scalars, *mine, *recv, left, right, by_block(h), by_block(pre), taps, small_two, *flat)


def mix_kernel(counts, sc, attn, tokens, gain, bias, *refs):
    lists, refs = split_lists(refs, counts)
    y_ref, h_ref, w, sems = refs
    copies = piece_copies(lists, w, sems, sc[5], sc[3], rows=lists[1][0].shape[1])
    for copy in copies:
        copy.start()
    for copy in copies:
        copy.wait()
    nseq, rows, width = tokens.shape
    parts = h_ref.shape[0]
    own = width // parts
    for i in range(nseq):
        y = tokens[i].astype(F32) + tn(attn[i], w[...])
        y_ref[i] = y
        n, _ = normed_parts(y)
        h = (n * gain[...] + bias[...]).astype(BF16)
        for p in range(parts):
            h_ref[p, i * rows : (i + 1) * rows, :] = h[:, p * own : (p + 1) * own]


def mix(scalars, attn, tokens, gain, bias, w_lists, parts):
    counts = [len(pieces) for pieces in w_lists]
    flat = [piece for pieces in w_lists for piece in pieces]
    nseq, rows, width = tokens.shape
    whole = lambda a: pl.BlockSpec(a.shape, lambda i, sc: (0,) * len(a.shape))
    out_shape = [
        jax.ShapeDtypeStruct((nseq, rows, width), F32),
        jax.ShapeDtypeStruct((parts, nseq * rows, width // parts), BF16),
    ]
    args = (attn, tokens, gain, bias)
    return pl.pallas_call(
        functools.partial(mix_kernel, counts),
        grid_spec=pltpu.PrefetchScalarGridSpec(
            num_scalar_prefetch=1,
            grid=(1,),
            in_specs=[whole(a) for a in args] + [ANY] * len(flat),
            out_specs=[whole(a) for a in out_shape],
            scratch_shapes=[pltpu.VMEM((width, width), BF16), pltpu.SemaphoreType.DMA((2 * PIECES,))],
        ),
        out_shape=out_shape,
        compiler_params=pltpu.CompilerParams(vmem_limit_bytes=12 * MIB),
        cost_estimate=FREE,
        name="mix",
    )(scalars, *args, *flat)


def feed_kernel(counts, merged, sc, h_own, h_other, d_own, d_other, *refs):
    (ups, downs), refs = split_lists(refs, counts)
    r_ref, du_ref, dh_keep, dh_send, y_keep, y_send, up, down, sems = refs
    parts, rows, own = h_own.shape
    split = r_ref.shape[2]
    copies, later = [], []
    if merged:
        for p in range(parts):
            take = (p * own, own)
            cols = pl.ds(p * split, split)
            copies += piece_copies([ups], up, sems.at[0, p], sc[5], 0, take, cols)
        later += piece_copies([ups], down, sems.at[1, 0], sc[5], 0, (parts * own, split))
    else:
        copies += piece_copies([ups], up, sems.at[0, 0], sc[5], 0)
        later += piece_copies([downs], down, sems.at[1, 0], sc[5], 0)
    for copy in copies + later:
        copy.start()
    for copy in copies:
        copy.wait()
    h = jnp.concatenate(
        [jnp.concatenate([ref[p] for p in range(parts)], axis=1) for ref in (h_own, h_other)], axis=0
    )
    d = jnp.concatenate([d_own[...], d_other[...]], axis=0)
    dh = None
    y = None
    for p in range(parts):
        cols = slice(p * split, (p + 1) * split)
        act = jnp.maximum(nn(h, up[:, cols]), 0.0)
        r = jnp.square(act).astype(BF16)
        r_ref[p] = r
        if p == 0:
            for copy in later:
                copy.wait()
        dr = nt(d, down[cols, :])
        du = (dr * 2.0 * act).astype(BF16)
        du_ref[:, cols] = du
        term = nt(du, up[:, cols])
        dh = term if dh is None else dh + term
        term = nn(r, down[cols, :])
        y = term if y is None else y + term
    dh_keep[...] = dh[:rows]
    dh_send[...] = dh[rows:].astype(BF16)
    y_keep[...] = y[:rows]
    y_send[...] = y[rows:].astype(BF16)


def feed(scalars, h_own, h_other, d_own, d_other, ups, downs, split):
    parts, rows, own = h_own.shape
    width = parts * own
    cols = split * parts
    whole = lambda a: pl.BlockSpec(a.shape, lambda i, sc: (0,) * len(a.shape))
    out_shape = [
        jax.ShapeDtypeStruct((parts, 2 * rows, split), BF16),
        jax.ShapeDtypeStruct((2 * rows, cols), BF16),
        pltpu.HBM((rows, width), F32),
        jax.ShapeDtypeStruct((rows, width), BF16),
        pltpu.HBM((rows, width), F32),
        jax.ShapeDtypeStruct((rows, width), BF16),
    ]
    args = (h_own, h_other, d_own, d_other)
    return pl.pallas_call(
        functools.partial(feed_kernel, (len(ups), len(downs)), not downs),
        grid_spec=pltpu.PrefetchScalarGridSpec(
            num_scalar_prefetch=1,
            grid=(1,),
            in_specs=[whole(a) for a in args] + [ANY] * (len(ups) + len(downs)),
            out_specs=[whole(a) for a in out_shape],
            scratch_shapes=[
                pltpu.VMEM((width, cols), BF16),
                pltpu.VMEM((cols, width), BF16),
                pltpu.SemaphoreType.DMA((2, parts, PIECES)),
            ],
        ),
        out_shape=out_shape,
        compiler_params=pltpu.CompilerParams(vmem_limit_bytes=28 * MIB),
        cost_estimate=FREE,
        name="feed",
    )(scalars, *args, *ups, *downs)


def mix_back_kernel(counts, sc, dh_own, dh_other, y, dtop, gain, *refs):
    lists, refs = split_lists(refs, counts)
    dy_ref, low_ref, dout_ref, small_ref, w, sems = refs
    copies = piece_copies(lists, w, sems, sc[5], sc[3], rows=lists[1][0].shape[1])
    for copy in copies:
        copy.start()
    for copy in copies:
        copy.wait()
    nseq, rows, width = y.shape
    sums = None
    for i in range(nseq):
        at_i = slice(i * rows, (i + 1) * rows)
        dh = dh_own[at_i, :] + dh_other[at_i, :].astype(F32)
        n, scale = normed_parts(y[i])
        dy = dtop[at_i, :].astype(F32) + norm_back(dh, n, scale, gain[...])
        dy_ref[i] = dy
        low = dy.astype(BF16)
        low_ref[i] = low
        dout_ref[i] = nt(w[...], low).astype(BF16)
        term = jnp.concatenate([jnp.sum(dh * n, axis=0, keepdims=True), jnp.sum(dh, axis=0, keepdims=True)], axis=0)
        sums = term if sums is None else sums + term
    small_ref[...] = sums


def mix_back(scalars, dh_own, dh_other, y, dtop, gain, w_lists):
    counts = [len(pieces) for pieces in w_lists]
    flat = [piece for pieces in w_lists for piece in pieces]
    nseq, rows, width = y.shape
    whole = lambda a: pl.BlockSpec(a.shape, lambda i, sc: (0,) * len(a.shape))
    out_shape = [
        pltpu.HBM((nseq, rows, width), F32),
        jax.ShapeDtypeStruct((nseq, rows, width), BF16),
        jax.ShapeDtypeStruct((nseq, width, rows), BF16),
        jax.ShapeDtypeStruct((2, width), F32),
    ]
    args = (dh_own, dh_other, y, dtop, gain)
    return pl.pallas_call(
        functools.partial(mix_back_kernel, counts),
        grid_spec=pltpu.PrefetchScalarGridSpec(
            num_scalar_prefetch=1,
            grid=(1,),
            in_specs=[whole(a) for a in args] + [ANY] * len(flat),
            out_specs=[whole(a) for a in out_shape],
            scratch_shapes=[pltpu.VMEM((width, width), BF16), pltpu.SemaphoreType.DMA((2 * PIECES,))],
        ),
        out_shape=out_shape,
        compiler_params=pltpu.CompilerParams(vmem_limit_bytes=16 * MIB),
        cost_estimate=FREE,
        name="mix_back",
    )(scalars, *args, *flat)


def whole_call(body, scalars, args, out_shape, name, scratch=()):
    whole = lambda a: pl.BlockSpec(a.shape, lambda i, sc: (0,) * len(a.shape))
    return pl.pallas_call(
        body,
        grid_spec=pltpu.PrefetchScalarGridSpec(
            num_scalar_prefetch=1,
            grid=(1,),
            in_specs=[whole(a) for a in args],
            out_specs=[whole(a) for a in out_shape],
            scratch_shapes=list(scratch),
        ),
        out_shape=out_shape,
        compiler_params=pltpu.CompilerParams(vmem_limit_bytes=12 * MIB),
        cost_estimate=FREE,
        name=name,
    )(scalars, *args)


def fold(scalars, keep, got, which):
    def body(sc, keep_ref, got_ref, keep_out, send_out):
        bit = 0 if which is None else sc[which]
        for i in range(keep_ref.shape[0]):
            keep_out[i] = keep_ref[i, bit].astype(F32) + got_ref[i, bit].astype(F32)
            send_out[i] = (keep_ref[i, 1 - bit].astype(F32) + got_ref[i, 1 - bit].astype(F32)).astype(BF16)

    shape = (keep.shape[0], *keep.shape[2:])
    out_shape = [jax.ShapeDtypeStruct(shape, F32), jax.ShapeDtypeStruct(shape, BF16)]
    return whole_call(body, scalars, (keep, got.reshape(keep.shape)), out_shape, "fold")


def fold_halves(scalars, left, left_got, right, right_got):
    rows, half = left.shape[2:]

    def body(sc, lk, lg, rk, rg, left_out, right_out, send_out):
        left_out[0] = lk[0, 0] + lg[0, 0].astype(F32)
        right_out[0] = rk[0, 0] + rg[0, 0].astype(F32)
        send_out[0, :, :half] = (lk[0, 1] + lg[0, 1].astype(F32)).astype(BF16)
        send_out[0, :, half:] = (rk[0, 1] + rg[0, 1].astype(F32)).astype(BF16)

    one = jax.ShapeDtypeStruct((1, rows, half), F32)
    out_shape = [one, one, jax.ShapeDtypeStruct((1, rows, 2 * half), BF16)]
    args = (left, left_got.reshape(left.shape), right, right_got.reshape(right.shape))
    return whole_call(body, scalars, args, out_shape, "fold_halves")


def join(scalars, keep, got):
    def body(sc, keep_ref, got_ref, out):
        out[...] = (keep_ref[...].astype(F32) + got_ref[...].astype(F32)).astype(BF16)

    out_shape = [jax.ShapeDtypeStruct(keep.shape, BF16)]
    return whole_call(body, scalars, (keep, got.reshape(keep.shape)), out_shape, "join")[0]


def append(scalars, held, got):
    def body(sc, held_ref, got_ref, out):
        count = held_ref.shape[0]
        out[0:count] = held_ref[...]
        out[count : 2 * count] = got_ref[...]

    out_shape = [jax.ShapeDtypeStruct((2 * held.shape[0], *held.shape[1:]), held.dtype)]
    return whole_call(body, scalars, (held, got), out_shape, "append")[0]


def merge_low(scalars, down, down_got, out, out_got, which):
    zys, lows, width = down.shape
    outs = out.shape[1]
    fill = -outs % 16

    def body(sc, down_ref, down_got_ref, out_ref, out_got_ref, keep_out, send_out):
        for i in range(zys // 2):
            for target, bit in ((keep_out, sc[which]), (send_out, 1 - sc[which])):
                t = 2 * i + bit
                first = down_ref[t].astype(F32) + down_got_ref[t].astype(F32)
                second = out_ref[t].astype(F32) + out_got_ref[t].astype(F32)
                rows = [first, second] + ([jnp.zeros((fill, width), F32)] if fill else [])
                target[i] = jnp.concatenate(rows, axis=0).astype(target.dtype)

    shape = (zys // 2, lows + outs + fill, width)
    out_shape = [jax.ShapeDtypeStruct(shape, F32), jax.ShapeDtypeStruct(shape, BF16)]
    args = (down, down_got.reshape(down.shape), out, out_got.reshape(out.shape))
    return whole_call(body, scalars, args, out_shape, "merge_low")


def first_norm_back(scalars, tokens, dy, gain, parts):
    nseq, rows, width = tokens.shape

    def body(sc, tokens_ref, dy_ref, gain_ref, lk, rk, got, out):
        seq = sc[6]
        for i in range(nseq):
            here = seq == i
            dh = jnp.where(here, jnp.concatenate([lk[0], rk[0]], axis=1), got[0].astype(F32))
            n, scale = normed_parts(tokens_ref[i].astype(F32))
            out[i] = dy_ref[i] + norm_back(dh, n, scale, gain_ref[...])

    out_shape = [jax.ShapeDtypeStruct(tokens.shape, F32)]
    return whole_call(body, scalars, (tokens, dy, gain, *parts), out_shape, "first_norm_back")[0]


def piece_of(places):
    def block(t, sc):
        d = t ^ sc[0]
        return (d % 2 * 2 ** places[0] + d // 2 % 2 * 2 ** places[1] + d // 4 % 2 * 2 ** places[2], 0, 0)

    return block


def up_rows_kernel(parts, sc, own_ref, other_ref, out_ref):
    first = sc[3] == 0
    own, other = own_ref[0].astype(F32), other_ref[0].astype(F32)
    split = own.shape[1] // parts
    for p in range(parts):
        cols = slice(p * split, (p + 1) * split)
        out_ref[0, :, 2 * p * split : (2 * p + 1) * split] = jnp.where(first, own[:, cols], other[:, cols])
        out_ref[0, :, (2 * p + 1) * split : (2 * p + 2) * split] = jnp.where(first, other[:, cols], own[:, cols])


def up_rows(scalars, own, other, parts):
    pieces, high, wide = own.shape
    return pl.pallas_call(
        functools.partial(up_rows_kernel, parts),
        grid_spec=pltpu.PrefetchScalarGridSpec(
            num_scalar_prefetch=1,
            grid=(pieces,),
            in_specs=[pl.BlockSpec((1, high, wide), piece_of((2, 1, 0)))] * 2,
            out_specs=pl.BlockSpec((1, high, 2 * wide), lambda t, sc: (t, 0, 0)),
        ),
        out_shape=jax.ShapeDtypeStruct((pieces, high, 2 * wide), F32),
        compiler_params=pltpu.CompilerParams(vmem_limit_bytes=8 * MIB),
        cost_estimate=FREE,
        name="up_rows",
    )(scalars, own, other)


def low_rows_kernel(lows, outs, sc, own_ref, other_ref, down_ref, out_ref):
    first = sc[3] == 0
    own, other = own_ref[0].astype(F32), other_ref[0].astype(F32)
    for c, value in enumerate((jnp.where(first, own, other), jnp.where(first, other, own))):
        down_ref[c, 0] = value[:lows]
        out_ref[c, 0] = value[lows : lows + outs]


def low_rows(scalars, own, other, lows, outs):
    pieces, low, width = own.shape
    return pl.pallas_call(
        functools.partial(low_rows_kernel, lows, outs),
        grid_spec=pltpu.PrefetchScalarGridSpec(
            num_scalar_prefetch=1,
            grid=(pieces,),
            in_specs=[pl.BlockSpec((1, low, width), piece_of((1, 2, 0)))] * 2,
            out_specs=[
                pl.BlockSpec((2, 1, lows, width), lambda t, sc: (0, t, 0, 0)),
                pl.BlockSpec((2, 1, outs, width), lambda t, sc: (0, t, 0, 0)),
            ],
        ),
        out_shape=[
            jax.ShapeDtypeStruct((2, pieces, lows, width), F32),
            jax.ShapeDtypeStruct((2, pieces, outs, width), F32),
        ],
        compiler_params=pltpu.CompilerParams(vmem_limit_bytes=8 * MIB),
        cost_estimate=FREE,
        name="low_rows",
    )(scalars, own, other)


def qkv_rows_kernel(groups, high, own, gw, sc, own_ref, other_ref, out_ref, gain_ref, conv_ref):
    core = sc[3]
    swapped = [(g ^ sc[4]) % 2 * 2 + (g ^ sc[4]) // 2 for g in range(groups)]
    convs = []
    gains = None
    for k in swapped:
        tail = own_ref[k].astype(F32)[high:]
        gains = tail[0:4, :own] if gains is None else gains + tail[0:4, :own]
        convs.append(tail[4:7, :])
    gain_ref[...] = gains
    for j in range(3):
        cols = slice(j * gw, (j + 1) * gw)
        conv_ref[:, j * groups * gw : (j + 1) * groups * gw] = jnp.concatenate([c[:, cols] for c in convs], axis=1)
    for c in range(2):
        pieces = [jnp.where(core == c, own_ref[k], other_ref[k]).astype(F32) for k in swapped]
        for j in range(3):
            cols = slice(j * gw, (j + 1) * gw)
            out = slice(j * groups * gw, (j + 1) * groups * gw)
            out_ref[c, :, out] = jnp.concatenate([p[:high, cols] for p in pieces], axis=1)


def qkv_rows(scalars, args, high):
    groups, _, cols = args[0].shape
    own = 2 * high
    shapes = [(2, high, groups * cols), (4, own), (3, groups * cols)]
    out_shape = [jax.ShapeDtypeStruct(shape, F32) for shape in shapes]
    return whole_call(
        functools.partial(qkv_rows_kernel, groups, high, own, cols // 3), scalars, args, out_shape, "qkv_rows"
    )


def per_device(tokens, cotangent, lengths, ln1_gain, ln1_bias, w_qkv, w_conv, w_out, ln2_gain, ln2_bias, w_up, w_down):
    nseq, rows, width = tokens.shape
    half = width // 2
    count = lax.axis_size("ctx")
    parts = lax.axis_size("fsdp")
    rank = lax.axis_index("ctx")
    index = lax.axis_index("fsdp")
    hidden = w_up.shape[1]
    zys = nseq * GROUPS
    share = count // zys
    hp = HEADS // GROUPS
    hd = width // HEADS
    gw = hp * hd
    mine = rank % share
    core = rank % 2
    zy = rank // share
    seq = zy // GROUPS
    group = zy % GROUPS
    bit_b, bit_a, bit_s = share, 2 * share, 4 * share
    share_bits = bits(share)
    positions = rank * rows + jnp.arange(rows, dtype=jnp.int32)
    valid = positions[None, :] < lengths[:, None]
    high_bits = [index // mask % 2 for mask in reversed(bits(parts))]
    scalars = [zy, mine, lengths[seq], core, group, index, seq, zy // 2 % 2, zy % 2] + high_bits
    scalars = jnp.stack(scalars).astype(jnp.int32)
    at_s, at_a, at_b, at_x = 6, 7, 8, 9

    own_seq, far_seq = at(tokens, seq), at(tokens, 1 - seq)
    w_qkv, w_conv = lax.optimization_barrier((w_qkv, w_conv, far_seq))[:2]
    pair = jnp.stack([own_seq, exch(far_seq, "ctx", bit_s)])
    left, right = pair[..., :half], pair[..., half:]
    w_up, w_down, w_out = lax.optimization_barrier((w_up, w_down, w_out, left, right))[:3]
    left = jnp.stack([left, exch(left, "ctx", bit_a)], axis=1)
    right = jnp.stack([right, exch(right, "ctx", bit_b)], axis=1)
    left = jnp.stack([left, exch(left, "ctx", bit_b)], axis=2)
    right = jnp.stack([right, exch(right, "ctx", bit_a)], axis=1)
    left = gather_list(left.reshape(1, zys, rows, half), "ctx", share_bits)
    right = gather_list(right.reshape(1, zys, rows, half), "ctx", share_bits)

    small = jnp.concatenate([ln1_gain, ln1_bias, ln2_gain, ln2_bias, w_conv.reshape(-1)])
    small = gather_fsdp(small.reshape(1, -1)).reshape(parts, -1).astype(F32)
    own_rows = ln1_gain.shape[0]
    gains = small[:, : 4 * own_rows].reshape(parts, 4, own_rows).transpose(1, 0, 2).reshape(4, 1, width)
    gain_one, bias_one, gain_two, bias_two = gains[0], gains[1], gains[2], gains[3]
    taps = small[:, 4 * own_rows :].reshape(parts, 3, -1).transpose(1, 0, 2).reshape(3, 3, width)
    taps = lax.dynamic_slice_in_dim(taps, group * gw, gw, 2).reshape(3, 3 * gw)
    fsdp_bits = bits(parts)
    split = hidden // parts // 2
    both_cores = lambda pieces: [pieces, [exch(piece, "ctx", 1) for piece in pieces]]
    qkv = both_cores(gather_list(qkv_part(scalars, w_qkv, gw)[None], "fsdp", fsdp_bits))
    if split == width:
        ups = gather_list(rest_part(scalars, w_up, w_down, w_out, parts), "fsdp", fsdp_bits)
        downs = []
        out_w = [ups, [exch(rest[:, parts * own_rows + split :], "ctx", 1) for rest in ups]]
    else:
        out_w = both_cores(gather_list(at(w_out.reshape(2, own_rows // 2, width), core)[None], "fsdp", fsdp_bits))
        ups = gather_list(up_part(scalars, w_up, parts)[None], "fsdp", fsdp_bits)
        downs = gather_list(at(w_down.reshape(2, split, width), core)[None], "fsdp", fsdp_bits)

    h_one, pre, attn_t, o, lse, q, k, kt, v = attention(
        scalars, left, right, qkv, taps, gain_one, bias_one, share, hp, hd
    )
    classes = [[i for i in range(count) if i % share == s] for s in range(share)]
    swap = lambda x: lax.all_to_all(x, "ctx", 0, 0, tiled=True, axis_index_groups=classes)
    attn_t = swap(attn_t).reshape(nseq, width, rows)

    order = Order()
    dtop = jnp.where(valid[..., None], cotangent, jnp.zeros_like(cotangent)).reshape(nseq * rows, width)
    dtop_other = exch(dtop, "ctx", 1)
    y_one, h_two = mix(scalars, attn_t, tokens, gain_two, bias_two, out_w, parts)
    h_other = exch(h_two, "ctx", 1)
    r, dupper, dh_keep, dh_send, y_keep, y_send = feed(
        scalars, h_two, h_other, dtop, dtop_other, ups, downs, split
    )
    dh_other = exch(dh_send, "ctx", 1)
    h_pair = jnp.concatenate([h_two, h_other], axis=1)
    dtop_pair = jnp.concatenate([dtop, dtop_other])

    near_base = index // (parts // 2) * (parts // 2)

    def near(term):
        return jnp.stack([term(near_base + p) for p in range(parts // 2)])

    def fsdp_start(term):
        far = [term(parts // 2 - near_base + p) for p in range(parts // 2)]
        return exch(jnp.stack(far).astype(BF16), "fsdp", parts // 2)

    def fsdp_more(keep, got):
        for i, mask in enumerate(reversed(fsdp_bits[:-1])):
            keep, send = fold(scalars, keep.reshape(1, 2, mask, *keep.shape[1:]), got, at_x + 1 + i)
            keep, got = keep[0], exch(send[0], "fsdp", mask)
        return keep, got

    down_term = lambda p: tn(at(r, p), dtop_pair)
    down_got = fsdp_start(down_term)
    dh_keep, dh_other = order(dh_keep, dh_other)
    dy_one, dy_low, dout_t, small_two = mix_back(scalars, dh_keep, dh_other, y_one, dtop, gain_two, out_w)
    order.mark(dout_t)
    r, dupper, y_keep, y_send, h_pair = order(r, dupper, y_keep, y_send, h_pair)
    dout_t = swap(dout_t.reshape(zys, gw, rows))

    def cut(held, axis, bit):
        keep = lax.dynamic_slice_in_dim(held, bit, 1, axis)
        send = lax.dynamic_slice_in_dim(held, 1 - bit, 1, axis)
        return keep, send.astype(BF16)

    zy_bits = {"s": (0, bit_s, zy // 4), "a": (1, bit_a, zy // 2 % 2), "b": (2, bit_b, zy % 2)}
    grad_out = jnp.einsum("sct,std->cd", attn_t, dy_low, preferred_element_type=F32)
    grad_out = grad_out.reshape(parts, 2, own_rows // 2, width)
    grad_out = lax.dynamic_index_in_dim(grad_out, core, 1, keepdims=False) + exch(
        lax.dynamic_index_in_dim(grad_out, 1 - core, 1, keepdims=False).astype(BF16), "ctx", 1
    ).astype(F32)
    out_got = fsdp_start(lambda p: at(grad_out, p))
    out_keep = near(lambda p: at(grad_out, p))
    grad_up = jnp.einsum("pnk,nf->pkf", h_pair, dupper, preferred_element_type=F32)
    grad_up = grad_up.reshape(parts, 2, 2, 2, own_rows // zys, hidden // 2)
    up_keep, up_send = cut(grad_up, 2, zy_bits["a"][2])
    down_keep = near(down_term)
    result = y_one + (y_keep + exch(y_send, "ctx", 1).astype(F32)).reshape(nseq, rows, width)
    output = jnp.where(valid[..., None], result, 0.0).astype(BF16)

    dout_t, up_keep, up_send, down_keep, out_keep, output = lax.optimization_barrier(
        (dout_t, up_keep, up_send, down_keep, out_keep, output)
    )
    up_got = exch(up_send, "ctx", bit_a)
    lows = down_keep.shape[1] // zys
    outs = out_keep.shape[1] // zys
    high = own_rows // zys
    up_rest = (high, hidden // 2)
    tail_rows = own_rows // 2 + TAIL
    dw_rest = (tail_rows, 3 * gw)

    keep = {"up": up_keep, "down": down_keep, "out": out_keep, "dout": dout_t}
    got = {"up": up_got, "down": down_got, "out": out_got}
    heads_keep, heads_got = [], []
    done = {}

    def fold_step(x, which, shape, axis, mask):
        def run():
            kept, send = fold(scalars, order(keep[x]).reshape(shape), got[x], which)
            order.mark(send)
            keep[x] = kept
            got[x] = exch(send, axis, mask)

        return run

    def join_step(x, shape, mask):
        def run():
            keep[x] = order.mark(join(scalars, order(keep[x]).reshape(shape), got[x]))
            got[x] = exch(keep[x], "ctx", mask)

        return run

    def append_step(x, mask):
        def run():
            keep[x] = order.mark(append(scalars, order(keep[x]), got[x]))
            got[x] = exch(keep[x], "ctx", mask)

        return run

    def head(h):
        def run():
            kept, sent = attend_back(scalars, h, q, k, kt, v, order(keep["dout"]), o, lse, share, rows)
            heads_keep.append(order.mark(kept))
            heads_got.extend(exch(sent[x - 1 : x], "ctx", x) for x in range(1, share))

        return run

    def low_first():
        keep["down"], keep["out"] = order(keep["down"], keep["out"])
        for x in ("down", "out"):
            keep[x], got[x] = fsdp_more(keep[x], got[x])
        kept, send = merge_low(
            scalars,
            keep["down"].reshape(zys, lows, width),
            got["down"],
            keep["out"].reshape(zys, outs, width),
            got["out"],
            at_b,
        )
        order.mark(send)
        keep["low"] = kept
        got["low"] = exch(send, "ctx", bit_b)

    low_rest = (lows + outs + -outs % 16, width)

    def up_between():
        keep["up"], got["up"] = fsdp_more(keep["up"].reshape(parts // 2, 2, 2, *up_rest), got["up"])
        fold_step("up", at_b, (2, 2, *up_rest), "ctx", bit_b)()

    def back():
        last = order(heads_keep[-1])
        left_keep, left_send, right_keep, right_send, dw_keep, dw_send = project_back(
            scalars, heads_keep[:-1] + [last], heads_got, left[0], right[0], h_one, pre, taps, small_two, qkv,
            share, rows, parts,
        )
        order.mark(dw_send)
        keep.update(left=left_keep, right=right_keep, qkv=dw_keep)
        got["left"] = exch(left_send, "ctx", bit_a)
        got["right"] = exch(right_send, "ctx", bit_b)
        got["qkv"] = exch(dw_send, "ctx", 1)

    def qkv_between():
        keep["qkv"], got["qkv"] = fsdp_more(keep["qkv"].reshape(parts // 2, *dw_rest), got["qkv"])
        join_step("qkv", dw_rest, bit_s)()

    def qkv_whole():
        block = join(scalars, order(keep["qkv"]), got["qkv"])
        for mask in share_bits[1:]:
            block = join(scalars, block, exch(block, "ctx", mask))
        keep["qkv"] = order.mark(block[None])
        got["qkv"] = exch(keep["qkv"], "ctx", bit_a)

    def halves():
        kept = order(keep["left"], keep["right"])
        keep["left"], keep["right"], send = fold_halves(scalars, kept[0], got["left"], kept[1], got["right"])
        order.mark(send)
        got["input"] = exch(send, "ctx", bit_s)

    def input_end():
        kept = (keep["left"], keep["right"], got["input"])
        done["input"] = order.mark(first_norm_back(scalars, tokens, order(dy_one), gain_one, kept))

    def qkv_end():
        grad, gains, convs = qkv_rows(scalars, (order(keep["qkv"]), got["qkv"]), own_rows // 2)
        done["qkv"] = order.mark(grad.reshape(own_rows, 3 * width))
        share_cols = 3 * width // parts
        done["gains"] = gains
        done["conv"] = lax.dynamic_slice_in_dim(convs, index * share_cols, share_cols, 1)

    def low_end():
        down_grad, out_grad = low_rows(scalars, order(keep["low"]), got["low"], lows, outs)
        done["down"] = order.mark(down_grad.reshape(hidden // parts, width))
        done["out"] = out_grad.reshape(own_rows, width)

    def up_end():
        grad = up_rows(scalars, order(keep["up"]), got["up"], parts)
        done["up"] = order.mark(grad.reshape(own_rows, hidden))

    steps = {
        "head 0": head(0),
        "head 1": head(1),
        "head 2": head(2),
        "low b": low_first,
        "low a": fold_step("low", at_a, (2, 2, *low_rest), "ctx", bit_a),
        "low s": fold_step("low", at_s, (1, 2, *low_rest), "ctx", bit_s),
        "low sum": join_step("low", (1, *low_rest), bit_s),
        "low gather b": append_step("low", bit_b),
        "low gather a": append_step("low", bit_a),
        "low core": append_step("low", 1),
        "low end": low_end,
        "up x": fold_step("up", at_x, (1, 2, parts // 2 * 4 * high, hidden // 2), "fsdp", parts // 2),
        "up b": up_between,
        "up s": fold_step("up", at_s, (1, 2, *up_rest), "ctx", bit_s),
        "up sum": join_step("up", (1, *up_rest), bit_s),
        "up gather a": append_step("up", bit_a),
        "up gather b": append_step("up", bit_b),
        "up core": append_step("up", 1),
        "up end": up_end,
        "back": back,
        "qkv x": fold_step("qkv", at_x, (1, 2, parts // 2, *dw_rest), "fsdp", parts // 2),
        "qkv s": qkv_between,
        "qkv a": qkv_whole,
        "qkv gather b": append_step("qkv", bit_b),
        "qkv core": append_step("qkv", 1),
        "qkv end": qkv_end,
        "right a": fold_step("right", None, (1, 2, 2, rows, half), "ctx", bit_a),
        "left b": fold_step("left", None, (1, 2, 2, rows, half), "ctx", bit_b),
        "input s": halves,
        "input end": input_end,
    }
    for name in LINE:
        steps[name]()
    input_grad, gains = done["input"], done["gains"]
    w_qkv_grad, w_conv_grad, w_out_grad = done["qkv"], done["conv"], done["out"]
    w_up_grad, w_down_grad = done["up"], done["down"]

    return (
        output,
        input_grad,
        gains[0],
        gains[1],
        w_qkv_grad,
        w_conv_grad,
        w_out_grad,
        gains[2],
        gains[3],
        w_up_grad,
        w_down_grad,
    )


def solution(mesh):
    rows = P("fsdp", "ctx", None)
    first = P("fsdp")
    weight = P("fsdp", None)
    second = P(None, "fsdp")
    in_specs = (rows, rows, first, first, first, weight, second, weight, first, first, weight, weight)
    out_specs = (rows, rows, first, first, weight, second, weight, first, first, weight, weight)
    return jax.shard_map(per_device, mesh=mesh, in_specs=in_specs, out_specs=out_specs, check_vma=False)
```

```python
import functools

import jax
import jax.numpy as jnp
from jax import lax
from jax.experimental import pallas as pl
from jax.experimental.pallas import tpu as pltpu
from jax.sharding import PartitionSpec as P

HEADS = 12
GROUPS = 4
EPS = 1e-05
RIM = 16
PIECES = 8
TAIL = 16
MASKED = -1e30
MIB = 1024 * 1024
F32 = jnp.float32
BF16 = jnp.bfloat16
LINE = (
    "head 0",
    "low b",
    "head 1",
    "head 2",
    "up x",
    "low a",
    "back",
    "low s",
    "up b",
    "qkv x",
    "low sum",
    "up s",
    "right a",
    "low gather b",
    "up sum",
    "left b",
    "qkv s",
    "up gather a",
    "input s",
    "low gather a",
    "qkv a",
    "up gather b",
    "qkv gather b",
    "up core",
    "low core",
    "low end",
    "input end",
    "qkv core",
    "up end",
    "qkv end",
)
FREE = pl.CostEstimate(flops=0, bytes_accessed=0, transcendentals=0)


def exch(value, axis, mask):
    count = lax.axis_size(axis)
    return lax.ppermute(value, axis, [(i, i ^ mask) for i in range(count)])


def bits(count):
    return [1 << b for b in range(count.bit_length() - 1)]


def at(stack, index):
    return lax.dynamic_index_in_dim(stack, index, 0, keepdims=False)


def flip(stack, index):
    return jnp.stack([at(stack, k ^ index) for k in range(stack.shape[0])])


def gather_list(value, axis, masks):
    held = [value]
    for mask in masks:
        held.append(exch(held[0] if len(held) == 1 else jnp.concatenate(held), axis, mask))
    return held


def after(value, *others):
    return lax.optimization_barrier((value, *others))[0]


class Order:
    def __init__(self):
        self.last = None

    def __call__(self, *values):
        if self.last is not None:
            values = lax.optimization_barrier((*values, self.last))[:-1]
        return values if len(values) > 1 else values[0]

    def mark(self, value):
        self.last = value
        return value


def normed_parts(values):
    centre = values - jnp.mean(values, axis=-1, keepdims=True)
    scale = lax.rsqrt(jnp.mean(centre * centre, axis=-1, keepdims=True) + EPS)
    return centre * scale, scale


def norm_back(grad, normed, scale, gain):
    dnorm = grad * gain
    return scale * (
        dnorm
        - jnp.mean(dnorm, axis=-1, keepdims=True)
        - normed * jnp.mean(dnorm * normed, axis=-1, keepdims=True)
    )


def nn(a, b):
    return lax.dot_general(a, b, (((1,), (0,)), ((), ())), preferred_element_type=F32)


def nt(a, b):
    return lax.dot_general(a, b, (((1,), (1,)), ((), ())), preferred_element_type=F32)


def tn(a, b):
    return lax.dot_general(a, b, (((0,), (0,)), ((), ())), preferred_element_type=F32)


def piece_copies(lists, scratch, sems, index, core, take=None, cols=None):
    copies = []
    cores = len(lists)
    for r, pieces in enumerate(lists):
        k = 0
        for stack in pieces:
            for i in range(stack.shape[0]):
                first, size = take or (0, stack.shape[1])
                part = (core ^ r) if cores == 2 else 0
                start = pl.multiple_of(((index ^ k) * cores + part) * size, size)
                target = scratch.at[pl.ds(start, size)] if cols is None else scratch.at[pl.ds(start, size), cols]
                source = stack.at[i, pl.ds(first, size)]
                copies.append(pltpu.make_async_copy(source, target, sems.at[len(copies)]))
                k += 1
    return copies


def fsdp_size(lists):
    return sum(stack.shape[0] for stack in lists[0])


def split_lists(refs, counts):
    lists, at_ref = [], 0
    for n in counts:
        lists.append(refs[at_ref : at_ref + n])
        at_ref += n
    return lists, refs[at_ref:]


ANY = pl.BlockSpec(memory_space=pl.ANY)


def pack(scalars, gains, w_conv):
    own = gains[0].shape[0]
    cols = w_conv.shape[1]

    def body(sc, *refs):
        rows = [jnp.concatenate([ref[...].astype(F32), jnp.zeros((1, cols - own), F32)], axis=1) for ref in refs[:4]]
        rows += [refs[4][...].astype(F32), jnp.zeros((16 - 7, cols), F32)]
        refs[5][0] = jnp.concatenate(rows, axis=0).astype(BF16)

    args = [g.reshape(1, own) for g in gains] + [w_conv]
    return whole_call(body, scalars, args, [jax.ShapeDtypeStruct((1, 16, cols), BF16)], "pack")[0]


def parameters(scalars, packed, own, gw):
    parts = sum(stack.shape[0] for stack in packed)
    cols = packed[0].shape[2]
    total = parts * cols // 3

    def body(sc, *refs):
        held = [ref[i].astype(F32) for ref in refs[:-2] for i in range(ref.shape[0])]
        ordered = []
        for p in range(parts):
            picked = held[0]
            for k in range(1, parts):
                picked = jnp.where((p ^ sc[5]) == k, held[k], picked)
            ordered.append(picked)
        refs[-2][...] = jnp.concatenate([x[0:4, :own] for x in ordered], axis=1)
        taps = jnp.concatenate([x[4:7] for x in ordered], axis=1)
        for j in range(3):
            picked = taps[:, j * total : j * total + gw]
            for g in range(1, GROUPS):
                start = j * total + g * gw
                picked = jnp.where(sc[4] == g, taps[:, start : start + gw], picked)
            refs[-1][:, j * gw : (j + 1) * gw] = picked

    out_shape = [jax.ShapeDtypeStruct((4, parts * own), F32), jax.ShapeDtypeStruct((3, 3 * gw), F32)]
    return whole_call(body, scalars, packed, out_shape, "parameters")


def first_part_kernel(groups, gw, sc, w, w_out, out):
    group = sc[4]
    rows = w.shape[0]
    width = groups * gw
    for j in range(3):
        picked = w[:, j * width : j * width + gw]
        for g in range(1, groups):
            start = j * width + g * gw
            picked = jnp.where(group == g, w[:, start : start + gw], picked)
        out[0, :rows, j * gw : (j + 1) * gw] = picked
    out[0, :rows, 3 * gw :] = jnp.zeros((rows, width - 3 * gw), BF16)
    out[0, rows:, :] = w_out[...]


def first_part(scalars, w_qkv, w_out, gw):
    rows, cols = w_qkv.shape
    width = w_out.shape[1]
    return pl.pallas_call(
        functools.partial(first_part_kernel, GROUPS, gw),
        grid_spec=pltpu.PrefetchScalarGridSpec(
            num_scalar_prefetch=1,
            grid=(1,),
            in_specs=[
                pl.BlockSpec((rows // 2, cols), lambda i, sc: (sc[3], 0)),
                pl.BlockSpec((rows // 2, width), lambda i, sc: (sc[3], 0)),
            ],
            out_specs=pl.BlockSpec((1, rows, width), lambda i, sc: (0, 0, 0)),
        ),
        out_shape=jax.ShapeDtypeStruct((1, rows, width), BF16),
        compiler_params=pltpu.CompilerParams(vmem_limit_bytes=8 * MIB),
        cost_estimate=FREE,
        name="first_part",
    )(scalars, w_qkv, w_out)


def up_part_kernel(sc, w, out):
    out[...] = w[...]


def up_part(scalars, w_up, parts):
    rows, cols = w_up.shape
    split = cols // parts // 2
    if split % 128:
        picked = lax.dynamic_index_in_dim(w_up.reshape(rows, parts, 2, split), scalars[3], 2, keepdims=False)
        return picked.reshape(rows, cols // 2)
    return pl.pallas_call(
        up_part_kernel,
        grid_spec=pltpu.PrefetchScalarGridSpec(
            num_scalar_prefetch=1,
            grid=(parts,),
            in_specs=[pl.BlockSpec((rows, split), lambda p, sc: (0, 2 * p + sc[3]))],
            out_specs=pl.BlockSpec((rows, split), lambda p, sc: (0, p)),
        ),
        out_shape=jax.ShapeDtypeStruct((rows, cols // 2), BF16),
        compiler_params=pltpu.CompilerParams(vmem_limit_bytes=8 * MIB),
        cost_estimate=FREE,
        name="up_part",
    )(scalars, w_up)


def rest_part_kernel(parts, sc, w_up, w_down, out, sems):
    core = sc[3]
    own, cols = w_up.shape
    split = cols // parts // 2
    copies = []
    for p in range(parts):
        source = w_up.at[:, pl.ds(pl.multiple_of((2 * p + core) * split, split), split)]
        copies.append(pltpu.make_async_copy(source, out.at[0, pl.ds(p * own, own)], sems.at[p]))
    source = w_down.at[pl.ds(pl.multiple_of(core * split, split), split)]
    copies.append(pltpu.make_async_copy(source, out.at[0, pl.ds(parts * own, split)], sems.at[parts]))
    for copy in copies:
        copy.start()
    for copy in copies:
        copy.wait()


def rest_part(scalars, w_up, w_down, parts):
    own, cols = w_up.shape
    split = cols // parts // 2
    rows = parts * own + split
    return pl.pallas_call(
        functools.partial(rest_part_kernel, parts),
        grid_spec=pltpu.PrefetchScalarGridSpec(
            num_scalar_prefetch=1,
            grid=(1,),
            in_specs=[ANY] * 2,
            out_specs=ANY,
            scratch_shapes=[pltpu.SemaphoreType.DMA((parts + 1,))],
        ),
        out_shape=jax.ShapeDtypeStruct((1, rows, split), BF16),
        compiler_params=pltpu.CompilerParams(vmem_limit_bytes=2 * MIB),
        cost_estimate=FREE,
        name="rest_part",
    )(scalars, w_up, w_down)


def attention_kernel(share, hp, hd, rows, per, last, shares, counts, sc, *refs):
    (left, right), refs = split_lists(refs, (len(shares), len(shares)))
    taps, gain, bias = refs[:3]
    lists, refs = split_lists(refs[3:], counts)
    h_ref, pre_ref, at_ref, o_ref, lse_ref = refs[:5]
    kept = refs[5:9]
    buf, w, sems, save_sems, q_ref, k_ref, kt_ref, v_ref, vt_ref = refs[9:]
    step = pl.program_id(0)
    saves = [
        pltpu.make_async_copy(source, target, save_sems.at[i])
        for i, (source, target) in enumerate(zip((q_ref, k_ref, kt_ref, v_ref), kept))
    ]

    @pl.when(step <= last)
    def _():
        project_step(share, hp, hd, rows, per, sc, left, right, taps, gain, bias, lists, h_ref, pre_ref, q_ref, k_ref,
                     kt_ref, v_ref, vt_ref, buf, w, sems)

    @pl.when(step == last + 1)
    def _():
        for copy in saves:
            copy.start()

    @pl.when(step > last)
    def _():
        attend_step(share, rows, sc, step - last - 1, q_ref, k_ref, vt_ref, at_ref, o_ref, lse_ref)

    @pl.when(step == last + hp)
    def _():
        for copy in saves:
            copy.wait()


def project_step(share, hp, hd, rows, per, sc, left, right, taps, gain, bias, lists, h_ref, pre_ref, q_ref, k_ref,
                 kt_ref, v_ref, vt_ref, buf, w, sems):
    step = pl.program_id(0)

    @pl.when(step == 0)
    def _():
        copies = piece_copies(lists, w, sems, sc[5], sc[3], (0, w.shape[0] // 2 // fsdp_size(lists)))
        for copy in copies:
            copy.start()
        for copy in copies:
            copy.wait()

    mine = sc[1]
    length = sc[2]
    gw = hp * hd
    size = per * share * rows
    parts = []
    for z in range(per):
        at_z = z ^ (sc[0] % per)
        pieces = []
        for refs_l, refs_r in zip(left, right):
            pieces += [jnp.concatenate([refs_l[i, at_z], refs_r[i, at_z]], axis=1) for i in range(refs_l.shape[0])]
        for j in range(share):
            picked = pieces[0]
            for k in range(1, share):
                picked = jnp.where((j ^ mine) == k, pieces[k], picked)
            parts.append(picked.astype(F32))
    x = jnp.concatenate(parts, axis=0)
    n, _ = normed_parts(x)
    h = (n * gain[...] + bias[...]).astype(BF16)
    h_ref[...] = h
    pre = nn(h, w[:, : 3 * gw]).astype(BF16)
    pre_ref[...] = pre

    @pl.when(step == 0)
    def _():
        buf[0:8, :] = jnp.zeros((8, 3 * gw), F32)

    buf[8:, :] = pre.astype(F32)
    conv = (
        taps[0:1, :] * buf[8 : 8 + size, :]
        + taps[1:2, :] * buf[7 : 7 + size, :]
        + taps[2:3, :] * buf[6 : 6 + size, :]
    )
    buf[0:8, :] = buf[size : size + 8, :]
    qs = conv[:, :gw].astype(BF16)
    kf = conv[:, gw : 2 * gw]
    vf = conv[:, 2 * gw :]
    q_own = []
    for z in range(per):
        start = z * share * rows
        picked = qs[start : start + rows]
        for j in range(1, share):
            picked = jnp.where(mine == j, qs[start + j * rows : start + (j + 1) * rows], picked)
        q_own.append(picked)
    q_own = (jnp.concatenate(q_own, axis=0).astype(F32) * 0.125).astype(BF16)
    lane = lax.broadcasted_iota(jnp.int32, (per * rows, hd), 1)
    ones = jnp.where(lane == 0, 1.0, 0.0).astype(BF16)
    lane = lax.broadcasted_iota(jnp.int32, (size, hd), 1)
    pos = step * size + lax.broadcasted_iota(jnp.int32, (size, hd), 0)
    mask = jnp.where((lane == 0) & (pos >= length), MASKED, 0.0).astype(BF16)
    ks = kf.astype(BF16)
    vs = vf.astype(BF16)
    kt = kf.T.astype(BF16)
    vt = vf.T.astype(BF16)
    own = pl.ds(pl.multiple_of(step * per * rows, per * rows), per * rows)
    every = pl.ds(pl.multiple_of(step * size, size), size)
    for h in range(hp):
        cols = slice(h * hd, (h + 1) * hd)
        q_ref[h, own, :] = jnp.concatenate([q_own[:, cols], ones], axis=1)
        k_ref[h, every, :] = jnp.concatenate([ks[:, cols], mask], axis=1)
        v_ref[h, every, :] = vs[:, cols]
        kt_ref[h, :, every] = kt[cols]
        vt_ref[h, :, every] = vt[cols]


def attention(scalars, left, right, w_lists, taps, gain, bias, share, hp, hd):
    counts = [len(pieces) for pieces in w_lists]
    flat = [piece for pieces in w_lists for piece in pieces]
    _, zys, rows, half = left[0].shape
    width = 2 * half
    gw = hp * hd
    per = 2
    last = zys // per - 1
    total = zys * share * rows
    own = zys * rows
    size = per * share * rows
    shares = [a.shape[0] for a in left]
    body = functools.partial(attention_kernel, share, hp, hd, rows, per, last, shares, counts)
    whole = lambda *shape: pl.BlockSpec(shape, lambda t, sc: (0,) * len(shape))
    block = lambda t: jnp.minimum(t, last)
    head = lambda t: jnp.maximum(t - last - 1, 0)
    pieces = [pl.BlockSpec((n, per, rows, half), lambda t, sc: (0, block(t) ^ (sc[0] // per), 0, 0)) for n in shares]
    kept = [(hp, own, 2 * hd), (hp, total, 2 * hd), (hp, hd, total), (hp, total, hd)]
    return pl.pallas_call(
        body,
        grid_spec=pltpu.PrefetchScalarGridSpec(
            num_scalar_prefetch=1,
            grid=(last + 1 + hp,),
            in_specs=pieces * 2 + [whole(3, 3 * gw), whole(1, width), whole(1, width)] + [ANY] * len(flat),
            out_specs=[
                pl.BlockSpec((size, width), lambda t, sc: (block(t), 0)),
                pl.BlockSpec((size, 3 * gw), lambda t, sc: (block(t), 0)),
                pl.BlockSpec((zys, hd, rows), lambda t, sc: (0, head(t), 0)),
                pl.BlockSpec((1, hd, own), lambda t, sc: (head(t), 0, 0)),
                pl.BlockSpec((1, 1, own), lambda t, sc: (head(t), 0, 0)),
            ]
            + [ANY] * 4,
            scratch_shapes=[
                pltpu.VMEM((8 + size, 3 * gw), F32),
                pltpu.VMEM((width, width), BF16),
                pltpu.SemaphoreType.DMA((2 * PIECES,)),
                pltpu.SemaphoreType.DMA((4,)),
            ]
            + [pltpu.VMEM(shape, BF16) for shape in kept + [(hp, hd, total)]],
        ),
        out_shape=[
            pltpu.HBM((total, width), BF16),
            pltpu.HBM((total, 3 * gw), BF16),
            jax.ShapeDtypeStruct((zys, gw, rows), BF16),
            pltpu.HBM((hp, hd, own), F32),
            jax.ShapeDtypeStruct((hp, 1, own), F32),
        ]
        + [pltpu.HBM(shape, BF16) for shape in kept],
        compiler_params=pltpu.CompilerParams(vmem_limit_bytes=32 * MIB),
        cost_estimate=FREE,
        name="attention",
    )(scalars, *left, *right, taps, gain, bias, *flat)


def seen(share, rows, mine, shape):
    key = lax.broadcasted_iota(jnp.int32, shape, 0)
    col = lax.broadcasted_iota(jnp.int32, shape, 1)
    query = jnp.where(col >= rows, share * rows + col - rows, col) + mine * rows
    return key <= query


def head_copies(sources, targets, sems, head, slot):
    return [
        pltpu.make_async_copy(source.at[pl.ds(head, 1)], target.at[pl.ds(slot, 1)], sems.at[i, slot])
        for i, (source, target) in enumerate(zip(sources, targets))
    ]


def attend_step(share, rows, sc, head, q_all, k_all, vt_all, at_ref, o_ref, lse_ref):
    mine = sc[1]
    q, k, vt = (buf.at[pl.ds(head, 1)] for buf in (q_all, k_all, vt_all))
    tile = 2 * rows
    step = share * tile
    hd = vt.shape[1]
    tiles = q.shape[1] // tile
    for t in range(tiles):
        queries = q[0, t * tile : (t + 1) * tile, :]
        scores = [nt(k[0, j * step : (j + 1) * step, :], queries) for j in range(t + 1)]
        scores[t] = jnp.where(seen(share, rows, mine, scores[t].shape), scores[t], MASKED)
        top = jnp.max(scores[t], axis=0, keepdims=True)
        for j in range(t):
            top = jnp.maximum(top, jnp.max(scores[j], axis=0, keepdims=True))
        total, accum = None, None
        for j in range(t + 1):
            probs = jnp.exp(scores[j] - top)
            term = jnp.sum(probs, axis=0, keepdims=True)
            total = term if total is None else total + term
            term = nn(vt[0, :, j * step : (j + 1) * step], probs.astype(BF16))
            accum = term if accum is None else accum + term
        out = accum / total
        o_ref[0, :, t * tile : (t + 1) * tile] = out
        lse_ref[0, :, t * tile : (t + 1) * tile] = top + jnp.log(total)
        low = out.astype(BF16)
        at_ref[2 * t] = low[:, :rows]
        at_ref[2 * t + 1] = low[:, rows:]


def attend_back_kernel(share, rows, head, sc, q_all, k_all, kt_all, v_all, o_all, dot_ref, lse, mine_ref, send_ref,
                       dq_acc, dk_acc, dv_acc, q, k, kt, v, o, sems):
    mine = sc[1]
    copies = head_copies((q_all, k_all, kt_all, v_all, o_all), (q, k, kt, v, o), sems, head, 0)
    for copy in copies:
        copy.start()
    own = q.shape[1]
    hd = v.shape[2]
    tile = 2 * rows
    step = share * tile
    tiles = own // tile
    total = tiles * step
    dq_acc[...] = jnp.zeros(dq_acc.shape, F32)
    dk_acc[total:, :] = jnp.zeros((RIM, hd), F32)
    dv_acc[total:, :] = jnp.zeros((RIM, hd), F32)
    for copy in copies:
        copy.wait()
    for t in reversed(range(tiles)):
        queries = q[0, t * tile : (t + 1) * tile, :]
        douts = jnp.concatenate([dot_ref[2 * t], dot_ref[2 * t + 1]], axis=1)
        outs = o[0, :, t * tile : (t + 1) * tile]
        logs = lse[0, :, t * tile : (t + 1) * tile]
        inner = jnp.sum(outs * douts.astype(F32), axis=0, keepdims=True)
        dqt = jnp.zeros((hd, tile), F32)
        for j in reversed(range(t + 1)):
            at_j = slice(j * step, (j + 1) * step)
            probs = jnp.exp(nt(k[0, at_j, :], queries) - logs)
            if j == t:
                probs = jnp.where(seen(share, rows, mine, probs.shape), probs, 0.0)
            dv = nt(probs.astype(BF16), douts)
            dprobs = nn(v[0, at_j, :], douts)
            dscores = (probs * (dprobs - inner)).astype(BF16)
            dk = nn(dscores, queries)[:, :hd]
            if t == tiles - 1:
                dv_acc[at_j, :] = dv
                dk_acc[at_j, :] = dk
            else:
                dv_acc[at_j, :] += dv
                dk_acc[at_j, :] += dk
            dqt += nn(kt[0, :, at_j], dscores)
        dq = (dqt * 0.125).T
        for b in (2 * t, 2 * t + 1):
            at_b = pl.ds(pl.multiple_of((b * share + mine) * rows, rows), rows)
            dq_acc[at_b, :] = dq[(b % 2) * rows : (b % 2 + 1) * rows]
    for b in range(own // rows):
        for r in range(share):
            start = (b * share + (mine ^ r)) * rows
            rows_i = pl.ds(pl.multiple_of(start, rows), rows + RIM)
            block = jnp.concatenate([acc[rows_i, :] for acc in (dq_acc, dk_acc, dv_acc)], axis=1)
            if r == 0:
                mine_ref[b] = block
            else:
                send_ref[r - 1, b] = block.astype(BF16)


def attend_back(scalars, head, q, k, kt, v, dout_t, o, lse, share, rows):
    hp, own, wide = q.shape
    total = k.shape[1]
    hd = v.shape[2]
    blocks = own // rows
    whole = lambda a: pl.BlockSpec(a.shape, lambda i, sc: (0,) * len(a.shape))
    one = lambda a: pl.BlockSpec((1, *a.shape[1:]), lambda i, sc: (head, 0, 0))
    out_shape = [
        pltpu.HBM((blocks, rows + RIM, 3 * hd), F32),
        jax.ShapeDtypeStruct((share - 1, blocks, rows + RIM, 3 * hd), BF16),
    ]
    return pl.pallas_call(
        functools.partial(attend_back_kernel, share, rows, head),
        grid_spec=pltpu.PrefetchScalarGridSpec(
            num_scalar_prefetch=1,
            grid=(1,),
            in_specs=[ANY] * 5 + [pl.BlockSpec((blocks, hd, rows), lambda i, sc: (0, head, 0)), one(lse)],
            out_specs=[whole(a) for a in out_shape],
            scratch_shapes=[pltpu.VMEM((total + RIM, hd), F32)] * 3
            + [pltpu.VMEM((1, *a.shape[1:]), a.dtype) for a in (q, k, kt, v, o)]
            + [pltpu.SemaphoreType.DMA((5, 1))],
        ),
        out_shape=out_shape,
        compiler_params=pltpu.CompilerParams(vmem_limit_bytes=16 * MIB),
        cost_estimate=FREE,
        name="attend_back",
    )(scalars, q, k, kt, v, o, dout_t, lse)


def project_back_kernel(share, rows, heads, parts, counts, sc, *refs):
    (kept, recv), refs = split_lists(refs, (heads, heads * (share - 1)))
    left, right, h_ref, pre_ref, taps, small_two = refs[:6]
    lists, refs = split_lists(refs[6:], counts)
    left_keep, left_send, right_keep, right_send, dw_keep, dw_send, buf, w, dw_acc, small_acc, conv_acc, sems = refs
    step = pl.program_id(0)
    steps = pl.num_programs(0)
    width = w.shape[0]
    half = width // 2

    @pl.when(step == 0)
    def _():
        copies = piece_copies(lists, w, sems, sc[5], sc[3], (0, w.shape[0] // 2 // fsdp_size(lists)))
        for copy in copies:
            copy.start()
        dw_acc[...] = jnp.zeros(dw_acc.shape, F32)
        small_acc[...] = jnp.zeros(small_acc.shape, F32)
        conv_acc[...] = jnp.zeros(conv_acc.shape, F32)
        for copy in copies:
            copy.wait()

    hd = kept[0].shape[2] // 3
    per = kept[0].shape[0]
    now, one, two, x = [], [], [], []
    for z in range(per):
        for i in range(heads):
            total = kept[i][z]
            for r in recv[i * (share - 1) : (i + 1) * (share - 1)]:
                total = total + r[0, z].astype(F32)
            for j in range(3):
                start = (j * heads + i) * hd
                buf[z, :, start : start + hd] = total[:, j * hd : (j + 1) * hd]
        now.append(buf[z, 0:rows, :])
        one.append(buf[z, 1 : rows + 1, :])
        two.append(buf[z, 2 : rows + 2, :])
        at_z = z ^ (sc[0] % per)
        x.append(jnp.concatenate([left[0, at_z], right[0, at_z]], axis=1))
    now, one, two, x = (jnp.concatenate(v, axis=0) for v in (now, one, two, x))
    dpre = (taps[0:1, :] * now + taps[1:2, :] * one + taps[2:3, :] * two).astype(BF16)
    pre = jnp.concatenate([pre_ref[z, 0] for z in range(per)], axis=0).astype(F32)
    n, _ = normed_parts(x.astype(F32))
    dh = nt(dpre, w[:, : dpre.shape[1]])
    for z in range(per):
        k = (per * step + z) ^ sc[0]
        bit_s, bit_a, bit_b = k // 4, k // 2 % 2, k % 2
        dh_z = dh[z * rows : (z + 1) * rows]
        to_left, to_right = 2 * bit_b + bit_s, 2 * bit_a + bit_s

        @pl.when(bit_a == 0)
        def _(dh_z=dh_z, to_left=to_left):
            left_keep[to_left] = dh_z[:, :half]

        @pl.when(bit_a == 1)
        def _(dh_z=dh_z, to_left=to_left):
            left_send[to_left] = dh_z[:, :half].astype(BF16)

        @pl.when(bit_b == 0)
        def _(dh_z=dh_z, to_right=to_right):
            right_keep[to_right] = dh_z[:, half:]

        @pl.when(bit_b == 1)
        def _(dh_z=dh_z, to_right=to_right):
            right_send[to_right] = dh_z[:, half:].astype(BF16)

    h = jnp.concatenate([h_ref[z, 0] for z in range(per)], axis=0)
    dw_acc[...] += tn(h, dpre)
    small_acc[0:1, :] += jnp.sum(dh * n, axis=0, keepdims=True)
    small_acc[1:2, :] += jnp.sum(dh, axis=0, keepdims=True)
    conv_acc[0:3, :] += jnp.concatenate([jnp.sum(pre * d, axis=0, keepdims=True) for d in (now, one, two)], axis=0)

    @pl.when(step == steps - 1)
    def _():
        core = sc[3]
        own = width // parts
        high = own // 2
        cols = dw_acc.shape[1]
        small_acc[2:4, :] = small_two[...]
        for p in range(parts):
            gains = small_acc[0:4, p * own : (p + 1) * own]
            gains = jnp.concatenate([gains, jnp.zeros((4, cols - own), F32)], axis=1)
            tail = jnp.concatenate([gains, conv_acc[0:3, :], jnp.zeros((TAIL - 7, cols), F32)], axis=0)
            keep = pl.ds(pl.multiple_of((2 * p + core) * high, high), high)
            send = pl.ds(pl.multiple_of((2 * p + 1 - core) * high, high), high)
            dw_keep[p, 0:high, :] = dw_acc[keep, :]
            dw_keep[p, high : high + TAIL, :] = tail
            dw_send[p, 0:high, :] = dw_acc[send, :].astype(BF16)
            dw_send[p, high : high + TAIL, :] = tail.astype(BF16)


def project_back(scalars, mine, recv, left, right, h, pre, taps, small_two, w_lists, share, rows, parts):
    counts = [len(pieces) for pieces in w_lists]
    flat = [piece for pieces in w_lists for piece in pieces]
    blocks, ext, thin = mine[0].shape
    heads = len(mine)
    cols = heads * thin
    width = h.shape[1]
    half = width // 2
    high = width // parts // 2
    whole = lambda *shape: pl.BlockSpec(shape, lambda t, sc: (0,) * len(shape))
    per = blocks // 2
    piece = pl.BlockSpec((1, per, rows, half), lambda t, sc: (0, t ^ (sc[0] // per), 0, 0))
    by_block = lambda a: a.reshape(blocks, share, rows, a.shape[1])
    out_shape = [
        jax.ShapeDtypeStruct((blocks // 2, rows, half), F32),
        jax.ShapeDtypeStruct((blocks // 2, rows, half), BF16),
        jax.ShapeDtypeStruct((blocks // 2, rows, half), F32),
        jax.ShapeDtypeStruct((blocks // 2, rows, half), BF16),
        jax.ShapeDtypeStruct((parts, high + TAIL, cols), F32),
        jax.ShapeDtypeStruct((parts, high + TAIL, cols), BF16),
    ]
    return pl.pallas_call(
        functools.partial(project_back_kernel, share, rows, heads, parts, counts),
        grid_spec=pltpu.PrefetchScalarGridSpec(
            num_scalar_prefetch=1,
            grid=(blocks // per,),
            in_specs=[pl.BlockSpec((per, ext, thin), lambda t, sc: (t, 0, 0))] * heads
            + [pl.BlockSpec((1, per, ext, thin), lambda t, sc: (0, t, 0, 0))] * len(recv)
            + [
                piece,
                piece,
                pl.BlockSpec((per, 1, rows, width), lambda t, sc: (t, sc[1], 0, 0)),
                pl.BlockSpec((per, 1, rows, cols), lambda t, sc: (t, sc[1], 0, 0)),
                whole(3, cols),
                whole(2, width),
            ]
            + [ANY] * len(flat),
            out_specs=[whole(*o.shape) for o in out_shape],
            scratch_shapes=[
                pltpu.VMEM((per, ext, cols), F32),
                pltpu.VMEM((width, width), BF16),
                pltpu.VMEM((width, cols), F32),
                pltpu.VMEM((8, width), F32),
                pltpu.VMEM((8, cols), F32),
                pltpu.SemaphoreType.DMA((2 * PIECES,)),
            ],
        ),
        out_shape=out_shape,
        compiler_params=pltpu.CompilerParams(vmem_limit_bytes=28 * MIB),
        cost_estimate=FREE,
        name="project_back",
    )(scalars, *mine, *recv, left, right, by_block(h), by_block(pre), taps, small_two, *flat)


def mix_kernel(counts, sc, attn, tokens, gain, bias, *refs):
    lists, refs = split_lists(refs, counts)
    y_ref, h_ref, w_ref, w, sems, save_sem = refs
    size = w.shape[0] // 2 // fsdp_size(lists)
    copies = piece_copies(lists, w, sems, sc[5], sc[3], (size, size))
    for copy in copies:
        copy.start()
    for copy in copies:
        copy.wait()
    save = pltpu.make_async_copy(w, w_ref, save_sem)
    save.start()
    nseq, rows, width = tokens.shape
    parts = h_ref.shape[0]
    own = width // parts
    for i in range(nseq):
        y = tokens[i].astype(F32) + tn(attn[i], w[...])
        y_ref[i] = y
        n, _ = normed_parts(y)
        h = (n * gain[...] + bias[...]).astype(BF16)
        for p in range(parts):
            h_ref[p, i * rows : (i + 1) * rows, :] = h[:, p * own : (p + 1) * own]
    save.wait()


def mix(scalars, attn, tokens, gain, bias, w_lists, parts):
    counts = [len(pieces) for pieces in w_lists]
    flat = [piece for pieces in w_lists for piece in pieces]
    nseq, rows, width = tokens.shape
    whole = lambda a: pl.BlockSpec(a.shape, lambda i, sc: (0,) * len(a.shape))
    out_shape = [
        pltpu.HBM((nseq, rows, width), F32),
        jax.ShapeDtypeStruct((parts, nseq * rows, width // parts), BF16),
    ]
    args = (attn, tokens, gain, bias)
    return pl.pallas_call(
        functools.partial(mix_kernel, counts),
        grid_spec=pltpu.PrefetchScalarGridSpec(
            num_scalar_prefetch=1,
            grid=(1,),
            in_specs=[whole(a) for a in args] + [ANY] * len(flat),
            out_specs=[whole(a) for a in out_shape] + [ANY],
            scratch_shapes=[
                pltpu.VMEM((width, width), BF16),
                pltpu.SemaphoreType.DMA((2 * PIECES,)),
                pltpu.SemaphoreType.DMA,
            ],
        ),
        out_shape=out_shape + [pltpu.HBM((width, width), BF16)],
        compiler_params=pltpu.CompilerParams(vmem_limit_bytes=12 * MIB),
        cost_estimate=FREE,
        name="mix",
    )(scalars, *args, *flat)


def feed_kernel(counts, merged, sc, h_own, h_other, d_own, d_other, *refs):
    (ups, downs), refs = split_lists(refs, counts)
    r_ref, du_ref, dh_keep, dh_send, y_keep, y_send, up, down, sems = refs
    parts, rows, own = h_own.shape
    split = r_ref.shape[2]
    copies, later = [], []
    if merged:
        for p in range(parts):
            take = (p * own, own)
            cols = pl.ds(p * split, split)
            copies += piece_copies([ups], up, sems.at[0, p], sc[5], 0, take, cols)
        later += piece_copies([ups], down, sems.at[1, 0], sc[5], 0, (parts * own, split))
    else:
        copies += piece_copies([ups], up, sems.at[0, 0], sc[5], 0)
        later += piece_copies([downs], down, sems.at[1, 0], sc[5], 0)
    for copy in copies + later:
        copy.start()
    for copy in copies:
        copy.wait()
    h = jnp.concatenate(
        [jnp.concatenate([ref[p] for p in range(parts)], axis=1) for ref in (h_own, h_other)], axis=0
    )
    d = jnp.concatenate([d_own[...], d_other[...]], axis=0)
    dh = None
    y = None
    for p in range(parts):
        cols = slice(p * split, (p + 1) * split)
        act = jnp.maximum(nn(h, up[:, cols]), 0.0)
        r = jnp.square(act).astype(BF16)
        r_ref[p] = r
        if p == 0:
            for copy in later:
                copy.wait()
        dr = nt(d, down[cols, :])
        du = (dr * 2.0 * act).astype(BF16)
        du_ref[:, cols] = du
        term = nt(du, up[:, cols])
        dh = term if dh is None else dh + term
        term = nn(r, down[cols, :])
        y = term if y is None else y + term
    dh_keep[...] = dh[:rows]
    dh_send[...] = dh[rows:].astype(BF16)
    y_keep[...] = y[:rows]
    y_send[...] = y[rows:].astype(BF16)


def feed(scalars, h_own, h_other, d_own, d_other, ups, downs, split):
    parts, rows, own = h_own.shape
    width = parts * own
    cols = split * parts
    whole = lambda a: pl.BlockSpec(a.shape, lambda i, sc: (0,) * len(a.shape))
    out_shape = [
        jax.ShapeDtypeStruct((parts, 2 * rows, split), BF16),
        pltpu.HBM((2 * rows, cols), BF16),
        pltpu.HBM((rows, width), F32),
        jax.ShapeDtypeStruct((rows, width), BF16),
        pltpu.HBM((rows, width), F32),
        jax.ShapeDtypeStruct((rows, width), BF16),
    ]
    args = (h_own, h_other, d_own, d_other)
    return pl.pallas_call(
        functools.partial(feed_kernel, (len(ups), len(downs)), not downs),
        grid_spec=pltpu.PrefetchScalarGridSpec(
            num_scalar_prefetch=1,
            grid=(1,),
            in_specs=[whole(a) for a in args] + [ANY] * (len(ups) + len(downs)),
            out_specs=[whole(a) for a in out_shape],
            scratch_shapes=[
                pltpu.VMEM((width, cols), BF16),
                pltpu.VMEM((cols, width), BF16),
                pltpu.SemaphoreType.DMA((2, parts, PIECES)),
            ],
        ),
        out_shape=out_shape,
        compiler_params=pltpu.CompilerParams(vmem_limit_bytes=28 * MIB),
        cost_estimate=FREE,
        name="feed",
    )(scalars, *args, *ups, *downs)


def mix_back_kernel(sc, dh_own, dh_other, y, dtop, gain, w, attn, dy_ref, dout_ref, small_ref, keep_ref, send_ref,
                    grad):
    nseq, rows, width = y.shape
    sums = None
    for i in range(nseq):
        at_i = slice(i * rows, (i + 1) * rows)
        dh = dh_own[at_i, :] + dh_other[at_i, :].astype(F32)
        n, scale = normed_parts(y[i])
        dy = dtop[at_i, :].astype(F32) + norm_back(dh, n, scale, gain[...])
        dy_ref[i] = dy
        low = dy.astype(BF16)
        dout_ref[i] = nt(w[...], low).astype(BF16)
        term = nn(attn[i], low)
        grad[...] = term if i == 0 else grad[...] + term
        term = jnp.concatenate([jnp.sum(dh * n, axis=0, keepdims=True), jnp.sum(dh, axis=0, keepdims=True)], axis=0)
        sums = term if sums is None else sums + term
    small_ref[...] = sums
    parts, size, _ = keep_ref.shape
    for p in range(parts):
        keep_ref[p] = grad[pl.ds(pl.multiple_of((2 * p + sc[3]) * size, size), size), :]
        send_ref[p] = grad[pl.ds(pl.multiple_of((2 * p + 1 - sc[3]) * size, size), size), :].astype(BF16)


def mix_back(scalars, dh_own, dh_other, y, dtop, gain, w, attn, parts):
    nseq, rows, width = y.shape
    out_shape = [
        pltpu.HBM((nseq, rows, width), F32),
        jax.ShapeDtypeStruct((nseq, width, rows), BF16),
        pltpu.HBM((2, width), F32),
        pltpu.HBM((parts, width // parts // 2, width), F32),
        jax.ShapeDtypeStruct((parts, width // parts // 2, width), BF16),
    ]
    args = (dh_own, dh_other, y, dtop, gain, w, attn)
    return whole_call(mix_back_kernel, scalars, args, out_shape, "mix_back", [pltpu.VMEM((width, width), F32)])


def whole_call(body, scalars, args, out_shape, name, scratch=()):
    whole = lambda a: pl.BlockSpec(a.shape, lambda i, sc: (0,) * len(a.shape))
    return pl.pallas_call(
        body,
        grid_spec=pltpu.PrefetchScalarGridSpec(
            num_scalar_prefetch=1,
            grid=(1,),
            in_specs=[whole(a) for a in args],
            out_specs=[whole(a) for a in out_shape],
            scratch_shapes=list(scratch),
        ),
        out_shape=out_shape,
        compiler_params=pltpu.CompilerParams(vmem_limit_bytes=12 * MIB),
        cost_estimate=FREE,
        name=name,
    )(scalars, *args)


def fold(scalars, keep, got, which):
    def body(sc, keep_ref, got_ref, keep_out, send_out):
        bit = 0 if which is None else sc[which]
        for i in range(keep_ref.shape[0]):
            keep_out[i] = keep_ref[i, bit].astype(F32) + got_ref[i, bit].astype(F32)
            send_out[i] = (keep_ref[i, 1 - bit].astype(F32) + got_ref[i, 1 - bit].astype(F32)).astype(BF16)

    shape = (keep.shape[0], *keep.shape[2:])
    out_shape = [jax.ShapeDtypeStruct(shape, F32), jax.ShapeDtypeStruct(shape, BF16)]
    return whole_call(body, scalars, (keep, got.reshape(keep.shape)), out_shape, "fold")


def fold_halves(scalars, left, left_got, right, right_got):
    rows, half = left.shape[2:]

    def body(sc, lk, lg, rk, rg, left_out, right_out, send_out):
        left_out[0] = lk[0, 0] + lg[0, 0].astype(F32)
        right_out[0] = rk[0, 0] + rg[0, 0].astype(F32)
        send_out[0, :, :half] = (lk[0, 1] + lg[0, 1].astype(F32)).astype(BF16)
        send_out[0, :, half:] = (rk[0, 1] + rg[0, 1].astype(F32)).astype(BF16)

    one = jax.ShapeDtypeStruct((1, rows, half), F32)
    out_shape = [one, one, jax.ShapeDtypeStruct((1, rows, 2 * half), BF16)]
    args = (left, left_got.reshape(left.shape), right, right_got.reshape(right.shape))
    return whole_call(body, scalars, args, out_shape, "fold_halves")


def join(scalars, keep, got):
    def body(sc, keep_ref, got_ref, out):
        out[...] = (keep_ref[...].astype(F32) + got_ref[...].astype(F32)).astype(BF16)

    out_shape = [jax.ShapeDtypeStruct(keep.shape, BF16)]
    return whole_call(body, scalars, (keep, got.reshape(keep.shape)), out_shape, "join")[0]


def append(scalars, held, got):
    def body(sc, held_ref, got_ref, out):
        count = held_ref.shape[0]
        out[0:count] = held_ref[...]
        out[count : 2 * count] = got_ref[...]

    out_shape = [jax.ShapeDtypeStruct((2 * held.shape[0], *held.shape[1:]), held.dtype)]
    return whole_call(body, scalars, (held, got), out_shape, "append")[0]


def merge_low(scalars, down, down_got, out, out_got, which):
    zys, lows, width = down.shape
    outs = out.shape[1]
    fill = -outs % 16

    def body(sc, down_ref, down_got_ref, out_ref, out_got_ref, keep_out, send_out):
        for i in range(zys // 2):
            for target, bit in ((keep_out, sc[which]), (send_out, 1 - sc[which])):
                t = 2 * i + bit
                first = down_ref[t].astype(F32) + down_got_ref[t].astype(F32)
                second = out_ref[t].astype(F32) + out_got_ref[t].astype(F32)
                rows = [first, second] + ([jnp.zeros((fill, width), F32)] if fill else [])
                target[i] = jnp.concatenate(rows, axis=0).astype(target.dtype)

    shape = (zys // 2, lows + outs + fill, width)
    out_shape = [jax.ShapeDtypeStruct(shape, F32), jax.ShapeDtypeStruct(shape, BF16)]
    args = (down, down_got.reshape(down.shape), out, out_got.reshape(out.shape))
    return whole_call(body, scalars, args, out_shape, "merge_low")


def first_norm_back(scalars, tokens, dy, gain, parts):
    nseq, rows, width = tokens.shape

    def body(sc, tokens_ref, dy_ref, gain_ref, lk, rk, got, out):
        seq = sc[6]
        for i in range(nseq):
            here = seq == i
            dh = jnp.where(here, jnp.concatenate([lk[0], rk[0]], axis=1), got[0].astype(F32))
            n, scale = normed_parts(tokens_ref[i].astype(F32))
            out[i] = dy_ref[i] + norm_back(dh, n, scale, gain_ref[...])

    out_shape = [jax.ShapeDtypeStruct(tokens.shape, F32)]
    return whole_call(body, scalars, (tokens, dy, gain, *parts), out_shape, "first_norm_back")[0]


def piece_of(places):
    def block(t, sc):
        d = t ^ sc[0]
        return (d % 2 * 2 ** places[0] + d // 2 % 2 * 2 ** places[1] + d // 4 % 2 * 2 ** places[2], 0, 0)

    return block


def up_rows_kernel(parts, sc, own_ref, other_ref, out_ref):
    first = sc[3] == 0
    own, other = own_ref[0].astype(F32), other_ref[0].astype(F32)
    split = own.shape[1] // parts
    for p in range(parts):
        cols = slice(p * split, (p + 1) * split)
        out_ref[0, :, 2 * p * split : (2 * p + 1) * split] = jnp.where(first, own[:, cols], other[:, cols])
        out_ref[0, :, (2 * p + 1) * split : (2 * p + 2) * split] = jnp.where(first, other[:, cols], own[:, cols])


def up_rows(scalars, own, other, parts):
    pieces, high, wide = own.shape
    return pl.pallas_call(
        functools.partial(up_rows_kernel, parts),
        grid_spec=pltpu.PrefetchScalarGridSpec(
            num_scalar_prefetch=1,
            grid=(pieces,),
            in_specs=[pl.BlockSpec((1, high, wide), piece_of((2, 1, 0)))] * 2,
            out_specs=pl.BlockSpec((1, high, 2 * wide), lambda t, sc: (t, 0, 0)),
        ),
        out_shape=jax.ShapeDtypeStruct((pieces, high, 2 * wide), F32),
        compiler_params=pltpu.CompilerParams(vmem_limit_bytes=8 * MIB),
        cost_estimate=FREE,
        name="up_rows",
    )(scalars, own, other)


def low_rows_kernel(lows, outs, sc, own_ref, other_ref, down_ref, out_ref):
    first = sc[3] == 0
    own, other = own_ref[0].astype(F32), other_ref[0].astype(F32)
    for c, value in enumerate((jnp.where(first, own, other), jnp.where(first, other, own))):
        down_ref[c, 0] = value[:lows]
        out_ref[c, 0] = value[lows : lows + outs]


def low_rows(scalars, own, other, lows, outs):
    pieces, low, width = own.shape
    return pl.pallas_call(
        functools.partial(low_rows_kernel, lows, outs),
        grid_spec=pltpu.PrefetchScalarGridSpec(
            num_scalar_prefetch=1,
            grid=(pieces,),
            in_specs=[pl.BlockSpec((1, low, width), piece_of((1, 2, 0)))] * 2,
            out_specs=[
                pl.BlockSpec((2, 1, lows, width), lambda t, sc: (0, t, 0, 0)),
                pl.BlockSpec((2, 1, outs, width), lambda t, sc: (0, t, 0, 0)),
            ],
        ),
        out_shape=[
            jax.ShapeDtypeStruct((2, pieces, lows, width), F32),
            jax.ShapeDtypeStruct((2, pieces, outs, width), F32),
        ],
        compiler_params=pltpu.CompilerParams(vmem_limit_bytes=8 * MIB),
        cost_estimate=FREE,
        name="low_rows",
    )(scalars, own, other)


def qkv_rows_kernel(groups, high, own, gw, sc, own_ref, other_ref, out_ref, gain_ref, conv_ref):
    core = sc[3]
    swapped = [(g ^ sc[4]) % 2 * 2 + (g ^ sc[4]) // 2 for g in range(groups)]
    convs = []
    gains = None
    for k in swapped:
        tail = own_ref[k].astype(F32)[high:]
        gains = tail[0:4, :own] if gains is None else gains + tail[0:4, :own]
        convs.append(tail[4:7, :])
    gain_ref[...] = gains
    for j in range(3):
        cols = slice(j * gw, (j + 1) * gw)
        conv_ref[:, j * groups * gw : (j + 1) * groups * gw] = jnp.concatenate([c[:, cols] for c in convs], axis=1)
    for c in range(2):
        pieces = [jnp.where(core == c, own_ref[k], other_ref[k]).astype(F32) for k in swapped]
        for j in range(3):
            cols = slice(j * gw, (j + 1) * gw)
            out = slice(j * groups * gw, (j + 1) * groups * gw)
            out_ref[c, :, out] = jnp.concatenate([p[:high, cols] for p in pieces], axis=1)


def qkv_rows(scalars, args, high):
    groups, _, cols = args[0].shape
    own = 2 * high
    shapes = [(2, high, groups * cols), (4, own), (3, groups * cols)]
    out_shape = [jax.ShapeDtypeStruct(shape, F32) for shape in shapes]
    return whole_call(
        functools.partial(qkv_rows_kernel, groups, high, own, cols // 3), scalars, args, out_shape, "qkv_rows"
    )


def per_device(tokens, cotangent, lengths, ln1_gain, ln1_bias, w_qkv, w_conv, w_out, ln2_gain, ln2_bias, w_up, w_down):
    nseq, rows, width = tokens.shape
    half = width // 2
    count = lax.axis_size("ctx")
    parts = lax.axis_size("fsdp")
    rank = lax.axis_index("ctx")
    index = lax.axis_index("fsdp")
    hidden = w_up.shape[1]
    own_rows = ln1_gain.shape[0]
    zys = nseq * GROUPS
    share = count // zys
    hp = HEADS // GROUPS
    hd = width // HEADS
    gw = hp * hd
    mine = rank % share
    core = rank % 2
    zy = rank // share
    seq = zy // GROUPS
    group = zy % GROUPS
    bit_b, bit_a, bit_s = share, 2 * share, 4 * share
    share_bits = bits(share)
    positions = rank * rows + jnp.arange(rows, dtype=jnp.int32)
    valid = positions[None, :] < lengths[:, None]
    high_bits = [index // mask % 2 for mask in reversed(bits(parts))]
    scalars = [zy, mine, lengths[seq], core, group, index, seq, zy // 2 % 2, zy % 2] + high_bits
    scalars = jnp.stack(scalars).astype(jnp.int32)
    at_s, at_a, at_b, at_x = 6, 7, 8, 9

    own_seq, far_seq = at(tokens, seq), at(tokens, 1 - seq)
    w_conv = lax.optimization_barrier((w_conv, far_seq))[0]
    fsdp_bits = bits(parts)
    split = hidden // parts // 2
    packed = pack(scalars, (ln1_gain, ln1_bias, ln2_gain, ln2_bias), w_conv)
    w_qkv, w_out = lax.optimization_barrier((w_qkv, w_out, packed))[:2]
    first = first_part(scalars, w_qkv, w_out, gw)
    pair = jnp.stack([own_seq, exch(far_seq, "ctx", bit_s)])
    left, right = pair[..., :half], pair[..., half:]
    gains, taps = parameters(scalars, gather_list(packed, "fsdp", fsdp_bits), own_rows, gw)
    gain_one, bias_one, gain_two, bias_two = (gains[i : i + 1] for i in range(4))
    first = gather_list(first, "fsdp", fsdp_bits)
    w_up, w_down = lax.optimization_barrier((w_up, w_down, left, gains, first[-1]))[:2]
    left = jnp.stack([left, exch(left, "ctx", bit_a)], axis=1)
    right = jnp.stack([right, exch(right, "ctx", bit_b)], axis=1)
    left = jnp.stack([left, exch(left, "ctx", bit_b)], axis=2)
    right = jnp.stack([right, exch(right, "ctx", bit_a)], axis=1)
    left = gather_list(left.reshape(1, zys, rows, half), "ctx", share_bits)
    right = gather_list(right.reshape(1, zys, rows, half), "ctx", share_bits)

    both_cores = lambda pieces: [pieces, [exch(piece, "ctx", 1) for piece in pieces]]
    first = both_cores(first)
    if split == width:
        ups = gather_list(rest_part(scalars, w_up, w_down, parts), "fsdp", fsdp_bits)
        downs = []
    else:
        ups = gather_list(up_part(scalars, w_up, parts)[None], "fsdp", fsdp_bits)
        downs = gather_list(at(w_down.reshape(2, split, width), core)[None], "fsdp", fsdp_bits)

    dtop = jnp.where(valid[..., None], cotangent, jnp.zeros_like(cotangent)).reshape(nseq * rows, width)
    dtop_other = exch(dtop, "ctx", 1)
    left[0], taps, gain_one, bias_one = lax.optimization_barrier(
        (left[0], taps, gain_one, bias_one, gain_two, bias_two, dtop)
    )[:4]
    h_one, pre, attn_t, o, lse, q, k, kt, v = attention(
        scalars, left, right, first, taps, gain_one, bias_one, share, hp, hd
    )
    classes = [[i for i in range(count) if i % share == s] for s in range(share)]
    swap = lambda x: lax.all_to_all(x, "ctx", 0, 0, tiled=True, axis_index_groups=classes)
    attn_t = swap(attn_t).reshape(nseq, width, rows)

    order = Order()
    y_one, h_two, w_out_full = mix(scalars, attn_t, tokens, gain_two, bias_two, first, parts)
    h_other = exch(h_two, "ctx", 1)
    r, dupper, dh_keep, dh_send, y_keep, y_send = feed(
        scalars, h_two, h_other, dtop, dtop_other, ups, downs, split
    )
    dh_other = exch(dh_send, "ctx", 1)
    dtop_pair = jnp.concatenate([dtop, dtop_other])

    near_base = index // (parts // 2) * (parts // 2)

    def near(term):
        return jnp.stack([term(near_base + p) for p in range(parts // 2)])

    def fsdp_start(term):
        far = [term(parts // 2 - near_base + p) for p in range(parts // 2)]
        return exch(jnp.stack(far).astype(BF16), "fsdp", parts // 2)

    def fsdp_more(keep, got):
        for i, mask in enumerate(reversed(fsdp_bits[:-1])):
            keep, send = fold(scalars, keep.reshape(1, 2, mask, *keep.shape[1:]), got, at_x + 1 + i)
            keep, got = keep[0], exch(send[0], "fsdp", mask)
        return keep, got

    down_term = lambda p: tn(at(r, p), dtop_pair)
    down_got = fsdp_start(down_term)
    dh_keep, dh_other = order(dh_keep, dh_other)
    dy_one, dout_t, small_two, out_keep, out_send = mix_back(
        scalars, dh_keep, dh_other, y_one, dtop, gain_two, w_out_full, attn_t, parts
    )
    order.mark(dout_t)
    r, dupper, y_keep, y_send, h_two, h_other = order(r, dupper, y_keep, y_send, h_two, h_other)
    h_pair = jnp.concatenate([h_two, h_other], axis=1)
    dout_t = swap(dout_t.reshape(zys, gw, rows))

    def cut(held, axis, bit):
        keep = lax.dynamic_slice_in_dim(held, bit, 1, axis)
        send = lax.dynamic_slice_in_dim(held, 1 - bit, 1, axis)
        return keep, send.astype(BF16)

    zy_bits = {"s": (0, bit_s, zy // 4), "a": (1, bit_a, zy // 2 % 2), "b": (2, bit_b, zy % 2)}
    out_keep = out_keep.reshape(1, 2, parts // 2, *out_keep.shape[1:])
    out_keep, out_send = fold(scalars, out_keep, exch(out_send, "ctx", 1), at_x)
    out_keep, out_got = out_keep[0], exch(out_send[0], "fsdp", parts // 2)
    grad_up = jnp.einsum("pnk,nf->pkf", h_pair, dupper, preferred_element_type=F32)
    grad_up = grad_up.reshape(parts, 2, 2, 2, own_rows // zys, hidden // 2)
    up_keep, up_send = cut(grad_up, 2, zy_bits["a"][2])
    down_keep = near(down_term)
    result = y_one + (y_keep + exch(y_send, "ctx", 1).astype(F32)).reshape(nseq, rows, width)
    output = jnp.where(valid[..., None], result, 0.0).astype(BF16)

    dout_t, up_keep, up_send, down_keep, out_keep, output = lax.optimization_barrier(
        (dout_t, up_keep, up_send, down_keep, out_keep, output)
    )
    up_got = exch(up_send, "ctx", bit_a)
    lows = down_keep.shape[1] // zys
    outs = out_keep.shape[1] // zys
    high = own_rows // zys
    up_rest = (high, hidden // 2)
    tail_rows = own_rows // 2 + TAIL
    dw_rest = (tail_rows, 3 * gw)

    keep = {"up": up_keep, "down": down_keep, "out": out_keep, "dout": dout_t}
    got = {"up": up_got, "down": down_got, "out": out_got}
    heads_keep, heads_got = [], []
    done = {}

    def fold_step(x, which, shape, axis, mask):
        def run():
            kept, send = fold(scalars, order(keep[x]).reshape(shape), got[x], which)
            order.mark(send)
            keep[x] = kept
            got[x] = exch(send, axis, mask)

        return run

    def join_step(x, shape, mask):
        def run():
            keep[x] = order.mark(join(scalars, order(keep[x]).reshape(shape), got[x]))
            got[x] = exch(keep[x], "ctx", mask)

        return run

    def append_step(x, mask):
        def run():
            keep[x] = order.mark(append(scalars, order(keep[x]), got[x]))
            got[x] = exch(keep[x], "ctx", mask)

        return run

    def head(h):
        def run():
            kept, sent = attend_back(scalars, h, q, k, kt, v, order(keep["dout"]), o, lse, share, rows)
            heads_keep.append(order.mark(kept))
            heads_got.extend(exch(sent[x - 1 : x], "ctx", x) for x in range(1, share))

        return run

    def low_first():
        keep["down"], keep["out"] = order(keep["down"], keep["out"])
        for x in ("down", "out"):
            keep[x], got[x] = fsdp_more(keep[x], got[x])
        kept, send = merge_low(
            scalars,
            keep["down"].reshape(zys, lows, width),
            got["down"],
            keep["out"].reshape(zys, outs, width),
            got["out"],
            at_b,
        )
        order.mark(send)
        keep["low"] = kept
        got["low"] = exch(send, "ctx", bit_b)

    low_rest = (lows + outs + -outs % 16, width)

    def up_between():
        keep["up"], got["up"] = fsdp_more(keep["up"].reshape(parts // 2, 2, 2, *up_rest), got["up"])
        fold_step("up", at_b, (2, 2, *up_rest), "ctx", bit_b)()

    def back():
        last = order(heads_keep[-1])
        left_keep, left_send, right_keep, right_send, dw_keep, dw_send = project_back(
            scalars, heads_keep[:-1] + [last], heads_got, left[0], right[0], h_one, pre, taps, small_two, first,
            share, rows, parts,
        )
        order.mark(dw_send)
        keep.update(left=left_keep, right=right_keep, qkv=dw_keep)
        got["left"] = exch(left_send, "ctx", bit_a)
        got["right"] = exch(right_send, "ctx", bit_b)
        got["qkv"] = exch(dw_send, "ctx", 1)

    def qkv_between():
        keep["qkv"], got["qkv"] = fsdp_more(keep["qkv"].reshape(parts // 2, *dw_rest), got["qkv"])
        join_step("qkv", dw_rest, bit_s)()

    def qkv_whole():
        block = join(scalars, order(keep["qkv"]), got["qkv"])
        for mask in share_bits[1:]:
            block = join(scalars, block, exch(block, "ctx", mask))
        keep["qkv"] = order.mark(block[None])
        got["qkv"] = exch(keep["qkv"], "ctx", bit_a)

    def halves():
        kept = order(keep["left"], keep["right"])
        keep["left"], keep["right"], send = fold_halves(scalars, kept[0], got["left"], kept[1], got["right"])
        order.mark(send)
        got["input"] = exch(send, "ctx", bit_s)

    def input_end():
        kept = (keep["left"], keep["right"], got["input"])
        done["input"] = order.mark(first_norm_back(scalars, tokens, order(dy_one), gain_one, kept))

    def qkv_end():
        grad, gains, convs = qkv_rows(scalars, (order(keep["qkv"]), got["qkv"]), own_rows // 2)
        done["qkv"] = order.mark(grad.reshape(own_rows, 3 * width))
        share_cols = 3 * width // parts
        done["gains"] = gains
        done["conv"] = lax.dynamic_slice_in_dim(convs, index * share_cols, share_cols, 1)

    def low_end():
        down_grad, out_grad = low_rows(scalars, order(keep["low"]), got["low"], lows, outs)
        done["down"] = order.mark(down_grad.reshape(hidden // parts, width))
        done["out"] = out_grad.reshape(own_rows, width)

    def up_end():
        grad = up_rows(scalars, order(keep["up"]), got["up"], parts)
        done["up"] = order.mark(grad.reshape(own_rows, hidden))

    steps = {
        "head 0": head(0),
        "head 1": head(1),
        "head 2": head(2),
        "low b": low_first,
        "low a": fold_step("low", at_a, (2, 2, *low_rest), "ctx", bit_a),
        "low s": fold_step("low", at_s, (1, 2, *low_rest), "ctx", bit_s),
        "low sum": join_step("low", (1, *low_rest), bit_s),
        "low gather b": append_step("low", bit_b),
        "low gather a": append_step("low", bit_a),
        "low core": append_step("low", 1),
        "low end": low_end,
        "up x": fold_step("up", at_x, (1, 2, parts // 2 * 4 * high, hidden // 2), "fsdp", parts // 2),
        "up b": up_between,
        "up s": fold_step("up", at_s, (1, 2, *up_rest), "ctx", bit_s),
        "up sum": join_step("up", (1, *up_rest), bit_s),
        "up gather a": append_step("up", bit_a),
        "up gather b": append_step("up", bit_b),
        "up core": append_step("up", 1),
        "up end": up_end,
        "back": back,
        "qkv x": fold_step("qkv", at_x, (1, 2, parts // 2, *dw_rest), "fsdp", parts // 2),
        "qkv s": qkv_between,
        "qkv a": qkv_whole,
        "qkv gather b": append_step("qkv", bit_b),
        "qkv core": append_step("qkv", 1),
        "qkv end": qkv_end,
        "right a": fold_step("right", None, (1, 2, 2, rows, half), "ctx", bit_a),
        "left b": fold_step("left", None, (1, 2, 2, rows, half), "ctx", bit_b),
        "input s": halves,
        "input end": input_end,
    }
    for name in LINE:
        steps[name]()
    input_grad, gains = done["input"], done["gains"]
    w_qkv_grad, w_conv_grad, w_out_grad = done["qkv"], done["conv"], done["out"]
    w_up_grad, w_down_grad = done["up"], done["down"]

    return (
        output,
        input_grad,
        gains[0],
        gains[1],
        w_qkv_grad,
        w_conv_grad,
        w_out_grad,
        gains[2],
        gains[3],
        w_up_grad,
        w_down_grad,
    )


def solution(mesh):
    rows = P("fsdp", "ctx", None)
    first = P("fsdp")
    weight = P("fsdp", None)
    second = P(None, "fsdp")
    in_specs = (rows, rows, first, first, first, weight, second, weight, first, first, weight, weight)
    out_specs = (rows, rows, first, first, weight, second, weight, first, first, weight, weight)
    return jax.shard_map(per_device, mesh=mesh, in_specs=in_specs, out_specs=out_specs, check_vma=False)
```

```python
import functools

import jax
import jax.numpy as jnp
from jax import lax
from jax.experimental import pallas as pl
from jax.experimental.pallas import tpu as pltpu
from jax.sharding import PartitionSpec as P

HEADS = 12
GROUPS = 4
EPS = 1e-05
RIM = 16
PIECES = 8
TAIL = 16
MASKED = -1e30
MIB = 1024 * 1024
F32 = jnp.float32
BF16 = jnp.bfloat16
LINE = (
    "head 0",
    "low b",
    "head 1",
    "head 2",
    "up x",
    "low a",
    "back",
    "low s",
    "up b",
    "qkv x",
    "low sum",
    "up s",
    "right a",
    "low gather b",
    "up sum",
    "left b",
    "qkv s",
    "up gather a",
    "input s",
    "low gather a",
    "qkv a",
    "up gather b",
    "qkv gather b",
    "up core",
    "low core",
    "low end",
    "input end",
    "qkv core",
    "up end",
    "qkv end",
)
FREE = pl.CostEstimate(flops=0, bytes_accessed=0, transcendentals=0)


def exch(value, axis, mask):
    count = lax.axis_size(axis)
    return lax.ppermute(value, axis, [(i, i ^ mask) for i in range(count)])


def bits(count):
    return [1 << b for b in range(count.bit_length() - 1)]


def at(stack, index):
    return lax.dynamic_index_in_dim(stack, index, 0, keepdims=False)


def flip(stack, index):
    return jnp.stack([at(stack, k ^ index) for k in range(stack.shape[0])])


def gather_list(value, axis, masks):
    held = [value]
    for mask in masks:
        held.append(exch(held[0] if len(held) == 1 else jnp.concatenate(held), axis, mask))
    return held


def after(value, *others):
    return lax.optimization_barrier((value, *others))[0]


class Order:
    def __init__(self):
        self.last = None

    def __call__(self, *values):
        if self.last is not None:
            values = lax.optimization_barrier((*values, self.last))[:-1]
        return values if len(values) > 1 else values[0]

    def mark(self, value):
        self.last = value
        return value


def normed_parts(values):
    centre = values - jnp.mean(values, axis=-1, keepdims=True)
    scale = lax.rsqrt(jnp.mean(centre * centre, axis=-1, keepdims=True) + EPS)
    return centre * scale, scale


def norm_back(grad, normed, scale, gain):
    dnorm = grad * gain
    return scale * (
        dnorm
        - jnp.mean(dnorm, axis=-1, keepdims=True)
        - normed * jnp.mean(dnorm * normed, axis=-1, keepdims=True)
    )


def nn(a, b):
    return lax.dot_general(a, b, (((1,), (0,)), ((), ())), preferred_element_type=F32)


def nt(a, b):
    return lax.dot_general(a, b, (((1,), (1,)), ((), ())), preferred_element_type=F32)


def tn(a, b):
    return lax.dot_general(a, b, (((0,), (0,)), ((), ())), preferred_element_type=F32)


def piece_copies(lists, scratch, sems, index, core, take=None, cols=None):
    copies = []
    cores = len(lists)
    for r, pieces in enumerate(lists):
        k = 0
        for stack in pieces:
            for i in range(stack.shape[0]):
                first, size = take or (0, stack.shape[1])
                part = (core ^ r) if cores == 2 else 0
                start = pl.multiple_of(((index ^ k) * cores + part) * size, size)
                target = scratch.at[pl.ds(start, size)] if cols is None else scratch.at[pl.ds(start, size), cols]
                source = stack.at[i, pl.ds(first, size)]
                copies.append(pltpu.make_async_copy(source, target, sems.at[len(copies)]))
                k += 1
    return copies


def fsdp_size(lists):
    return sum(stack.shape[0] for stack in lists[0])


def split_lists(refs, counts):
    lists, at_ref = [], 0
    for n in counts:
        lists.append(refs[at_ref : at_ref + n])
        at_ref += n
    return lists, refs[at_ref:]


ANY = pl.BlockSpec(memory_space=pl.ANY)


def pack(scalars, gains, w_conv):
    own = gains[0].shape[0]
    cols = w_conv.shape[1]

    def body(sc, *refs):
        rows = [jnp.concatenate([ref[...].astype(F32), jnp.zeros((1, cols - own), F32)], axis=1) for ref in refs[:4]]
        rows += [refs[4][...].astype(F32), jnp.zeros((16 - 7, cols), F32)]
        refs[5][0] = jnp.concatenate(rows, axis=0).astype(BF16)

    args = [g.reshape(1, own) for g in gains] + [w_conv]
    return whole_call(body, scalars, args, [jax.ShapeDtypeStruct((1, 16, cols), BF16)], "pack")[0]


def parameters(scalars, packed, own, gw):
    parts = sum(stack.shape[0] for stack in packed)
    cols = packed[0].shape[2]
    total = parts * cols // 3

    def body(sc, *refs):
        held = [ref[i].astype(F32) for ref in refs[:-2] for i in range(ref.shape[0])]
        ordered = []
        for p in range(parts):
            picked = held[0]
            for k in range(1, parts):
                picked = jnp.where((p ^ sc[5]) == k, held[k], picked)
            ordered.append(picked)
        refs[-2][...] = jnp.concatenate([x[0:4, :own] for x in ordered], axis=1)
        taps = jnp.concatenate([x[4:7] for x in ordered], axis=1)
        for j in range(3):
            picked = taps[:, j * total : j * total + gw]
            for g in range(1, GROUPS):
                start = j * total + g * gw
                picked = jnp.where(sc[4] == g, taps[:, start : start + gw], picked)
            refs[-1][:, j * gw : (j + 1) * gw] = picked

    out_shape = [jax.ShapeDtypeStruct((4, parts * own), F32), jax.ShapeDtypeStruct((3, 3 * gw), F32)]
    return whole_call(body, scalars, packed, out_shape, "parameters")


def first_part_kernel(groups, gw, sc, w, w_out, out):
    group = sc[4]
    rows = w.shape[0]
    width = groups * gw
    for j in range(3):
        picked = w[:, j * width : j * width + gw]
        for g in range(1, groups):
            start = j * width + g * gw
            picked = jnp.where(group == g, w[:, start : start + gw], picked)
        out[0, :rows, j * gw : (j + 1) * gw] = picked
    out[0, :rows, 3 * gw :] = jnp.zeros((rows, width - 3 * gw), BF16)
    out[0, rows:, :] = w_out[...]


def first_part(scalars, w_qkv, w_out, gw):
    rows, cols = w_qkv.shape
    width = w_out.shape[1]
    return pl.pallas_call(
        functools.partial(first_part_kernel, GROUPS, gw),
        grid_spec=pltpu.PrefetchScalarGridSpec(
            num_scalar_prefetch=1,
            grid=(1,),
            in_specs=[
                pl.BlockSpec((rows // 2, cols), lambda i, sc: (sc[3], 0)),
                pl.BlockSpec((rows // 2, width), lambda i, sc: (sc[3], 0)),
            ],
            out_specs=pl.BlockSpec((1, rows, width), lambda i, sc: (0, 0, 0)),
        ),
        out_shape=jax.ShapeDtypeStruct((1, rows, width), BF16),
        compiler_params=pltpu.CompilerParams(vmem_limit_bytes=8 * MIB),
        cost_estimate=FREE,
        name="first_part",
    )(scalars, w_qkv, w_out)


def up_part_kernel(sc, w, out):
    out[...] = w[...]


def up_part(scalars, w_up, parts):
    rows, cols = w_up.shape
    split = cols // parts // 2
    if split % 128:
        picked = lax.dynamic_index_in_dim(w_up.reshape(rows, parts, 2, split), scalars[3], 2, keepdims=False)
        return picked.reshape(rows, cols // 2)
    return pl.pallas_call(
        up_part_kernel,
        grid_spec=pltpu.PrefetchScalarGridSpec(
            num_scalar_prefetch=1,
            grid=(parts,),
            in_specs=[pl.BlockSpec((rows, split), lambda p, sc: (0, 2 * p + sc[3]))],
            out_specs=pl.BlockSpec((rows, split), lambda p, sc: (0, p)),
        ),
        out_shape=jax.ShapeDtypeStruct((rows, cols // 2), BF16),
        compiler_params=pltpu.CompilerParams(vmem_limit_bytes=8 * MIB),
        cost_estimate=FREE,
        name="up_part",
    )(scalars, w_up)


def rest_part_kernel(parts, sc, w_up, w_down, out, sems):
    core = sc[3]
    own, cols = w_up.shape
    split = cols // parts // 2
    copies = []
    for p in range(parts):
        source = w_up.at[:, pl.ds(pl.multiple_of((2 * p + core) * split, split), split)]
        copies.append(pltpu.make_async_copy(source, out.at[0, pl.ds(p * own, own)], sems.at[p]))
    source = w_down.at[pl.ds(pl.multiple_of(core * split, split), split)]
    copies.append(pltpu.make_async_copy(source, out.at[0, pl.ds(parts * own, split)], sems.at[parts]))
    for copy in copies:
        copy.start()
    for copy in copies:
        copy.wait()


def rest_part(scalars, w_up, w_down, parts):
    own, cols = w_up.shape
    split = cols // parts // 2
    rows = parts * own + split
    return pl.pallas_call(
        functools.partial(rest_part_kernel, parts),
        grid_spec=pltpu.PrefetchScalarGridSpec(
            num_scalar_prefetch=1,
            grid=(1,),
            in_specs=[ANY] * 2,
            out_specs=ANY,
            scratch_shapes=[pltpu.SemaphoreType.DMA((parts + 1,))],
        ),
        out_shape=jax.ShapeDtypeStruct((1, rows, split), BF16),
        compiler_params=pltpu.CompilerParams(vmem_limit_bytes=2 * MIB),
        cost_estimate=FREE,
        name="rest_part",
    )(scalars, w_up, w_down)


def attention_kernel(share, hp, hd, rows, per, last, shares, counts, sc, *refs):
    (left, right), refs = split_lists(refs, (len(shares), len(shares)))
    taps, gain, bias = refs[:3]
    lists, refs = split_lists(refs[3:], counts)
    h_ref, pre_ref, at_ref, o_ref, lse_ref = refs[:5]
    kept = refs[5:9]
    buf, w, sems, save_sems, q_ref, k_ref, kt_ref, v_ref, vt_ref = refs[9:]
    step = pl.program_id(0)
    saves = [
        pltpu.make_async_copy(source, target, save_sems.at[i])
        for i, (source, target) in enumerate(zip((q_ref, k_ref, kt_ref, v_ref), kept))
    ]

    @pl.when(step <= last)
    def _():
        project_step(share, hp, hd, rows, per, sc, left, right, taps, gain, bias, lists, h_ref, pre_ref, q_ref, k_ref,
                     kt_ref, v_ref, vt_ref, buf, w, sems)

    @pl.when(step == last + 1)
    def _():
        for copy in saves:
            copy.start()

    @pl.when(step > last)
    def _():
        attend_step(share, rows, sc, step - last - 1, q_ref, k_ref, vt_ref, at_ref, o_ref, lse_ref)

    @pl.when(step == last + hp)
    def _():
        for copy in saves:
            copy.wait()


def project_step(share, hp, hd, rows, per, sc, left, right, taps, gain, bias, lists, h_ref, pre_ref, q_ref, k_ref,
                 kt_ref, v_ref, vt_ref, buf, w, sems):
    step = pl.program_id(0)

    @pl.when(step == 0)
    def _():
        copies = piece_copies(lists, w, sems, sc[5], sc[3], (0, w.shape[0] // 2 // fsdp_size(lists)))
        for copy in copies:
            copy.start()
        for copy in copies:
            copy.wait()

    mine = sc[1]
    length = sc[2]
    gw = hp * hd
    size = per * share * rows
    parts = []
    for z in range(per):
        at_z = z ^ (sc[0] % per)
        pieces = []
        for refs_l, refs_r in zip(left, right):
            pieces += [jnp.concatenate([refs_l[i, at_z], refs_r[i, at_z]], axis=1) for i in range(refs_l.shape[0])]
        for j in range(share):
            picked = pieces[0]
            for k in range(1, share):
                picked = jnp.where((j ^ mine) == k, pieces[k], picked)
            parts.append(picked.astype(F32))
    x = jnp.concatenate(parts, axis=0)
    n, _ = normed_parts(x)
    h = (n * gain[...] + bias[...]).astype(BF16)
    h_ref[...] = h
    pre = nn(h, w[:, : 3 * gw]).astype(BF16)
    pre_ref[...] = pre

    @pl.when(step == 0)
    def _():
        buf[0:8, :] = jnp.zeros((8, 3 * gw), F32)

    buf[8:, :] = pre.astype(F32)
    conv = (
        taps[0:1, :] * buf[8 : 8 + size, :]
        + taps[1:2, :] * buf[7 : 7 + size, :]
        + taps[2:3, :] * buf[6 : 6 + size, :]
    )
    buf[0:8, :] = buf[size : size + 8, :]
    qs = conv[:, :gw].astype(BF16)
    kf = conv[:, gw : 2 * gw]
    vf = conv[:, 2 * gw :]
    q_own = []
    for z in range(per):
        start = z * share * rows
        picked = qs[start : start + rows]
        for j in range(1, share):
            picked = jnp.where(mine == j, qs[start + j * rows : start + (j + 1) * rows], picked)
        q_own.append(picked)
    q_own = (jnp.concatenate(q_own, axis=0).astype(F32) * 0.125).astype(BF16)
    lane = lax.broadcasted_iota(jnp.int32, (per * rows, hd), 1)
    ones = jnp.where(lane == 0, 1.0, 0.0).astype(BF16)
    lane = lax.broadcasted_iota(jnp.int32, (size, hd), 1)
    pos = step * size + lax.broadcasted_iota(jnp.int32, (size, hd), 0)
    mask = jnp.where((lane == 0) & (pos >= length), MASKED, 0.0).astype(BF16)
    ks = kf.astype(BF16)
    vs = vf.astype(BF16)
    kt = kf.T.astype(BF16)
    vt = vf.T.astype(BF16)
    own = pl.ds(pl.multiple_of(step * per * rows, per * rows), per * rows)
    every = pl.ds(pl.multiple_of(step * size, size), size)
    for h in range(hp):
        cols = slice(h * hd, (h + 1) * hd)
        q_ref[h, own, :] = jnp.concatenate([q_own[:, cols], ones], axis=1)
        k_ref[h, every, :] = jnp.concatenate([ks[:, cols], mask], axis=1)
        v_ref[h, every, :] = vs[:, cols]
        kt_ref[h, :, every] = kt[cols]
        vt_ref[h, :, every] = vt[cols]


def attention(scalars, left, right, w_lists, taps, gain, bias, share, hp, hd):
    counts = [len(pieces) for pieces in w_lists]
    flat = [piece for pieces in w_lists for piece in pieces]
    _, zys, rows, half = left[0].shape
    width = 2 * half
    gw = hp * hd
    per = 2
    last = zys // per - 1
    total = zys * share * rows
    own = zys * rows
    size = per * share * rows
    shares = [a.shape[0] for a in left]
    body = functools.partial(attention_kernel, share, hp, hd, rows, per, last, shares, counts)
    whole = lambda *shape: pl.BlockSpec(shape, lambda t, sc: (0,) * len(shape))
    block = lambda t: jnp.minimum(t, last)
    head = lambda t: jnp.maximum(t - last - 1, 0)
    pieces = [pl.BlockSpec((n, per, rows, half), lambda t, sc: (0, block(t) ^ (sc[0] // per), 0, 0)) for n in shares]
    kept = [(hp, own, 2 * hd), (hp, total, 2 * hd), (hp, hd, total), (hp, total, hd)]
    return pl.pallas_call(
        body,
        grid_spec=pltpu.PrefetchScalarGridSpec(
            num_scalar_prefetch=1,
            grid=(last + 1 + hp,),
            in_specs=pieces * 2 + [whole(3, 3 * gw), whole(1, width), whole(1, width)] + [ANY] * len(flat),
            out_specs=[
                pl.BlockSpec((size, width), lambda t, sc: (block(t), 0)),
                pl.BlockSpec((size, 3 * gw), lambda t, sc: (block(t), 0)),
                pl.BlockSpec((zys, hd, rows), lambda t, sc: (0, head(t), 0)),
                pl.BlockSpec((1, hd, own), lambda t, sc: (head(t), 0, 0)),
                pl.BlockSpec((1, 1, own), lambda t, sc: (head(t), 0, 0)),
            ]
            + [ANY] * 4,
            scratch_shapes=[
                pltpu.VMEM((8 + size, 3 * gw), F32),
                pltpu.VMEM((width, width), BF16),
                pltpu.SemaphoreType.DMA((2 * PIECES,)),
                pltpu.SemaphoreType.DMA((4,)),
            ]
            + [pltpu.VMEM(shape, BF16) for shape in kept + [(hp, hd, total)]],
        ),
        out_shape=[
            pltpu.HBM((total, width), BF16),
            pltpu.HBM((total, 3 * gw), BF16),
            jax.ShapeDtypeStruct((zys, gw, rows), BF16),
            pltpu.HBM((hp, hd, own), F32),
            jax.ShapeDtypeStruct((hp, 1, own), F32),
        ]
        + [pltpu.HBM(shape, BF16) for shape in kept],
        compiler_params=pltpu.CompilerParams(vmem_limit_bytes=32 * MIB),
        cost_estimate=FREE,
        name="attention",
    )(scalars, *left, *right, taps, gain, bias, *flat)


def seen(share, rows, mine, shape):
    key = lax.broadcasted_iota(jnp.int32, shape, 0)
    col = lax.broadcasted_iota(jnp.int32, shape, 1)
    query = jnp.where(col >= rows, share * rows + col - rows, col) + mine * rows
    return key <= query


def head_copies(sources, targets, sems, head, slot):
    return [
        pltpu.make_async_copy(source.at[pl.ds(head, 1)], target.at[pl.ds(slot, 1)], sems.at[i, slot])
        for i, (source, target) in enumerate(zip(sources, targets))
    ]


def attend_step(share, rows, sc, head, q_all, k_all, vt_all, at_ref, o_ref, lse_ref):
    mine = sc[1]
    q, k, vt = (buf.at[pl.ds(head, 1)] for buf in (q_all, k_all, vt_all))
    tile = 2 * rows
    step = share * tile
    hd = vt.shape[1]
    tiles = q.shape[1] // tile
    for t in range(tiles):
        queries = q[0, t * tile : (t + 1) * tile, :]
        scores = [nt(k[0, j * step : (j + 1) * step, :], queries) for j in range(t + 1)]
        scores[t] = jnp.where(seen(share, rows, mine, scores[t].shape), scores[t], MASKED)
        top = jnp.max(scores[t], axis=0, keepdims=True)
        for j in range(t):
            top = jnp.maximum(top, jnp.max(scores[j], axis=0, keepdims=True))
        total, accum = None, None
        for j in range(t + 1):
            probs = jnp.exp(scores[j] - top)
            term = jnp.sum(probs, axis=0, keepdims=True)
            total = term if total is None else total + term
            term = nn(vt[0, :, j * step : (j + 1) * step], probs.astype(BF16))
            accum = term if accum is None else accum + term
        out = accum / total
        o_ref[0, :, t * tile : (t + 1) * tile] = out
        lse_ref[0, :, t * tile : (t + 1) * tile] = top + jnp.log(total)
        low = out.astype(BF16)
        at_ref[2 * t] = low[:, :rows]
        at_ref[2 * t + 1] = low[:, rows:]


def attend_back_kernel(share, rows, head, sc, q_all, k_all, kt_all, v_all, o_all, dot_ref, lse, mine_ref, send_ref,
                       dq_acc, dk_acc, dv_acc, q, k, kt, v, o, sems):
    mine = sc[1]
    copies = head_copies((q_all, k_all, kt_all, v_all, o_all), (q, k, kt, v, o), sems, head, 0)
    for copy in copies:
        copy.start()
    own = q.shape[1]
    hd = v.shape[2]
    tile = 2 * rows
    step = share * tile
    tiles = own // tile
    total = tiles * step
    dq_acc[...] = jnp.zeros(dq_acc.shape, F32)
    dk_acc[total:, :] = jnp.zeros((RIM, hd), F32)
    dv_acc[total:, :] = jnp.zeros((RIM, hd), F32)
    for copy in copies:
        copy.wait()
    for t in reversed(range(tiles)):
        queries = q[0, t * tile : (t + 1) * tile, :]
        douts = jnp.concatenate([dot_ref[2 * t], dot_ref[2 * t + 1]], axis=1)
        outs = o[0, :, t * tile : (t + 1) * tile]
        logs = lse[0, :, t * tile : (t + 1) * tile]
        inner = jnp.sum(outs * douts.astype(F32), axis=0, keepdims=True)
        dqt = jnp.zeros((hd, tile), F32)
        for j in reversed(range(t + 1)):
            at_j = slice(j * step, (j + 1) * step)
            probs = jnp.exp(nt(k[0, at_j, :], queries) - logs)
            if j == t:
                probs = jnp.where(seen(share, rows, mine, probs.shape), probs, 0.0)
            dv = nt(probs.astype(BF16), douts)
            dprobs = nn(v[0, at_j, :], douts)
            dscores = (probs * (dprobs - inner)).astype(BF16)
            dk = nn(dscores, queries)[:, :hd]
            if t == tiles - 1:
                dv_acc[at_j, :] = dv
                dk_acc[at_j, :] = dk
            else:
                dv_acc[at_j, :] += dv
                dk_acc[at_j, :] += dk
            dqt += nn(kt[0, :, at_j], dscores)
        dq = (dqt * 0.125).T
        for b in (2 * t, 2 * t + 1):
            at_b = pl.ds(pl.multiple_of((b * share + mine) * rows, rows), rows)
            dq_acc[at_b, :] = dq[(b % 2) * rows : (b % 2 + 1) * rows]
    for b in range(own // rows):
        for r in range(share):
            start = (b * share + (mine ^ r)) * rows
            rows_i = pl.ds(pl.multiple_of(start, rows), rows + RIM)
            block = jnp.concatenate([acc[rows_i, :] for acc in (dq_acc, dk_acc, dv_acc)], axis=1)
            if r == 0:
                mine_ref[b] = block
            else:
                send_ref[r - 1, b] = block.astype(BF16)


def attend_back(scalars, head, q, k, kt, v, dout_t, o, lse, share, rows):
    hp, own, wide = q.shape
    total = k.shape[1]
    hd = v.shape[2]
    blocks = own // rows
    whole = lambda a: pl.BlockSpec(a.shape, lambda i, sc: (0,) * len(a.shape))
    one = lambda a: pl.BlockSpec((1, *a.shape[1:]), lambda i, sc: (head, 0, 0))
    out_shape = [
        pltpu.HBM((blocks, rows + RIM, 3 * hd), F32),
        jax.ShapeDtypeStruct((share - 1, blocks, rows + RIM, 3 * hd), BF16),
    ]
    return pl.pallas_call(
        functools.partial(attend_back_kernel, share, rows, head),
        grid_spec=pltpu.PrefetchScalarGridSpec(
            num_scalar_prefetch=1,
            grid=(1,),
            in_specs=[ANY] * 5 + [pl.BlockSpec((blocks, hd, rows), lambda i, sc: (0, head, 0)), one(lse)],
            out_specs=[whole(a) for a in out_shape],
            scratch_shapes=[pltpu.VMEM((total + RIM, hd), F32)] * 3
            + [pltpu.VMEM((1, *a.shape[1:]), a.dtype) for a in (q, k, kt, v, o)]
            + [pltpu.SemaphoreType.DMA((5, 1))],
        ),
        out_shape=out_shape,
        compiler_params=pltpu.CompilerParams(vmem_limit_bytes=16 * MIB),
        cost_estimate=FREE,
        name="attend_back",
    )(scalars, q, k, kt, v, o, dout_t, lse)


def project_back_kernel(share, rows, heads, parts, counts, sc, *refs):
    (kept, recv), refs = split_lists(refs, (heads, heads * (share - 1)))
    left, right, h_ref, pre_ref, taps, small_two = refs[:6]
    lists, refs = split_lists(refs[6:], counts)
    left_keep, left_send, right_keep, right_send, dw_keep, dw_send, buf, w, dw_acc, small_acc, conv_acc, sems = refs
    step = pl.program_id(0)
    steps = pl.num_programs(0)
    width = w.shape[0]
    half = width // 2

    @pl.when(step == 0)
    def _():
        copies = piece_copies(lists, w, sems, sc[5], sc[3], (0, w.shape[0] // 2 // fsdp_size(lists)))
        for copy in copies:
            copy.start()
        dw_acc[...] = jnp.zeros(dw_acc.shape, F32)
        small_acc[...] = jnp.zeros(small_acc.shape, F32)
        conv_acc[...] = jnp.zeros(conv_acc.shape, F32)
        for copy in copies:
            copy.wait()

    hd = kept[0].shape[2] // 3
    per = kept[0].shape[0]
    now, one, two, x = [], [], [], []
    for z in range(per):
        for i in range(heads):
            total = kept[i][z]
            for r in recv[i * (share - 1) : (i + 1) * (share - 1)]:
                total = total + r[0, z].astype(F32)
            for j in range(3):
                start = (j * heads + i) * hd
                buf[z, :, start : start + hd] = total[:, j * hd : (j + 1) * hd]
        now.append(buf[z, 0:rows, :])
        one.append(buf[z, 1 : rows + 1, :])
        two.append(buf[z, 2 : rows + 2, :])
        at_z = z ^ (sc[0] % per)
        x.append(jnp.concatenate([left[0, at_z], right[0, at_z]], axis=1))
    now, one, two, x = (jnp.concatenate(v, axis=0) for v in (now, one, two, x))
    dpre = (taps[0:1, :] * now + taps[1:2, :] * one + taps[2:3, :] * two).astype(BF16)
    pre = jnp.concatenate([pre_ref[z, 0] for z in range(per)], axis=0).astype(F32)
    n, _ = normed_parts(x.astype(F32))
    dh = nt(dpre, w[:, : dpre.shape[1]])
    for z in range(per):
        k = (per * step + z) ^ sc[0]
        bit_s, bit_a, bit_b = k // 4, k // 2 % 2, k % 2
        dh_z = dh[z * rows : (z + 1) * rows]
        to_left, to_right = 2 * bit_b + bit_s, 2 * bit_a + bit_s

        @pl.when(bit_a == 0)
        def _(dh_z=dh_z, to_left=to_left):
            left_keep[to_left] = dh_z[:, :half]

        @pl.when(bit_a == 1)
        def _(dh_z=dh_z, to_left=to_left):
            left_send[to_left] = dh_z[:, :half].astype(BF16)

        @pl.when(bit_b == 0)
        def _(dh_z=dh_z, to_right=to_right):
            right_keep[to_right] = dh_z[:, half:]

        @pl.when(bit_b == 1)
        def _(dh_z=dh_z, to_right=to_right):
            right_send[to_right] = dh_z[:, half:].astype(BF16)

    h = jnp.concatenate([h_ref[z, 0] for z in range(per)], axis=0)
    dw_acc[...] += tn(h, dpre)
    small_acc[0:1, :] += jnp.sum(dh * n, axis=0, keepdims=True)
    small_acc[1:2, :] += jnp.sum(dh, axis=0, keepdims=True)
    conv_acc[0:3, :] += jnp.concatenate([jnp.sum(pre * d, axis=0, keepdims=True) for d in (now, one, two)], axis=0)

    @pl.when(step == steps - 1)
    def _():
        core = sc[3]
        own = width // parts
        high = own // 2
        cols = dw_acc.shape[1]
        small_acc[2:4, :] = small_two[...]
        for p in range(parts):
            gains = small_acc[0:4, p * own : (p + 1) * own]
            gains = jnp.concatenate([gains, jnp.zeros((4, cols - own), F32)], axis=1)
            tail = jnp.concatenate([gains, conv_acc[0:3, :], jnp.zeros((TAIL - 7, cols), F32)], axis=0)
            keep = pl.ds(pl.multiple_of((2 * p + core) * high, high), high)
            send = pl.ds(pl.multiple_of((2 * p + 1 - core) * high, high), high)
            dw_keep[p, 0:high, :] = dw_acc[keep, :]
            dw_keep[p, high : high + TAIL, :] = tail
            dw_send[p, 0:high, :] = dw_acc[send, :].astype(BF16)
            dw_send[p, high : high + TAIL, :] = tail.astype(BF16)


def project_back(scalars, mine, recv, left, right, h, pre, taps, small_two, w_lists, share, rows, parts):
    counts = [len(pieces) for pieces in w_lists]
    flat = [piece for pieces in w_lists for piece in pieces]
    blocks, ext, thin = mine[0].shape
    heads = len(mine)
    cols = heads * thin
    width = h.shape[1]
    half = width // 2
    high = width // parts // 2
    whole = lambda *shape: pl.BlockSpec(shape, lambda t, sc: (0,) * len(shape))
    per = blocks // 2
    piece = pl.BlockSpec((1, per, rows, half), lambda t, sc: (0, t ^ (sc[0] // per), 0, 0))
    by_block = lambda a: a.reshape(blocks, share, rows, a.shape[1])
    out_shape = [
        jax.ShapeDtypeStruct((blocks // 2, rows, half), F32),
        jax.ShapeDtypeStruct((blocks // 2, rows, half), BF16),
        jax.ShapeDtypeStruct((blocks // 2, rows, half), F32),
        jax.ShapeDtypeStruct((blocks // 2, rows, half), BF16),
        jax.ShapeDtypeStruct((parts, high + TAIL, cols), F32),
        jax.ShapeDtypeStruct((parts, high + TAIL, cols), BF16),
    ]
    return pl.pallas_call(
        functools.partial(project_back_kernel, share, rows, heads, parts, counts),
        grid_spec=pltpu.PrefetchScalarGridSpec(
            num_scalar_prefetch=1,
            grid=(blocks // per,),
            in_specs=[pl.BlockSpec((per, ext, thin), lambda t, sc: (t, 0, 0))] * heads
            + [pl.BlockSpec((1, per, ext, thin), lambda t, sc: (0, t, 0, 0))] * len(recv)
            + [
                piece,
                piece,
                pl.BlockSpec((per, 1, rows, width), lambda t, sc: (t, sc[1], 0, 0)),
                pl.BlockSpec((per, 1, rows, cols), lambda t, sc: (t, sc[1], 0, 0)),
                whole(3, cols),
                whole(2, width),
            ]
            + [ANY] * len(flat),
            out_specs=[whole(*o.shape) for o in out_shape],
            scratch_shapes=[
                pltpu.VMEM((per, ext, cols), F32),
                pltpu.VMEM((width, width), BF16),
                pltpu.VMEM((width, cols), F32),
                pltpu.VMEM((8, width), F32),
                pltpu.VMEM((8, cols), F32),
                pltpu.SemaphoreType.DMA((2 * PIECES,)),
            ],
        ),
        out_shape=out_shape,
        compiler_params=pltpu.CompilerParams(vmem_limit_bytes=28 * MIB),
        cost_estimate=FREE,
        name="project_back",
    )(scalars, *mine, *recv, left, right, by_block(h), by_block(pre), taps, small_two, *flat)


def mix_kernel(counts, sc, attn, tokens, gain, bias, *refs):
    lists, refs = split_lists(refs, counts)
    y_ref, h_ref, w_ref, w, sems, save_sem = refs
    size = w.shape[0] // 2 // fsdp_size(lists)
    copies = piece_copies(lists, w, sems, sc[5], sc[3], (size, size))
    for copy in copies:
        copy.start()
    for copy in copies:
        copy.wait()
    save = pltpu.make_async_copy(w, w_ref, save_sem)
    save.start()
    nseq, rows, width = tokens.shape
    parts = h_ref.shape[0]
    own = width // parts
    for i in range(nseq):
        y = tokens[i].astype(F32) + tn(attn[i], w[...])
        y_ref[i] = y
        n, _ = normed_parts(y)
        h = (n * gain[...] + bias[...]).astype(BF16)
        for p in range(parts):
            h_ref[p, i * rows : (i + 1) * rows, :] = h[:, p * own : (p + 1) * own]
    save.wait()


def mix(scalars, attn, tokens, gain, bias, w_lists, parts):
    counts = [len(pieces) for pieces in w_lists]
    flat = [piece for pieces in w_lists for piece in pieces]
    nseq, rows, width = tokens.shape
    whole = lambda a: pl.BlockSpec(a.shape, lambda i, sc: (0,) * len(a.shape))
    out_shape = [
        pltpu.HBM((nseq, rows, width), F32),
        jax.ShapeDtypeStruct((parts, nseq * rows, width // parts), BF16),
    ]
    args = (attn, tokens, gain, bias)
    return pl.pallas_call(
        functools.partial(mix_kernel, counts),
        grid_spec=pltpu.PrefetchScalarGridSpec(
            num_scalar_prefetch=1,
            grid=(1,),
            in_specs=[whole(a) for a in args] + [ANY] * len(flat),
            out_specs=[whole(a) for a in out_shape] + [ANY],
            scratch_shapes=[
                pltpu.VMEM((width, width), BF16),
                pltpu.SemaphoreType.DMA((2 * PIECES,)),
                pltpu.SemaphoreType.DMA,
            ],
        ),
        out_shape=out_shape + [pltpu.HBM((width, width), BF16)],
        compiler_params=pltpu.CompilerParams(vmem_limit_bytes=12 * MIB),
        cost_estimate=FREE,
        name="mix",
    )(scalars, *args, *flat)


def feed_kernel(counts, merged, sc, h_own, h_other, d_own, d_other, *refs):
    (ups, downs), refs = split_lists(refs, counts)
    r_ref, du_ref, dh_keep, dh_send, y_keep, y_send, far_ref, up, down, sems = refs
    parts, rows, own = h_own.shape
    split = r_ref.shape[2]
    copies, later = [], []
    if merged:
        for p in range(parts):
            take = (p * own, own)
            cols = pl.ds(p * split, split)
            copies += piece_copies([ups], up, sems.at[0, p], sc[5], 0, take, cols)
        later += piece_copies([ups], down, sems.at[1, 0], sc[5], 0, (parts * own, split))
    else:
        copies += piece_copies([ups], up, sems.at[0, 0], sc[5], 0)
        later += piece_copies([downs], down, sems.at[1, 0], sc[5], 0)
    for copy in copies + later:
        copy.start()
    for copy in copies:
        copy.wait()
    h = jnp.concatenate(
        [jnp.concatenate([ref[p] for p in range(parts)], axis=1) for ref in (h_own, h_other)], axis=0
    )
    d = jnp.concatenate([d_own[...], d_other[...]], axis=0)
    dh = None
    y = None
    for p in range(parts):
        cols = slice(p * split, (p + 1) * split)
        act = jnp.maximum(nn(h, up[:, cols]), 0.0)
        r = jnp.square(act).astype(BF16)
        r_ref[p] = r
        if p == 0:
            for copy in later:
                copy.wait()
        dr = nt(d, down[cols, :])
        du = (dr * 2.0 * act).astype(BF16)
        du_ref[:, cols] = du
        term = nt(du, up[:, cols])
        dh = term if dh is None else dh + term
        term = nn(r, down[cols, :])
        y = term if y is None else y + term
    dh_keep[...] = dh[:rows]
    dh_send[...] = dh[rows:].astype(BF16)
    y_keep[...] = y[:rows]
    y_send[...] = y[rows:].astype(BF16)
    for i in range(parts // 2):
        far_ref[i] = tn(r_ref[(1 - sc[9]) * (parts // 2) + i], d).astype(BF16)


def feed(scalars, h_own, h_other, d_own, d_other, ups, downs, split):
    parts, rows, own = h_own.shape
    width = parts * own
    cols = split * parts
    whole = lambda a: pl.BlockSpec(a.shape, lambda i, sc: (0,) * len(a.shape))
    out_shape = [
        jax.ShapeDtypeStruct((parts, 2 * rows, split), BF16),
        pltpu.HBM((2 * rows, cols), BF16),
        pltpu.HBM((rows, width), F32),
        jax.ShapeDtypeStruct((rows, width), BF16),
        pltpu.HBM((rows, width), F32),
        jax.ShapeDtypeStruct((rows, width), BF16),
        jax.ShapeDtypeStruct((parts // 2, split, width), BF16),
    ]
    args = (h_own, h_other, d_own, d_other)
    return pl.pallas_call(
        functools.partial(feed_kernel, (len(ups), len(downs)), not downs),
        grid_spec=pltpu.PrefetchScalarGridSpec(
            num_scalar_prefetch=1,
            grid=(1,),
            in_specs=[whole(a) for a in args] + [ANY] * (len(ups) + len(downs)),
            out_specs=[whole(a) for a in out_shape],
            scratch_shapes=[
                pltpu.VMEM((width, cols), BF16),
                pltpu.VMEM((cols, width), BF16),
                pltpu.SemaphoreType.DMA((2, parts, PIECES)),
            ],
        ),
        out_shape=out_shape,
        compiler_params=pltpu.CompilerParams(vmem_limit_bytes=28 * MIB),
        cost_estimate=FREE,
        name="feed",
    )(scalars, *args, *ups, *downs)


def mix_back_kernel(sc, dh_own, dh_other, y, dtop, gain, w, attn, dy_ref, dout_ref, small_ref, keep_ref, send_ref,
                    grad):
    nseq, rows, width = y.shape
    sums = None
    for i in range(nseq):
        at_i = slice(i * rows, (i + 1) * rows)
        dh = dh_own[at_i, :] + dh_other[at_i, :].astype(F32)
        n, scale = normed_parts(y[i])
        dy = dtop[at_i, :].astype(F32) + norm_back(dh, n, scale, gain[...])
        dy_ref[i] = dy
        low = dy.astype(BF16)
        dout_ref[i] = nt(w[...], low).astype(BF16)
        term = nn(attn[i], low)
        grad[...] = term if i == 0 else grad[...] + term
        term = jnp.concatenate([jnp.sum(dh * n, axis=0, keepdims=True), jnp.sum(dh, axis=0, keepdims=True)], axis=0)
        sums = term if sums is None else sums + term
    small_ref[...] = sums
    parts, size, _ = keep_ref.shape
    for p in range(parts):
        keep_ref[p] = grad[pl.ds(pl.multiple_of((2 * p + sc[3]) * size, size), size), :]
        send_ref[p] = grad[pl.ds(pl.multiple_of((2 * p + 1 - sc[3]) * size, size), size), :].astype(BF16)


def mix_back(scalars, dh_own, dh_other, y, dtop, gain, w, attn, parts):
    nseq, rows, width = y.shape
    out_shape = [
        pltpu.HBM((nseq, rows, width), F32),
        jax.ShapeDtypeStruct((nseq, width, rows), BF16),
        pltpu.HBM((2, width), F32),
        pltpu.HBM((parts, width // parts // 2, width), F32),
        jax.ShapeDtypeStruct((parts, width // parts // 2, width), BF16),
    ]
    args = (dh_own, dh_other, y, dtop, gain, w, attn)
    return whole_call(mix_back_kernel, scalars, args, out_shape, "mix_back", [pltpu.VMEM((width, width), F32)], 58)


def whole_call(body, scalars, args, out_shape, name, scratch=(), limit=12):
    whole = lambda a: pl.BlockSpec(a.shape, lambda i, sc: (0,) * len(a.shape))
    return pl.pallas_call(
        body,
        grid_spec=pltpu.PrefetchScalarGridSpec(
            num_scalar_prefetch=1,
            grid=(1,),
            in_specs=[whole(a) for a in args],
            out_specs=[whole(a) for a in out_shape],
            scratch_shapes=list(scratch),
        ),
        out_shape=out_shape,
        compiler_params=pltpu.CompilerParams(vmem_limit_bytes=limit * MIB),
        cost_estimate=FREE,
        name=name,
    )(scalars, *args)


def fold(scalars, keep, got, which):
    def body(sc, keep_ref, got_ref, keep_out, send_out):
        bit = 0 if which is None else sc[which]
        for i in range(keep_ref.shape[0]):
            keep_out[i] = keep_ref[i, bit].astype(F32) + got_ref[i, bit].astype(F32)
            send_out[i] = (keep_ref[i, 1 - bit].astype(F32) + got_ref[i, 1 - bit].astype(F32)).astype(BF16)

    shape = (keep.shape[0], *keep.shape[2:])
    out_shape = [jax.ShapeDtypeStruct(shape, F32), jax.ShapeDtypeStruct(shape, BF16)]
    return whole_call(body, scalars, (keep, got.reshape(keep.shape)), out_shape, "fold")


def fold_halves(scalars, left, left_got, right, right_got):
    rows, half = left.shape[2:]

    def body(sc, lk, lg, rk, rg, left_out, right_out, send_out):
        left_out[0] = lk[0, 0] + lg[0, 0].astype(F32)
        right_out[0] = rk[0, 0] + rg[0, 0].astype(F32)
        send_out[0, :, :half] = (lk[0, 1] + lg[0, 1].astype(F32)).astype(BF16)
        send_out[0, :, half:] = (rk[0, 1] + rg[0, 1].astype(F32)).astype(BF16)

    one = jax.ShapeDtypeStruct((1, rows, half), F32)
    out_shape = [one, one, jax.ShapeDtypeStruct((1, rows, 2 * half), BF16)]
    args = (left, left_got.reshape(left.shape), right, right_got.reshape(right.shape))
    return whole_call(body, scalars, args, out_shape, "fold_halves")


def join(scalars, keep, got):
    def body(sc, keep_ref, got_ref, out):
        out[...] = (keep_ref[...].astype(F32) + got_ref[...].astype(F32)).astype(BF16)

    out_shape = [jax.ShapeDtypeStruct(keep.shape, BF16)]
    return whole_call(body, scalars, (keep, got.reshape(keep.shape)), out_shape, "join")[0]


def append(scalars, held, got):
    def body(sc, held_ref, got_ref, out):
        count = held_ref.shape[0]
        out[0:count] = held_ref[...]
        out[count : 2 * count] = got_ref[...]

    out_shape = [jax.ShapeDtypeStruct((2 * held.shape[0], *held.shape[1:]), held.dtype)]
    return whole_call(body, scalars, (held, got), out_shape, "append")[0]


def merge_low(scalars, down, down_got, out, out_got, which):
    zys, lows, width = down.shape
    outs = out.shape[1]
    fill = -outs % 16

    def body(sc, down_ref, down_got_ref, out_ref, out_got_ref, keep_out, send_out):
        for i in range(zys // 2):
            for target, bit in ((keep_out, sc[which]), (send_out, 1 - sc[which])):
                t = 2 * i + bit
                first = down_ref[t].astype(F32) + down_got_ref[t].astype(F32)
                second = out_ref[t].astype(F32) + out_got_ref[t].astype(F32)
                rows = [first, second] + ([jnp.zeros((fill, width), F32)] if fill else [])
                target[i] = jnp.concatenate(rows, axis=0).astype(target.dtype)

    shape = (zys // 2, lows + outs + fill, width)
    out_shape = [jax.ShapeDtypeStruct(shape, F32), jax.ShapeDtypeStruct(shape, BF16)]
    args = (down, down_got.reshape(down.shape), out, out_got.reshape(out.shape))
    return whole_call(body, scalars, args, out_shape, "merge_low")


def first_norm_back(scalars, tokens, dy, gain, parts):
    nseq, rows, width = tokens.shape

    def body(sc, tokens_ref, dy_ref, gain_ref, lk, rk, got, out):
        seq = sc[6]
        for i in range(nseq):
            here = seq == i
            dh = jnp.where(here, jnp.concatenate([lk[0], rk[0]], axis=1), got[0].astype(F32))
            n, scale = normed_parts(tokens_ref[i].astype(F32))
            out[i] = dy_ref[i] + norm_back(dh, n, scale, gain_ref[...])

    out_shape = [jax.ShapeDtypeStruct(tokens.shape, F32)]
    return whole_call(body, scalars, (tokens, dy, gain, *parts), out_shape, "first_norm_back")[0]


def piece_of(places):
    def block(t, sc):
        d = t ^ sc[0]
        return (d % 2 * 2 ** places[0] + d // 2 % 2 * 2 ** places[1] + d // 4 % 2 * 2 ** places[2], 0, 0)

    return block


def up_rows_kernel(parts, sc, own_ref, other_ref, out_ref):
    first = sc[3] == 0
    own, other = own_ref[0].astype(F32), other_ref[0].astype(F32)
    split = own.shape[1] // parts
    for p in range(parts):
        cols = slice(p * split, (p + 1) * split)
        out_ref[0, :, 2 * p * split : (2 * p + 1) * split] = jnp.where(first, own[:, cols], other[:, cols])
        out_ref[0, :, (2 * p + 1) * split : (2 * p + 2) * split] = jnp.where(first, other[:, cols], own[:, cols])


def up_rows(scalars, own, other, parts):
    pieces, high, wide = own.shape
    return pl.pallas_call(
        functools.partial(up_rows_kernel, parts),
        grid_spec=pltpu.PrefetchScalarGridSpec(
            num_scalar_prefetch=1,
            grid=(pieces,),
            in_specs=[pl.BlockSpec((1, high, wide), piece_of((2, 1, 0)))] * 2,
            out_specs=pl.BlockSpec((1, high, 2 * wide), lambda t, sc: (t, 0, 0)),
        ),
        out_shape=jax.ShapeDtypeStruct((pieces, high, 2 * wide), F32),
        compiler_params=pltpu.CompilerParams(vmem_limit_bytes=8 * MIB),
        cost_estimate=FREE,
        name="up_rows",
    )(scalars, own, other)


def low_rows_kernel(lows, outs, sc, own_ref, other_ref, down_ref, out_ref):
    first = sc[3] == 0
    own, other = own_ref[0].astype(F32), other_ref[0].astype(F32)
    for c, value in enumerate((jnp.where(first, own, other), jnp.where(first, other, own))):
        down_ref[c, 0] = value[:lows]
        out_ref[c, 0] = value[lows : lows + outs]


def low_rows(scalars, own, other, lows, outs):
    pieces, low, width = own.shape
    return pl.pallas_call(
        functools.partial(low_rows_kernel, lows, outs),
        grid_spec=pltpu.PrefetchScalarGridSpec(
            num_scalar_prefetch=1,
            grid=(pieces,),
            in_specs=[pl.BlockSpec((1, low, width), piece_of((1, 2, 0)))] * 2,
            out_specs=[
                pl.BlockSpec((2, 1, lows, width), lambda t, sc: (0, t, 0, 0)),
                pl.BlockSpec((2, 1, outs, width), lambda t, sc: (0, t, 0, 0)),
            ],
        ),
        out_shape=[
            jax.ShapeDtypeStruct((2, pieces, lows, width), F32),
            jax.ShapeDtypeStruct((2, pieces, outs, width), F32),
        ],
        compiler_params=pltpu.CompilerParams(vmem_limit_bytes=8 * MIB),
        cost_estimate=FREE,
        name="low_rows",
    )(scalars, own, other)


def qkv_rows_kernel(groups, high, own, gw, sc, own_ref, other_ref, out_ref, gain_ref, conv_ref):
    core = sc[3]
    swapped = [(g ^ sc[4]) % 2 * 2 + (g ^ sc[4]) // 2 for g in range(groups)]
    convs = []
    gains = None
    for k in swapped:
        tail = own_ref[k].astype(F32)[high:]
        gains = tail[0:4, :own] if gains is None else gains + tail[0:4, :own]
        convs.append(tail[4:7, :])
    gain_ref[...] = gains
    for j in range(3):
        cols = slice(j * gw, (j + 1) * gw)
        conv_ref[:, j * groups * gw : (j + 1) * groups * gw] = jnp.concatenate([c[:, cols] for c in convs], axis=1)
    for c in range(2):
        pieces = [jnp.where(core == c, own_ref[k], other_ref[k]).astype(F32) for k in swapped]
        for j in range(3):
            cols = slice(j * gw, (j + 1) * gw)
            out = slice(j * groups * gw, (j + 1) * groups * gw)
            out_ref[c, :, out] = jnp.concatenate([p[:high, cols] for p in pieces], axis=1)


def qkv_rows(scalars, args, high):
    groups, _, cols = args[0].shape
    own = 2 * high
    shapes = [(2, high, groups * cols), (4, own), (3, groups * cols)]
    out_shape = [jax.ShapeDtypeStruct(shape, F32) for shape in shapes]
    return whole_call(
        functools.partial(qkv_rows_kernel, groups, high, own, cols // 3), scalars, args, out_shape, "qkv_rows"
    )


def per_device(tokens, cotangent, lengths, ln1_gain, ln1_bias, w_qkv, w_conv, w_out, ln2_gain, ln2_bias, w_up, w_down):
    nseq, rows, width = tokens.shape
    half = width // 2
    count = lax.axis_size("ctx")
    parts = lax.axis_size("fsdp")
    rank = lax.axis_index("ctx")
    index = lax.axis_index("fsdp")
    hidden = w_up.shape[1]
    own_rows = ln1_gain.shape[0]
    zys = nseq * GROUPS
    share = count // zys
    hp = HEADS // GROUPS
    hd = width // HEADS
    gw = hp * hd
    mine = rank % share
    core = rank % 2
    zy = rank // share
    seq = zy // GROUPS
    group = zy % GROUPS
    bit_b, bit_a, bit_s = share, 2 * share, 4 * share
    share_bits = bits(share)
    positions = rank * rows + jnp.arange(rows, dtype=jnp.int32)
    valid = positions[None, :] < lengths[:, None]
    high_bits = [index // mask % 2 for mask in reversed(bits(parts))]
    scalars = [zy, mine, lengths[seq], core, group, index, seq, zy // 2 % 2, zy % 2] + high_bits
    scalars = jnp.stack(scalars).astype(jnp.int32)
    at_s, at_a, at_b, at_x = 6, 7, 8, 9

    own_seq, far_seq = at(tokens, seq), at(tokens, 1 - seq)
    w_conv = lax.optimization_barrier((w_conv, far_seq))[0]
    fsdp_bits = bits(parts)
    split = hidden // parts // 2
    packed = pack(scalars, (ln1_gain, ln1_bias, ln2_gain, ln2_bias), w_conv)
    w_qkv, w_out = lax.optimization_barrier((w_qkv, w_out, packed))[:2]
    first = first_part(scalars, w_qkv, w_out, gw)
    pair = jnp.stack([own_seq, exch(far_seq, "ctx", bit_s)])
    left, right = pair[..., :half], pair[..., half:]
    gains, taps = parameters(scalars, gather_list(packed, "fsdp", fsdp_bits), own_rows, gw)
    gain_one, bias_one, gain_two, bias_two = (gains[i : i + 1] for i in range(4))
    first = gather_list(first, "fsdp", fsdp_bits)
    w_up, w_down = lax.optimization_barrier((w_up, w_down, left, gains, first[-1]))[:2]
    left = jnp.stack([left, exch(left, "ctx", bit_a)], axis=1)
    right = jnp.stack([right, exch(right, "ctx", bit_b)], axis=1)
    left = jnp.stack([left, exch(left, "ctx", bit_b)], axis=2)
    right = jnp.stack([right, exch(right, "ctx", bit_a)], axis=1)
    left = gather_list(left.reshape(1, zys, rows, half), "ctx", share_bits)
    right = gather_list(right.reshape(1, zys, rows, half), "ctx", share_bits)

    both_cores = lambda pieces: [pieces, [exch(piece, "ctx", 1) for piece in pieces]]
    first = both_cores(first)
    if split == width:
        ups = gather_list(rest_part(scalars, w_up, w_down, parts), "fsdp", fsdp_bits)
        downs = []
    else:
        ups = gather_list(up_part(scalars, w_up, parts)[None], "fsdp", fsdp_bits)
        downs = gather_list(at(w_down.reshape(2, split, width), core)[None], "fsdp", fsdp_bits)

    dtop = jnp.where(valid[..., None], cotangent, jnp.zeros_like(cotangent)).reshape(nseq * rows, width)
    dtop_other = exch(dtop, "ctx", 1)
    left[0], taps, gain_one, bias_one = lax.optimization_barrier(
        (left[0], taps, gain_one, bias_one, gain_two, bias_two, dtop)
    )[:4]
    h_one, pre, attn_t, o, lse, q, k, kt, v = attention(
        scalars, left, right, first, taps, gain_one, bias_one, share, hp, hd
    )
    classes = [[i for i in range(count) if i % share == s] for s in range(share)]
    swap = lambda x: lax.all_to_all(x, "ctx", 0, 0, tiled=True, axis_index_groups=classes)
    attn_t = swap(attn_t).reshape(nseq, width, rows)

    order = Order()
    y_one, h_two, w_out_full = mix(scalars, attn_t, tokens, gain_two, bias_two, first, parts)
    h_other = exch(h_two, "ctx", 1)
    r, dupper, dh_keep, dh_send, y_keep, y_send, down_far = feed(
        scalars, h_two, h_other, dtop, dtop_other, ups, downs, split
    )
    dh_other = exch(dh_send, "ctx", 1)
    dtop_pair = jnp.concatenate([dtop, dtop_other])

    near_base = index // (parts // 2) * (parts // 2)

    def near(term):
        return jnp.stack([term(near_base + p) for p in range(parts // 2)])

    def fsdp_more(keep, got):
        for i, mask in enumerate(reversed(fsdp_bits[:-1])):
            keep, send = fold(scalars, keep.reshape(1, 2, mask, *keep.shape[1:]), got, at_x + 1 + i)
            keep, got = keep[0], exch(send[0], "fsdp", mask)
        return keep, got

    down_term = lambda p: tn(at(r, p), dtop_pair)
    down_got = exch(down_far, "fsdp", parts // 2)
    dh_keep, dh_other = order(dh_keep, dh_other)
    dy_one, dout_t, small_two, out_keep, out_send = mix_back(
        scalars, dh_keep, dh_other, y_one, dtop, gain_two, w_out_full, attn_t, parts
    )
    order.mark(dout_t)
    r, dupper, y_keep, y_send, h_two, h_other = order(r, dupper, y_keep, y_send, h_two, h_other)
    h_pair = jnp.concatenate([h_two, h_other], axis=1)
    dout_t = swap(dout_t.reshape(zys, gw, rows))

    def cut(held, axis, bit):
        keep = lax.dynamic_slice_in_dim(held, bit, 1, axis)
        send = lax.dynamic_slice_in_dim(held, 1 - bit, 1, axis)
        return keep, send.astype(BF16)

    zy_bits = {"s": (0, bit_s, zy // 4), "a": (1, bit_a, zy // 2 % 2), "b": (2, bit_b, zy % 2)}
    out_keep = out_keep.reshape(1, 2, parts // 2, *out_keep.shape[1:])
    out_keep, out_send = fold(scalars, out_keep, exch(out_send, "ctx", 1), at_x)
    out_keep, out_got = out_keep[0], exch(out_send[0], "fsdp", parts // 2)
    grad_up = jnp.einsum("pnk,nf->pkf", h_pair, dupper, preferred_element_type=F32)
    grad_up = grad_up.reshape(parts, 2, 2, 2, own_rows // zys, hidden // 2)
    up_keep, up_send = cut(grad_up, 2, zy_bits["a"][2])
    down_keep = near(down_term)
    y_got = exch(y_send, "ctx", 1)

    dout_t, up_keep, up_send, down_keep, out_keep, y_got = lax.optimization_barrier(
        (dout_t, up_keep, up_send, down_keep, out_keep, y_got)
    )
    up_got = exch(up_send, "ctx", bit_a)
    lows = down_keep.shape[1] // zys
    outs = out_keep.shape[1] // zys
    high = own_rows // zys
    up_rest = (high, hidden // 2)
    tail_rows = own_rows // 2 + TAIL
    dw_rest = (tail_rows, 3 * gw)

    keep = {"up": up_keep, "down": down_keep, "out": out_keep, "dout": dout_t}
    got = {"up": up_got, "down": down_got, "out": out_got}
    heads_keep, heads_got = [], []
    done = {}

    def fold_step(x, which, shape, axis, mask):
        def run():
            kept, send = fold(scalars, order(keep[x]).reshape(shape), got[x], which)
            order.mark(send)
            keep[x] = kept
            got[x] = exch(send, axis, mask)

        return run

    def join_step(x, shape, mask):
        def run():
            keep[x] = order.mark(join(scalars, order(keep[x]).reshape(shape), got[x]))
            got[x] = exch(keep[x], "ctx", mask)

        return run

    def append_step(x, mask):
        def run():
            keep[x] = order.mark(append(scalars, order(keep[x]), got[x]))
            got[x] = exch(keep[x], "ctx", mask)

        return run

    def head(h):
        def run():
            kept, sent = attend_back(scalars, h, q, k, kt, v, order(keep["dout"]), o, lse, share, rows)
            heads_keep.append(order.mark(kept))
            heads_got.extend(exch(sent[x - 1 : x], "ctx", x) for x in range(1, share))

        return run

    def low_first():
        keep["down"], keep["out"] = order(keep["down"], keep["out"])
        for x in ("down", "out"):
            keep[x], got[x] = fsdp_more(keep[x], got[x])
        kept, send = merge_low(
            scalars,
            keep["down"].reshape(zys, lows, width),
            got["down"],
            keep["out"].reshape(zys, outs, width),
            got["out"],
            at_b,
        )
        order.mark(send)
        keep["low"] = kept
        got["low"] = exch(send, "ctx", bit_b)

    low_rest = (lows + outs + -outs % 16, width)

    def up_between():
        keep["up"], got["up"] = fsdp_more(keep["up"].reshape(parts // 2, 2, 2, *up_rest), got["up"])
        fold_step("up", at_b, (2, 2, *up_rest), "ctx", bit_b)()

    def back():
        last = order(heads_keep[-1])
        left_keep, left_send, right_keep, right_send, dw_keep, dw_send = project_back(
            scalars, heads_keep[:-1] + [last], heads_got, left[0], right[0], h_one, pre, taps, small_two, first,
            share, rows, parts,
        )
        order.mark(dw_send)
        keep.update(left=left_keep, right=right_keep, qkv=dw_keep)
        got["left"] = exch(left_send, "ctx", bit_a)
        got["right"] = exch(right_send, "ctx", bit_b)
        got["qkv"] = exch(dw_send, "ctx", 1)

    def qkv_between():
        keep["qkv"], got["qkv"] = fsdp_more(keep["qkv"].reshape(parts // 2, *dw_rest), got["qkv"])
        join_step("qkv", dw_rest, bit_s)()

    def qkv_whole():
        block = join(scalars, order(keep["qkv"]), got["qkv"])
        for mask in share_bits[1:]:
            block = join(scalars, block, exch(block, "ctx", mask))
        keep["qkv"] = order.mark(block[None])
        got["qkv"] = exch(keep["qkv"], "ctx", bit_a)

    def halves():
        kept = order(keep["left"], keep["right"])
        keep["left"], keep["right"], send = fold_halves(scalars, kept[0], got["left"], kept[1], got["right"])
        order.mark(send)
        got["input"] = exch(send, "ctx", bit_s)

    def input_end():
        kept = (keep["left"], keep["right"], got["input"])
        total = (order(y_keep) + y_got.astype(F32)).reshape(nseq, rows, width)
        done["output"] = order.mark(jnp.where(valid[..., None], y_one + total, 0.0).astype(BF16))
        done["input"] = order.mark(first_norm_back(scalars, tokens, order(dy_one), gain_one, kept))

    def qkv_end():
        grad, gains, convs = qkv_rows(scalars, (order(keep["qkv"]), got["qkv"]), own_rows // 2)
        done["qkv"] = order.mark(grad.reshape(own_rows, 3 * width))
        share_cols = 3 * width // parts
        done["gains"] = gains
        done["conv"] = lax.dynamic_slice_in_dim(convs, index * share_cols, share_cols, 1)

    def low_end():
        down_grad, out_grad = low_rows(scalars, order(keep["low"]), got["low"], lows, outs)
        done["down"] = order.mark(down_grad.reshape(hidden // parts, width))
        done["out"] = out_grad.reshape(own_rows, width)

    def up_end():
        grad = up_rows(scalars, order(keep["up"]), got["up"], parts)
        done["up"] = order.mark(grad.reshape(own_rows, hidden))

    steps = {
        "head 0": head(0),
        "head 1": head(1),
        "head 2": head(2),
        "low b": low_first,
        "low a": fold_step("low", at_a, (2, 2, *low_rest), "ctx", bit_a),
        "low s": fold_step("low", at_s, (1, 2, *low_rest), "ctx", bit_s),
        "low sum": join_step("low", (1, *low_rest), bit_s),
        "low gather b": append_step("low", bit_b),
        "low gather a": append_step("low", bit_a),
        "low core": append_step("low", 1),
        "low end": low_end,
        "up x": fold_step("up", at_x, (1, 2, parts // 2 * 4 * high, hidden // 2), "fsdp", parts // 2),
        "up b": up_between,
        "up s": fold_step("up", at_s, (1, 2, *up_rest), "ctx", bit_s),
        "up sum": join_step("up", (1, *up_rest), bit_s),
        "up gather a": append_step("up", bit_a),
        "up gather b": append_step("up", bit_b),
        "up core": append_step("up", 1),
        "up end": up_end,
        "back": back,
        "qkv x": fold_step("qkv", at_x, (1, 2, parts // 2, *dw_rest), "fsdp", parts // 2),
        "qkv s": qkv_between,
        "qkv a": qkv_whole,
        "qkv gather b": append_step("qkv", bit_b),
        "qkv core": append_step("qkv", 1),
        "qkv end": qkv_end,
        "right a": fold_step("right", None, (1, 2, 2, rows, half), "ctx", bit_a),
        "left b": fold_step("left", None, (1, 2, 2, rows, half), "ctx", bit_b),
        "input s": halves,
        "input end": input_end,
    }
    for name in LINE:
        steps[name]()
    output, input_grad, gains = done["output"], done["input"], done["gains"]
    w_qkv_grad, w_conv_grad, w_out_grad = done["qkv"], done["conv"], done["out"]
    w_up_grad, w_down_grad = done["up"], done["down"]

    return (
        output,
        input_grad,
        gains[0],
        gains[1],
        w_qkv_grad,
        w_conv_grad,
        w_out_grad,
        gains[2],
        gains[3],
        w_up_grad,
        w_down_grad,
    )


def solution(mesh):
    rows = P("fsdp", "ctx", None)
    first = P("fsdp")
    weight = P("fsdp", None)
    second = P(None, "fsdp")
    in_specs = (rows, rows, first, first, first, weight, second, weight, first, first, weight, weight)
    out_specs = (rows, rows, first, first, weight, second, weight, first, first, weight, weight)
    return jax.shard_map(per_device, mesh=mesh, in_specs=in_specs, out_specs=out_specs, check_vma=False)
```

```python
import functools

import jax
import jax.numpy as jnp
from jax import lax
from jax.experimental import pallas as pl
from jax.experimental.pallas import tpu as pltpu
from jax.sharding import PartitionSpec as P

HEADS = 12
GROUPS = 4
EPS = 1e-05
RIM = 16
PIECES = 8
TAIL = 16
MASKED = -1e30
MIB = 1024 * 1024
F32 = jnp.float32
BF16 = jnp.bfloat16
LINE = (
    "head 0",
    "low b",
    "head 1",
    "head 2",
    "up x",
    "low a",
    "back",
    "low s",
    "up b",
    "qkv x",
    "low sum",
    "up s",
    "right a",
    "low gather b",
    "up sum",
    "left b",
    "qkv s",
    "up gather a",
    "input s",
    "low gather a",
    "qkv a",
    "up gather b",
    "qkv gather b",
    "up core",
    "low core",
    "low end",
    "input end",
    "qkv core",
    "up end",
    "qkv end",
)
FREE = pl.CostEstimate(flops=0, bytes_accessed=0, transcendentals=0)


def exch(value, axis, mask):
    count = lax.axis_size(axis)
    return lax.ppermute(value, axis, [(i, i ^ mask) for i in range(count)])


def bits(count):
    return [1 << b for b in range(count.bit_length() - 1)]


def at(stack, index):
    return lax.dynamic_index_in_dim(stack, index, 0, keepdims=False)


def flip(stack, index):
    return jnp.stack([at(stack, k ^ index) for k in range(stack.shape[0])])


def gather_list(value, axis, masks):
    held = [value]
    for mask in masks:
        held.append(exch(held[0] if len(held) == 1 else jnp.concatenate(held), axis, mask))
    return held


def after(value, *others):
    return lax.optimization_barrier((value, *others))[0]


class Order:
    def __init__(self):
        self.last = None

    def __call__(self, *values):
        if self.last is not None:
            values = lax.optimization_barrier((*values, self.last))[:-1]
        return values if len(values) > 1 else values[0]

    def mark(self, value):
        self.last = value
        return value


def normed_parts(values):
    centre = values - jnp.mean(values, axis=-1, keepdims=True)
    scale = lax.rsqrt(jnp.mean(centre * centre, axis=-1, keepdims=True) + EPS)
    return centre * scale, scale


def norm_back(grad, normed, scale, gain):
    dnorm = grad * gain
    return scale * (
        dnorm
        - jnp.mean(dnorm, axis=-1, keepdims=True)
        - normed * jnp.mean(dnorm * normed, axis=-1, keepdims=True)
    )


def nn(a, b):
    return lax.dot_general(a, b, (((1,), (0,)), ((), ())), preferred_element_type=F32)


def nt(a, b):
    return lax.dot_general(a, b, (((1,), (1,)), ((), ())), preferred_element_type=F32)


def tn(a, b):
    return lax.dot_general(a, b, (((0,), (0,)), ((), ())), preferred_element_type=F32)


def piece_copies(lists, scratch, sems, index, core, take=None, cols=None):
    copies = []
    cores = len(lists)
    for r, pieces in enumerate(lists):
        k = 0
        for stack in pieces:
            for i in range(stack.shape[0]):
                first, size = take or (0, stack.shape[1])
                part = (core ^ r) if cores == 2 else 0
                start = pl.multiple_of(((index ^ k) * cores + part) * size, size)
                target = scratch.at[pl.ds(start, size)] if cols is None else scratch.at[pl.ds(start, size), cols]
                source = stack.at[i, pl.ds(first, size)]
                copies.append(pltpu.make_async_copy(source, target, sems.at[len(copies)]))
                k += 1
    return copies


def fsdp_size(lists):
    return sum(stack.shape[0] for stack in lists[0])


def split_lists(refs, counts):
    lists, at_ref = [], 0
    for n in counts:
        lists.append(refs[at_ref : at_ref + n])
        at_ref += n
    return lists, refs[at_ref:]


ANY = pl.BlockSpec(memory_space=pl.ANY)


def pack(scalars, gains, w_conv):
    own = gains[0].shape[0]
    cols = w_conv.shape[1]

    def body(sc, *refs):
        rows = [jnp.concatenate([ref[...].astype(F32), jnp.zeros((1, cols - own), F32)], axis=1) for ref in refs[:4]]
        rows += [refs[4][...].astype(F32), jnp.zeros((16 - 7, cols), F32)]
        refs[5][0] = jnp.concatenate(rows, axis=0).astype(BF16)

    args = [g.reshape(1, own) for g in gains] + [w_conv]
    return whole_call(body, scalars, args, [jax.ShapeDtypeStruct((1, 16, cols), BF16)], "pack")[0]


def parameters(scalars, packed, own, gw):
    parts = sum(stack.shape[0] for stack in packed)
    cols = packed[0].shape[2]
    total = parts * cols // 3

    def body(sc, *refs):
        held = [ref[i].astype(F32) for ref in refs[:-2] for i in range(ref.shape[0])]
        ordered = []
        for p in range(parts):
            picked = held[0]
            for k in range(1, parts):
                picked = jnp.where((p ^ sc[5]) == k, held[k], picked)
            ordered.append(picked)
        refs[-2][...] = jnp.concatenate([x[0:4, :own] for x in ordered], axis=1)
        taps = jnp.concatenate([x[4:7] for x in ordered], axis=1)
        for j in range(3):
            picked = taps[:, j * total : j * total + gw]
            for g in range(1, GROUPS):
                start = j * total + g * gw
                picked = jnp.where(sc[4] == g, taps[:, start : start + gw], picked)
            refs[-1][:, j * gw : (j + 1) * gw] = picked

    out_shape = [jax.ShapeDtypeStruct((4, parts * own), F32), jax.ShapeDtypeStruct((3, 3 * gw), F32)]
    return whole_call(body, scalars, packed, out_shape, "parameters")


def first_part_kernel(groups, gw, sc, w, w_out, out):
    group = sc[4]
    rows = w.shape[0]
    width = groups * gw
    for j in range(3):
        picked = w[:, j * width : j * width + gw]
        for g in range(1, groups):
            start = j * width + g * gw
            picked = jnp.where(group == g, w[:, start : start + gw], picked)
        out[0, :rows, j * gw : (j + 1) * gw] = picked
    out[0, :rows, 3 * gw :] = jnp.zeros((rows, width - 3 * gw), BF16)
    out[0, rows:, :] = w_out[...]


def first_part(scalars, w_qkv, w_out, gw):
    rows, cols = w_qkv.shape
    width = w_out.shape[1]
    return pl.pallas_call(
        functools.partial(first_part_kernel, GROUPS, gw),
        grid_spec=pltpu.PrefetchScalarGridSpec(
            num_scalar_prefetch=1,
            grid=(1,),
            in_specs=[
                pl.BlockSpec((rows // 2, cols), lambda i, sc: (sc[3], 0)),
                pl.BlockSpec((rows // 2, width), lambda i, sc: (sc[3], 0)),
            ],
            out_specs=pl.BlockSpec((1, rows, width), lambda i, sc: (0, 0, 0)),
        ),
        out_shape=jax.ShapeDtypeStruct((1, rows, width), BF16),
        compiler_params=pltpu.CompilerParams(vmem_limit_bytes=8 * MIB),
        cost_estimate=FREE,
        name="first_part",
    )(scalars, w_qkv, w_out)


def up_part_kernel(sc, w, out):
    out[...] = w[...]


def up_part(scalars, w_up, parts):
    rows, cols = w_up.shape
    split = cols // parts // 2
    if split % 128:
        picked = lax.dynamic_index_in_dim(w_up.reshape(rows, parts, 2, split), scalars[3], 2, keepdims=False)
        return picked.reshape(rows, cols // 2)
    return pl.pallas_call(
        up_part_kernel,
        grid_spec=pltpu.PrefetchScalarGridSpec(
            num_scalar_prefetch=1,
            grid=(parts,),
            in_specs=[pl.BlockSpec((rows, split), lambda p, sc: (0, 2 * p + sc[3]))],
            out_specs=pl.BlockSpec((rows, split), lambda p, sc: (0, p)),
        ),
        out_shape=jax.ShapeDtypeStruct((rows, cols // 2), BF16),
        compiler_params=pltpu.CompilerParams(vmem_limit_bytes=8 * MIB),
        cost_estimate=FREE,
        name="up_part",
    )(scalars, w_up)


def rest_part_kernel(parts, sc, w_up, w_down, out, sems):
    core = sc[3]
    own, cols = w_up.shape
    split = cols // parts // 2
    copies = []
    for p in range(parts):
        source = w_up.at[:, pl.ds(pl.multiple_of((2 * p + core) * split, split), split)]
        copies.append(pltpu.make_async_copy(source, out.at[0, pl.ds(p * own, own)], sems.at[p]))
    source = w_down.at[pl.ds(pl.multiple_of(core * split, split), split)]
    copies.append(pltpu.make_async_copy(source, out.at[0, pl.ds(parts * own, split)], sems.at[parts]))
    for copy in copies:
        copy.start()
    for copy in copies:
        copy.wait()


def rest_part(scalars, w_up, w_down, parts):
    own, cols = w_up.shape
    split = cols // parts // 2
    rows = parts * own + split
    return pl.pallas_call(
        functools.partial(rest_part_kernel, parts),
        grid_spec=pltpu.PrefetchScalarGridSpec(
            num_scalar_prefetch=1,
            grid=(1,),
            in_specs=[ANY] * 2,
            out_specs=ANY,
            scratch_shapes=[pltpu.SemaphoreType.DMA((parts + 1,))],
        ),
        out_shape=jax.ShapeDtypeStruct((1, rows, split), BF16),
        compiler_params=pltpu.CompilerParams(vmem_limit_bytes=2 * MIB),
        cost_estimate=FREE,
        name="rest_part",
    )(scalars, w_up, w_down)


def attention_kernel(share, hp, hd, rows, per, last, shares, counts, sc, *refs):
    (left, right), refs = split_lists(refs, (len(shares), len(shares)))
    taps, gain, bias = refs[:3]
    lists, refs = split_lists(refs[3:], counts)
    h_ref, pre_ref, at_ref, o_ref, lse_ref = refs[:5]
    kept = refs[5:9]
    buf, w, sems, save_sems, q_ref, k_ref, kt_ref, v_ref, vt_ref = refs[9:]
    step = pl.program_id(0)
    saves = [
        pltpu.make_async_copy(source, target, save_sems.at[i])
        for i, (source, target) in enumerate(zip((q_ref, k_ref, kt_ref, v_ref), kept))
    ]

    @pl.when(step <= last)
    def _():
        project_step(share, hp, hd, rows, per, sc, left, right, taps, gain, bias, lists, h_ref, pre_ref, q_ref, k_ref,
                     kt_ref, v_ref, vt_ref, buf, w, sems)

    @pl.when(step == last + 1)
    def _():
        for copy in saves:
            copy.start()

    @pl.when(step > last)
    def _():
        attend_step(share, rows, sc, step - last - 1, q_ref, k_ref, vt_ref, at_ref, o_ref, lse_ref)

    @pl.when(step == last + hp)
    def _():
        for copy in saves:
            copy.wait()


def project_step(share, hp, hd, rows, per, sc, left, right, taps, gain, bias, lists, h_ref, pre_ref, q_ref, k_ref,
                 kt_ref, v_ref, vt_ref, buf, w, sems):
    step = pl.program_id(0)

    @pl.when(step == 0)
    def _():
        copies = piece_copies(lists, w, sems, sc[5], sc[3], (0, w.shape[0] // 2 // fsdp_size(lists)))
        for copy in copies:
            copy.start()
        for copy in copies:
            copy.wait()

    mine = sc[1]
    length = sc[2]
    gw = hp * hd
    size = per * share * rows
    parts = []
    for z in range(per):
        at_z = z ^ (sc[0] % per)
        pieces = []
        for refs_l, refs_r in zip(left, right):
            pieces += [jnp.concatenate([refs_l[i, at_z], refs_r[i, at_z]], axis=1) for i in range(refs_l.shape[0])]
        for j in range(share):
            picked = pieces[0]
            for k in range(1, share):
                picked = jnp.where((j ^ mine) == k, pieces[k], picked)
            parts.append(picked.astype(F32))
    x = jnp.concatenate(parts, axis=0)
    n, _ = normed_parts(x)
    h = (n * gain[...] + bias[...]).astype(BF16)
    h_ref[...] = h
    pre = nn(h, w[:, : 3 * gw]).astype(BF16)
    pre_ref[...] = pre

    @pl.when(step == 0)
    def _():
        buf[0:8, :] = jnp.zeros((8, 3 * gw), F32)

    buf[8:, :] = pre.astype(F32)
    conv = (
        taps[0:1, :] * buf[8 : 8 + size, :]
        + taps[1:2, :] * buf[7 : 7 + size, :]
        + taps[2:3, :] * buf[6 : 6 + size, :]
    )
    buf[0:8, :] = buf[size : size + 8, :]
    qs = conv[:, :gw].astype(BF16)
    kf = conv[:, gw : 2 * gw]
    vf = conv[:, 2 * gw :]
    q_own = []
    for z in range(per):
        start = z * share * rows
        picked = qs[start : start + rows]
        for j in range(1, share):
            picked = jnp.where(mine == j, qs[start + j * rows : start + (j + 1) * rows], picked)
        q_own.append(picked)
    q_own = (jnp.concatenate(q_own, axis=0).astype(F32) * 0.125).astype(BF16)
    lane = lax.broadcasted_iota(jnp.int32, (per * rows, hd), 1)
    ones = jnp.where(lane == 0, 1.0, 0.0).astype(BF16)
    lane = lax.broadcasted_iota(jnp.int32, (size, hd), 1)
    pos = step * size + lax.broadcasted_iota(jnp.int32, (size, hd), 0)
    mask = jnp.where((lane == 0) & (pos >= length), MASKED, 0.0).astype(BF16)
    ks = kf.astype(BF16)
    vs = vf.astype(BF16)
    kt = kf.T.astype(BF16)
    vt = vf.T.astype(BF16)
    own = pl.ds(pl.multiple_of(step * per * rows, per * rows), per * rows)
    every = pl.ds(pl.multiple_of(step * size, size), size)
    for h in range(hp):
        cols = slice(h * hd, (h + 1) * hd)
        q_ref[h, own, :] = jnp.concatenate([q_own[:, cols], ones], axis=1)
        k_ref[h, every, :] = jnp.concatenate([ks[:, cols], mask], axis=1)
        v_ref[h, every, :] = vs[:, cols]
        kt_ref[h, :, every] = kt[cols]
        vt_ref[h, :, every] = vt[cols]


def attention(scalars, left, right, w_lists, taps, gain, bias, share, hp, hd):
    counts = [len(pieces) for pieces in w_lists]
    flat = [piece for pieces in w_lists for piece in pieces]
    _, zys, rows, half = left[0].shape
    width = 2 * half
    gw = hp * hd
    per = 2
    last = zys // per - 1
    total = zys * share * rows
    own = zys * rows
    size = per * share * rows
    shares = [a.shape[0] for a in left]
    body = functools.partial(attention_kernel, share, hp, hd, rows, per, last, shares, counts)
    whole = lambda *shape: pl.BlockSpec(shape, lambda t, sc: (0,) * len(shape))
    block = lambda t: jnp.minimum(t, last)
    head = lambda t: jnp.maximum(t - last - 1, 0)
    pieces = [pl.BlockSpec((n, per, rows, half), lambda t, sc: (0, block(t) ^ (sc[0] // per), 0, 0)) for n in shares]
    kept = [(hp, own, 2 * hd), (hp, total, 2 * hd), (hp, hd, total), (hp, total, hd)]
    return pl.pallas_call(
        body,
        grid_spec=pltpu.PrefetchScalarGridSpec(
            num_scalar_prefetch=1,
            grid=(last + 1 + hp,),
            in_specs=pieces * 2 + [whole(3, 3 * gw), whole(1, width), whole(1, width)] + [ANY] * len(flat),
            out_specs=[
                pl.BlockSpec((size, width), lambda t, sc: (block(t), 0)),
                pl.BlockSpec((size, 3 * gw), lambda t, sc: (block(t), 0)),
                pl.BlockSpec((zys, hd, rows), lambda t, sc: (0, head(t), 0)),
                pl.BlockSpec((1, hd, own), lambda t, sc: (head(t), 0, 0)),
                pl.BlockSpec((1, 1, own), lambda t, sc: (head(t), 0, 0)),
            ]
            + [ANY] * 4,
            scratch_shapes=[
                pltpu.VMEM((8 + size, 3 * gw), F32),
                pltpu.VMEM((width, width), BF16),
                pltpu.SemaphoreType.DMA((2 * PIECES,)),
                pltpu.SemaphoreType.DMA((4,)),
            ]
            + [pltpu.VMEM(shape, BF16) for shape in kept + [(hp, hd, total)]],
        ),
        out_shape=[
            pltpu.HBM((total, width), BF16),
            pltpu.HBM((total, 3 * gw), BF16),
            jax.ShapeDtypeStruct((zys, gw, rows), BF16),
            pltpu.HBM((hp, hd, own), F32),
            jax.ShapeDtypeStruct((hp, 1, own), F32),
        ]
        + [pltpu.HBM(shape, BF16) for shape in kept],
        compiler_params=pltpu.CompilerParams(vmem_limit_bytes=32 * MIB),
        cost_estimate=FREE,
        name="attention",
    )(scalars, *left, *right, taps, gain, bias, *flat)


def seen(share, rows, mine, shape):
    key = lax.broadcasted_iota(jnp.int32, shape, 0)
    col = lax.broadcasted_iota(jnp.int32, shape, 1)
    query = jnp.where(col >= rows, share * rows + col - rows, col) + mine * rows
    return key <= query


def head_copies(sources, targets, sems, head, slot):
    return [
        pltpu.make_async_copy(source.at[pl.ds(head, 1)], target.at[pl.ds(slot, 1)], sems.at[i, slot])
        for i, (source, target) in enumerate(zip(sources, targets))
    ]


def attend_step(share, rows, sc, head, q_all, k_all, vt_all, at_ref, o_ref, lse_ref):
    mine = sc[1]
    q, k, vt = (buf.at[pl.ds(head, 1)] for buf in (q_all, k_all, vt_all))
    tile = 2 * rows
    step = share * tile
    hd = vt.shape[1]
    tiles = q.shape[1] // tile
    for t in range(tiles):
        queries = q[0, t * tile : (t + 1) * tile, :]
        scores = [nt(k[0, j * step : (j + 1) * step, :], queries) for j in range(t + 1)]
        scores[t] = jnp.where(seen(share, rows, mine, scores[t].shape), scores[t], MASKED)
        top = jnp.max(scores[t], axis=0, keepdims=True)
        for j in range(t):
            top = jnp.maximum(top, jnp.max(scores[j], axis=0, keepdims=True))
        total, accum = None, None
        for j in range(t + 1):
            probs = jnp.exp(scores[j] - top)
            term = jnp.sum(probs, axis=0, keepdims=True)
            total = term if total is None else total + term
            term = nn(vt[0, :, j * step : (j + 1) * step], probs.astype(BF16))
            accum = term if accum is None else accum + term
        out = accum / total
        o_ref[0, :, t * tile : (t + 1) * tile] = out
        lse_ref[0, :, t * tile : (t + 1) * tile] = top + jnp.log(total)
        low = out.astype(BF16)
        at_ref[2 * t] = low[:, :rows]
        at_ref[2 * t + 1] = low[:, rows:]


def attend_back_kernel(share, rows, head, sc, q_all, k_all, kt_all, v_all, o_all, dot_ref, lse, mine_ref, send_ref,
                       dq_acc, dk_acc, dv_acc, q, k, kt, v, o, sems):
    mine = sc[1]
    copies = head_copies((q_all, k_all, kt_all, v_all, o_all), (q, k, kt, v, o), sems, head, 0)
    for copy in copies:
        copy.start()
    own = q.shape[1]
    hd = v.shape[2]
    tile = 2 * rows
    step = share * tile
    tiles = own // tile
    total = tiles * step
    dq_acc[...] = jnp.zeros(dq_acc.shape, F32)
    dk_acc[total:, :] = jnp.zeros((RIM, hd), F32)
    dv_acc[total:, :] = jnp.zeros((RIM, hd), F32)
    for copy in copies:
        copy.wait()
    for t in reversed(range(tiles)):
        queries = q[0, t * tile : (t + 1) * tile, :]
        douts = jnp.concatenate([dot_ref[2 * t], dot_ref[2 * t + 1]], axis=1)
        outs = o[0, :, t * tile : (t + 1) * tile]
        logs = lse[0, :, t * tile : (t + 1) * tile]
        inner = jnp.sum(outs * douts.astype(F32), axis=0, keepdims=True)
        dqt = jnp.zeros((hd, tile), F32)
        for j in reversed(range(t + 1)):
            at_j = slice(j * step, (j + 1) * step)
            probs = jnp.exp(nt(k[0, at_j, :], queries) - logs)
            if j == t:
                probs = jnp.where(seen(share, rows, mine, probs.shape), probs, 0.0)
            dv = nt(probs.astype(BF16), douts)
            dprobs = nn(v[0, at_j, :], douts)
            dscores = (probs * (dprobs - inner)).astype(BF16)
            dk = nn(dscores, queries)[:, :hd]
            if t == tiles - 1:
                dv_acc[at_j, :] = dv
                dk_acc[at_j, :] = dk
            else:
                dv_acc[at_j, :] += dv
                dk_acc[at_j, :] += dk
            dqt += nn(kt[0, :, at_j], dscores)
        dq = (dqt * 0.125).T
        for b in (2 * t, 2 * t + 1):
            at_b = pl.ds(pl.multiple_of((b * share + mine) * rows, rows), rows)
            dq_acc[at_b, :] = dq[(b % 2) * rows : (b % 2 + 1) * rows]
    for b in range(own // rows):
        for r in range(share):
            start = (b * share + (mine ^ r)) * rows
            rows_i = pl.ds(pl.multiple_of(start, rows), rows + RIM)
            block = jnp.concatenate([acc[rows_i, :] for acc in (dq_acc, dk_acc, dv_acc)], axis=1)
            if r == 0:
                mine_ref[b] = block
            else:
                send_ref[r - 1, b] = block.astype(BF16)


def attend_back(scalars, head, q, k, kt, v, dout_t, o, lse, share, rows):
    hp, own, wide = q.shape
    total = k.shape[1]
    hd = v.shape[2]
    blocks = own // rows
    whole = lambda a: pl.BlockSpec(a.shape, lambda i, sc: (0,) * len(a.shape))
    one = lambda a: pl.BlockSpec((1, *a.shape[1:]), lambda i, sc: (head, 0, 0))
    out_shape = [
        pltpu.HBM((blocks, rows + RIM, 3 * hd), F32),
        jax.ShapeDtypeStruct((share - 1, blocks, rows + RIM, 3 * hd), BF16),
    ]
    return pl.pallas_call(
        functools.partial(attend_back_kernel, share, rows, head),
        grid_spec=pltpu.PrefetchScalarGridSpec(
            num_scalar_prefetch=1,
            grid=(1,),
            in_specs=[ANY] * 5 + [pl.BlockSpec((blocks, hd, rows), lambda i, sc: (0, head, 0)), one(lse)],
            out_specs=[whole(a) for a in out_shape],
            scratch_shapes=[pltpu.VMEM((total + RIM, hd), F32)] * 3
            + [pltpu.VMEM((1, *a.shape[1:]), a.dtype) for a in (q, k, kt, v, o)]
            + [pltpu.SemaphoreType.DMA((5, 1))],
        ),
        out_shape=out_shape,
        compiler_params=pltpu.CompilerParams(vmem_limit_bytes=16 * MIB),
        cost_estimate=FREE,
        name="attend_back",
    )(scalars, q, k, kt, v, o, dout_t, lse)


def project_back_kernel(share, rows, heads, parts, counts, sc, *refs):
    (kept, recv), refs = split_lists(refs, (heads, heads * (share - 1)))
    left, right, h_ref, pre_ref, taps, small_two = refs[:6]
    lists, refs = split_lists(refs[6:], counts)
    left_keep, left_send, right_keep, right_send, dw_keep, dw_send, buf, w, dw_acc, small_acc, conv_acc, sems = refs
    step = pl.program_id(0)
    steps = pl.num_programs(0)
    width = w.shape[0]
    half = width // 2

    @pl.when(step == 0)
    def _():
        copies = piece_copies(lists, w, sems, sc[5], sc[3], (0, w.shape[0] // 2 // fsdp_size(lists)))
        for copy in copies:
            copy.start()
        dw_acc[...] = jnp.zeros(dw_acc.shape, F32)
        small_acc[...] = jnp.zeros(small_acc.shape, F32)
        conv_acc[...] = jnp.zeros(conv_acc.shape, F32)
        for copy in copies:
            copy.wait()

    hd = kept[0].shape[2] // 3
    per = kept[0].shape[0]
    now, one, two, x = [], [], [], []
    for z in range(per):
        for i in range(heads):
            total = kept[i][z]
            for r in recv[i * (share - 1) : (i + 1) * (share - 1)]:
                total = total + r[0, z].astype(F32)
            for j in range(3):
                start = (j * heads + i) * hd
                buf[z, :, start : start + hd] = total[:, j * hd : (j + 1) * hd]
        now.append(buf[z, 0:rows, :])
        one.append(buf[z, 1 : rows + 1, :])
        two.append(buf[z, 2 : rows + 2, :])
        at_z = z ^ (sc[0] % per)
        x.append(jnp.concatenate([left[0, at_z], right[0, at_z]], axis=1))
    now, one, two, x = (jnp.concatenate(v, axis=0) for v in (now, one, two, x))
    dpre = (taps[0:1, :] * now + taps[1:2, :] * one + taps[2:3, :] * two).astype(BF16)
    pre = jnp.concatenate([pre_ref[z, 0] for z in range(per)], axis=0).astype(F32)
    n, _ = normed_parts(x.astype(F32))
    dh = nt(dpre, w[:, : dpre.shape[1]])
    for z in range(per):
        k = (per * step + z) ^ sc[0]
        bit_s, bit_a, bit_b = k // 4, k // 2 % 2, k % 2
        dh_z = dh[z * rows : (z + 1) * rows]
        to_left, to_right = 2 * bit_b + bit_s, 2 * bit_a + bit_s

        @pl.when(bit_a == 0)
        def _(dh_z=dh_z, to_left=to_left):
            left_keep[to_left] = dh_z[:, :half]

        @pl.when(bit_a == 1)
        def _(dh_z=dh_z, to_left=to_left):
            left_send[to_left] = dh_z[:, :half].astype(BF16)

        @pl.when(bit_b == 0)
        def _(dh_z=dh_z, to_right=to_right):
            right_keep[to_right] = dh_z[:, half:]

        @pl.when(bit_b == 1)
        def _(dh_z=dh_z, to_right=to_right):
            right_send[to_right] = dh_z[:, half:].astype(BF16)

    h = jnp.concatenate([h_ref[z, 0] for z in range(per)], axis=0)
    dw_acc[...] += tn(h, dpre)
    small_acc[0:1, :] += jnp.sum(dh * n, axis=0, keepdims=True)
    small_acc[1:2, :] += jnp.sum(dh, axis=0, keepdims=True)
    conv_acc[0:3, :] += jnp.concatenate([jnp.sum(pre * d, axis=0, keepdims=True) for d in (now, one, two)], axis=0)

    @pl.when(step == steps - 1)
    def _():
        core = sc[3]
        own = width // parts
        high = own // 2
        cols = dw_acc.shape[1]
        small_acc[2:4, :] = small_two[...]
        for p in range(parts):
            gains = small_acc[0:4, p * own : (p + 1) * own]
            gains = jnp.concatenate([gains, jnp.zeros((4, cols - own), F32)], axis=1)
            tail = jnp.concatenate([gains, conv_acc[0:3, :], jnp.zeros((TAIL - 7, cols), F32)], axis=0)
            keep = pl.ds(pl.multiple_of((2 * p + core) * high, high), high)
            send = pl.ds(pl.multiple_of((2 * p + 1 - core) * high, high), high)
            dw_keep[p, 0:high, :] = dw_acc[keep, :]
            dw_keep[p, high : high + TAIL, :] = tail
            dw_send[p, 0:high, :] = dw_acc[send, :].astype(BF16)
            dw_send[p, high : high + TAIL, :] = tail.astype(BF16)


def project_back(scalars, mine, recv, left, right, h, pre, taps, small_two, w_lists, share, rows, parts):
    counts = [len(pieces) for pieces in w_lists]
    flat = [piece for pieces in w_lists for piece in pieces]
    blocks, ext, thin = mine[0].shape
    heads = len(mine)
    cols = heads * thin
    width = h.shape[1]
    half = width // 2
    high = width // parts // 2
    whole = lambda *shape: pl.BlockSpec(shape, lambda t, sc: (0,) * len(shape))
    per = blocks // 2
    piece = pl.BlockSpec((1, per, rows, half), lambda t, sc: (0, t ^ (sc[0] // per), 0, 0))
    by_block = lambda a: a.reshape(blocks, share, rows, a.shape[1])
    out_shape = [
        jax.ShapeDtypeStruct((blocks // 2, rows, half), F32),
        jax.ShapeDtypeStruct((blocks // 2, rows, half), BF16),
        jax.ShapeDtypeStruct((blocks // 2, rows, half), F32),
        jax.ShapeDtypeStruct((blocks // 2, rows, half), BF16),
        jax.ShapeDtypeStruct((parts, high + TAIL, cols), F32),
        jax.ShapeDtypeStruct((parts, high + TAIL, cols), BF16),
    ]
    return pl.pallas_call(
        functools.partial(project_back_kernel, share, rows, heads, parts, counts),
        grid_spec=pltpu.PrefetchScalarGridSpec(
            num_scalar_prefetch=1,
            grid=(blocks // per,),
            in_specs=[pl.BlockSpec((per, ext, thin), lambda t, sc: (t, 0, 0))] * heads
            + [pl.BlockSpec((1, per, ext, thin), lambda t, sc: (0, t, 0, 0))] * len(recv)
            + [
                piece,
                piece,
                pl.BlockSpec((per, 1, rows, width), lambda t, sc: (t, sc[1], 0, 0)),
                pl.BlockSpec((per, 1, rows, cols), lambda t, sc: (t, sc[1], 0, 0)),
                whole(3, cols),
                whole(2, width),
            ]
            + [ANY] * len(flat),
            out_specs=[whole(*o.shape) for o in out_shape],
            scratch_shapes=[
                pltpu.VMEM((per, ext, cols), F32),
                pltpu.VMEM((width, width), BF16),
                pltpu.VMEM((width, cols), F32),
                pltpu.VMEM((8, width), F32),
                pltpu.VMEM((8, cols), F32),
                pltpu.SemaphoreType.DMA((2 * PIECES,)),
            ],
        ),
        out_shape=out_shape,
        compiler_params=pltpu.CompilerParams(vmem_limit_bytes=28 * MIB),
        cost_estimate=FREE,
        name="project_back",
    )(scalars, *mine, *recv, left, right, by_block(h), by_block(pre), taps, small_two, *flat)


def mix_kernel(counts, sc, attn, tokens, gain, bias, *refs):
    lists, refs = split_lists(refs, counts)
    y_ref, h_ref, w_ref, w, sems, save_sem = refs
    size = w.shape[0] // 2 // fsdp_size(lists)
    copies = piece_copies(lists, w, sems, sc[5], sc[3], (size, size))
    for copy in copies:
        copy.start()
    for copy in copies:
        copy.wait()
    save = pltpu.make_async_copy(w, w_ref, save_sem)
    save.start()
    nseq, rows, width = tokens.shape
    parts = h_ref.shape[0]
    own = width // parts
    for i in range(nseq):
        y = tokens[i].astype(F32) + tn(attn[i], w[...])
        y_ref[i] = y
        n, _ = normed_parts(y)
        h = (n * gain[...] + bias[...]).astype(BF16)
        for p in range(parts):
            h_ref[p, i * rows : (i + 1) * rows, :] = h[:, p * own : (p + 1) * own]
    save.wait()


def mix(scalars, attn, tokens, gain, bias, w_lists, parts):
    counts = [len(pieces) for pieces in w_lists]
    flat = [piece for pieces in w_lists for piece in pieces]
    nseq, rows, width = tokens.shape
    whole = lambda a: pl.BlockSpec(a.shape, lambda i, sc: (0,) * len(a.shape))
    out_shape = [
        pltpu.HBM((nseq, rows, width), F32),
        jax.ShapeDtypeStruct((parts, nseq * rows, width // parts), BF16),
    ]
    args = (attn, tokens, gain, bias)
    return pl.pallas_call(
        functools.partial(mix_kernel, counts),
        grid_spec=pltpu.PrefetchScalarGridSpec(
            num_scalar_prefetch=1,
            grid=(1,),
            in_specs=[whole(a) for a in args] + [ANY] * len(flat),
            out_specs=[whole(a) for a in out_shape] + [ANY],
            scratch_shapes=[
                pltpu.VMEM((width, width), BF16),
                pltpu.SemaphoreType.DMA((2 * PIECES,)),
                pltpu.SemaphoreType.DMA,
            ],
        ),
        out_shape=out_shape + [pltpu.HBM((width, width), BF16)],
        compiler_params=pltpu.CompilerParams(vmem_limit_bytes=58 * MIB),
        cost_estimate=FREE,
        name="mix",
    )(scalars, *args, *flat)


def feed_kernel(counts, merged, sc, h_own, h_other, d_own, d_other, *refs):
    (ups, downs), refs = split_lists(refs, counts)
    r_ref, du_ref, dh_keep, dh_send, y_keep, y_send, far_ref, up, down, sems = refs
    parts, rows, own = h_own.shape
    split = r_ref.shape[2]
    copies, later = [], []
    if merged:
        for p in range(parts):
            take = (p * own, own)
            cols = pl.ds(p * split, split)
            copies += piece_copies([ups], up, sems.at[0, p], sc[5], 0, take, cols)
        later += piece_copies([ups], down, sems.at[1, 0], sc[5], 0, (parts * own, split))
    else:
        copies += piece_copies([ups], up, sems.at[0, 0], sc[5], 0)
        later += piece_copies([downs], down, sems.at[1, 0], sc[5], 0)
    for copy in copies + later:
        copy.start()
    for copy in copies:
        copy.wait()
    h = jnp.concatenate(
        [jnp.concatenate([ref[p] for p in range(parts)], axis=1) for ref in (h_own, h_other)], axis=0
    )
    d = jnp.concatenate([d_own[...], d_other[...]], axis=0)
    dh = None
    y = None
    for p in range(parts):
        cols = slice(p * split, (p + 1) * split)
        act = jnp.maximum(nn(h, up[:, cols]), 0.0)
        r = jnp.square(act).astype(BF16)
        r_ref[p] = r
        if p == 0:
            for copy in later:
                copy.wait()
        dr = nt(d, down[cols, :])
        du = (dr * 2.0 * act).astype(BF16)
        du_ref[:, cols] = du
        term = nt(du, up[:, cols])
        dh = term if dh is None else dh + term
        term = nn(r, down[cols, :])
        y = term if y is None else y + term
    dh_keep[...] = dh[:rows]
    dh_send[...] = dh[rows:].astype(BF16)
    y_keep[...] = y[:rows]
    y_send[...] = y[rows:].astype(BF16)
    for i in range(parts // 2):
        far_ref[i] = tn(r_ref[(1 - sc[9]) * (parts // 2) + i], d).astype(BF16)


def feed(scalars, h_own, h_other, d_own, d_other, ups, downs, split):
    parts, rows, own = h_own.shape
    width = parts * own
    cols = split * parts
    whole = lambda a: pl.BlockSpec(a.shape, lambda i, sc: (0,) * len(a.shape))
    out_shape = [
        jax.ShapeDtypeStruct((parts, 2 * rows, split), BF16),
        pltpu.HBM((2 * rows, cols), BF16),
        pltpu.HBM((rows, width), F32),
        jax.ShapeDtypeStruct((rows, width), BF16),
        pltpu.HBM((rows, width), F32),
        jax.ShapeDtypeStruct((rows, width), BF16),
        jax.ShapeDtypeStruct((parts // 2, split, width), BF16),
    ]
    args = (h_own, h_other, d_own, d_other)
    return pl.pallas_call(
        functools.partial(feed_kernel, (len(ups), len(downs)), not downs),
        grid_spec=pltpu.PrefetchScalarGridSpec(
            num_scalar_prefetch=1,
            grid=(1,),
            in_specs=[whole(a) for a in args] + [ANY] * (len(ups) + len(downs)),
            out_specs=[whole(a) for a in out_shape],
            scratch_shapes=[
                pltpu.VMEM((width, cols), BF16),
                pltpu.VMEM((cols, width), BF16),
                pltpu.SemaphoreType.DMA((2, parts, PIECES)),
            ],
        ),
        out_shape=out_shape,
        compiler_params=pltpu.CompilerParams(vmem_limit_bytes=28 * MIB),
        cost_estimate=FREE,
        name="feed",
    )(scalars, *args, *ups, *downs)


def mix_back_kernel(sc, dh_own, dh_other, y, dtop, gain, w, attn, dy_ref, dout_ref, small_ref, keep_ref, send_ref,
                    grad):
    nseq, rows, width = y.shape
    sums = None
    for i in range(nseq):
        at_i = slice(i * rows, (i + 1) * rows)
        dh = dh_own[at_i, :] + dh_other[at_i, :].astype(F32)
        n, scale = normed_parts(y[i])
        dy = dtop[at_i, :].astype(F32) + norm_back(dh, n, scale, gain[...])
        dy_ref[i] = dy
        low = dy.astype(BF16)
        dout_ref[i] = nt(w[...], low).astype(BF16)
        term = nn(attn[i], low)
        grad[...] = term if i == 0 else grad[...] + term
        term = jnp.concatenate([jnp.sum(dh * n, axis=0, keepdims=True), jnp.sum(dh, axis=0, keepdims=True)], axis=0)
        sums = term if sums is None else sums + term
    small_ref[...] = sums
    parts, size, _ = keep_ref.shape
    for p in range(parts):
        keep_ref[p] = grad[pl.ds(pl.multiple_of((2 * p + sc[3]) * size, size), size), :]
        send_ref[p] = grad[pl.ds(pl.multiple_of((2 * p + 1 - sc[3]) * size, size), size), :].astype(BF16)


def mix_back(scalars, dh_own, dh_other, y, dtop, gain, w, attn, parts):
    nseq, rows, width = y.shape
    out_shape = [
        pltpu.HBM((nseq, rows, width), F32),
        jax.ShapeDtypeStruct((nseq, width, rows), BF16),
        pltpu.HBM((2, width), F32),
        pltpu.HBM((parts, width // parts // 2, width), F32),
        jax.ShapeDtypeStruct((parts, width // parts // 2, width), BF16),
    ]
    args = (dh_own, dh_other, y, dtop, gain, w, attn)
    return whole_call(mix_back_kernel, scalars, args, out_shape, "mix_back", [pltpu.VMEM((width, width), F32)], 58)


def whole_call(body, scalars, args, out_shape, name, scratch=(), limit=12):
    whole = lambda a: pl.BlockSpec(a.shape, lambda i, sc: (0,) * len(a.shape))
    return pl.pallas_call(
        body,
        grid_spec=pltpu.PrefetchScalarGridSpec(
            num_scalar_prefetch=1,
            grid=(1,),
            in_specs=[whole(a) for a in args],
            out_specs=[whole(a) for a in out_shape],
            scratch_shapes=list(scratch),
        ),
        out_shape=out_shape,
        compiler_params=pltpu.CompilerParams(vmem_limit_bytes=limit * MIB),
        cost_estimate=FREE,
        name=name,
    )(scalars, *args)


def fold(scalars, keep, got, which):
    def body(sc, keep_ref, got_ref, keep_out, send_out):
        bit = 0 if which is None else sc[which]
        for i in range(keep_ref.shape[0]):
            keep_out[i] = keep_ref[i, bit].astype(F32) + got_ref[i, bit].astype(F32)
            send_out[i] = (keep_ref[i, 1 - bit].astype(F32) + got_ref[i, 1 - bit].astype(F32)).astype(BF16)

    shape = (keep.shape[0], *keep.shape[2:])
    out_shape = [jax.ShapeDtypeStruct(shape, F32), jax.ShapeDtypeStruct(shape, BF16)]
    return whole_call(body, scalars, (keep, got.reshape(keep.shape)), out_shape, "fold")


def fold_halves(scalars, left, left_got, right, right_got):
    rows, half = left.shape[2:]

    def body(sc, lk, lg, rk, rg, left_out, right_out, send_out):
        left_out[0] = lk[0, 0] + lg[0, 0].astype(F32)
        right_out[0] = rk[0, 0] + rg[0, 0].astype(F32)
        send_out[0, :, :half] = (lk[0, 1] + lg[0, 1].astype(F32)).astype(BF16)
        send_out[0, :, half:] = (rk[0, 1] + rg[0, 1].astype(F32)).astype(BF16)

    one = jax.ShapeDtypeStruct((1, rows, half), F32)
    out_shape = [one, one, jax.ShapeDtypeStruct((1, rows, 2 * half), BF16)]
    args = (left, left_got.reshape(left.shape), right, right_got.reshape(right.shape))
    return whole_call(body, scalars, args, out_shape, "fold_halves")


def join(scalars, keep, got):
    def body(sc, keep_ref, got_ref, out):
        out[...] = (keep_ref[...].astype(F32) + got_ref[...].astype(F32)).astype(BF16)

    out_shape = [jax.ShapeDtypeStruct(keep.shape, BF16)]
    return whole_call(body, scalars, (keep, got.reshape(keep.shape)), out_shape, "join")[0]


def append(scalars, held, got):
    def body(sc, held_ref, got_ref, out):
        count = held_ref.shape[0]
        out[0:count] = held_ref[...]
        out[count : 2 * count] = got_ref[...]

    out_shape = [jax.ShapeDtypeStruct((2 * held.shape[0], *held.shape[1:]), held.dtype)]
    return whole_call(body, scalars, (held, got), out_shape, "append")[0]


def merge_low(scalars, down, down_got, out, out_got, which):
    zys, lows, width = down.shape
    outs = out.shape[1]
    fill = -outs % 16

    def body(sc, down_ref, down_got_ref, out_ref, out_got_ref, keep_out, send_out):
        for i in range(zys // 2):
            for target, bit in ((keep_out, sc[which]), (send_out, 1 - sc[which])):
                t = 2 * i + bit
                first = down_ref[t].astype(F32) + down_got_ref[t].astype(F32)
                second = out_ref[t].astype(F32) + out_got_ref[t].astype(F32)
                rows = [first, second] + ([jnp.zeros((fill, width), F32)] if fill else [])
                target[i] = jnp.concatenate(rows, axis=0).astype(target.dtype)

    shape = (zys // 2, lows + outs + fill, width)
    out_shape = [jax.ShapeDtypeStruct(shape, F32), jax.ShapeDtypeStruct(shape, BF16)]
    args = (down, down_got.reshape(down.shape), out, out_got.reshape(out.shape))
    return whole_call(body, scalars, args, out_shape, "merge_low")


def first_norm_back(scalars, tokens, dy, gain, parts):
    nseq, rows, width = tokens.shape

    def body(sc, tokens_ref, dy_ref, gain_ref, lk, rk, got, out):
        seq = sc[6]
        for i in range(nseq):
            here = seq == i
            dh = jnp.where(here, jnp.concatenate([lk[0], rk[0]], axis=1), got[0].astype(F32))
            n, scale = normed_parts(tokens_ref[i].astype(F32))
            out[i] = dy_ref[i] + norm_back(dh, n, scale, gain_ref[...])

    out_shape = [jax.ShapeDtypeStruct(tokens.shape, F32)]
    return whole_call(body, scalars, (tokens, dy, gain, *parts), out_shape, "first_norm_back")[0]


def piece_of(places):
    def block(t, sc):
        d = t ^ sc[0]
        return (d % 2 * 2 ** places[0] + d // 2 % 2 * 2 ** places[1] + d // 4 % 2 * 2 ** places[2], 0, 0)

    return block


def up_rows_kernel(parts, sc, own_ref, other_ref, out_ref):
    first = sc[3] == 0
    own, other = own_ref[0].astype(F32), other_ref[0].astype(F32)
    split = own.shape[1] // parts
    for p in range(parts):
        cols = slice(p * split, (p + 1) * split)
        out_ref[0, :, 2 * p * split : (2 * p + 1) * split] = jnp.where(first, own[:, cols], other[:, cols])
        out_ref[0, :, (2 * p + 1) * split : (2 * p + 2) * split] = jnp.where(first, other[:, cols], own[:, cols])


def up_rows(scalars, own, other, parts):
    pieces, high, wide = own.shape
    return pl.pallas_call(
        functools.partial(up_rows_kernel, parts),
        grid_spec=pltpu.PrefetchScalarGridSpec(
            num_scalar_prefetch=1,
            grid=(pieces,),
            in_specs=[pl.BlockSpec((1, high, wide), piece_of((2, 1, 0)))] * 2,
            out_specs=pl.BlockSpec((1, high, 2 * wide), lambda t, sc: (t, 0, 0)),
        ),
        out_shape=jax.ShapeDtypeStruct((pieces, high, 2 * wide), F32),
        compiler_params=pltpu.CompilerParams(vmem_limit_bytes=8 * MIB),
        cost_estimate=FREE,
        name="up_rows",
    )(scalars, own, other)


def low_rows_kernel(lows, outs, sc, own_ref, other_ref, down_ref, out_ref):
    first = sc[3] == 0
    own, other = own_ref[0].astype(F32), other_ref[0].astype(F32)
    for c, value in enumerate((jnp.where(first, own, other), jnp.where(first, other, own))):
        down_ref[c, 0] = value[:lows]
        out_ref[c, 0] = value[lows : lows + outs]


def low_rows(scalars, own, other, lows, outs):
    pieces, low, width = own.shape
    return pl.pallas_call(
        functools.partial(low_rows_kernel, lows, outs),
        grid_spec=pltpu.PrefetchScalarGridSpec(
            num_scalar_prefetch=1,
            grid=(pieces,),
            in_specs=[pl.BlockSpec((1, low, width), piece_of((1, 2, 0)))] * 2,
            out_specs=[
                pl.BlockSpec((2, 1, lows, width), lambda t, sc: (0, t, 0, 0)),
                pl.BlockSpec((2, 1, outs, width), lambda t, sc: (0, t, 0, 0)),
            ],
        ),
        out_shape=[
            jax.ShapeDtypeStruct((2, pieces, lows, width), F32),
            jax.ShapeDtypeStruct((2, pieces, outs, width), F32),
        ],
        compiler_params=pltpu.CompilerParams(vmem_limit_bytes=8 * MIB),
        cost_estimate=FREE,
        name="low_rows",
    )(scalars, own, other)


def qkv_rows_kernel(groups, high, own, gw, sc, own_ref, other_ref, out_ref, gain_ref, conv_ref):
    core = sc[3]
    swapped = [(g ^ sc[4]) % 2 * 2 + (g ^ sc[4]) // 2 for g in range(groups)]
    convs = []
    gains = None
    for k in swapped:
        tail = own_ref[k].astype(F32)[high:]
        gains = tail[0:4, :own] if gains is None else gains + tail[0:4, :own]
        convs.append(tail[4:7, :])
    gain_ref[...] = gains
    for j in range(3):
        cols = slice(j * gw, (j + 1) * gw)
        conv_ref[:, j * groups * gw : (j + 1) * groups * gw] = jnp.concatenate([c[:, cols] for c in convs], axis=1)
    for c in range(2):
        pieces = [jnp.where(core == c, own_ref[k], other_ref[k]).astype(F32) for k in swapped]
        for j in range(3):
            cols = slice(j * gw, (j + 1) * gw)
            out = slice(j * groups * gw, (j + 1) * groups * gw)
            out_ref[c, :, out] = jnp.concatenate([p[:high, cols] for p in pieces], axis=1)


def qkv_rows(scalars, args, high):
    groups, _, cols = args[0].shape
    own = 2 * high
    shapes = [(2, high, groups * cols), (4, own), (3, groups * cols)]
    out_shape = [jax.ShapeDtypeStruct(shape, F32) for shape in shapes]
    return whole_call(
        functools.partial(qkv_rows_kernel, groups, high, own, cols // 3), scalars, args, out_shape, "qkv_rows"
    )


def per_device(tokens, cotangent, lengths, ln1_gain, ln1_bias, w_qkv, w_conv, w_out, ln2_gain, ln2_bias, w_up, w_down):
    nseq, rows, width = tokens.shape
    half = width // 2
    count = lax.axis_size("ctx")
    parts = lax.axis_size("fsdp")
    rank = lax.axis_index("ctx")
    index = lax.axis_index("fsdp")
    hidden = w_up.shape[1]
    own_rows = ln1_gain.shape[0]
    zys = nseq * GROUPS
    share = count // zys
    hp = HEADS // GROUPS
    hd = width // HEADS
    gw = hp * hd
    mine = rank % share
    core = rank % 2
    zy = rank // share
    seq = zy // GROUPS
    group = zy % GROUPS
    bit_b, bit_a, bit_s = share, 2 * share, 4 * share
    share_bits = bits(share)
    positions = rank * rows + jnp.arange(rows, dtype=jnp.int32)
    valid = positions[None, :] < lengths[:, None]
    high_bits = [index // mask % 2 for mask in reversed(bits(parts))]
    scalars = [zy, mine, lengths[seq], core, group, index, seq, zy // 2 % 2, zy % 2] + high_bits
    scalars = jnp.stack(scalars).astype(jnp.int32)
    at_s, at_a, at_b, at_x = 6, 7, 8, 9

    own_seq, far_seq = at(tokens, seq), at(tokens, 1 - seq)
    w_conv = lax.optimization_barrier((w_conv, far_seq))[0]
    fsdp_bits = bits(parts)
    split = hidden // parts // 2
    packed = pack(scalars, (ln1_gain, ln1_bias, ln2_gain, ln2_bias), w_conv)
    w_qkv, w_out = lax.optimization_barrier((w_qkv, w_out, packed))[:2]
    first = first_part(scalars, w_qkv, w_out, gw)
    pair = jnp.stack([own_seq, exch(far_seq, "ctx", bit_s)])
    left, right = pair[..., :half], pair[..., half:]
    gains, taps = parameters(scalars, gather_list(packed, "fsdp", fsdp_bits), own_rows, gw)
    gain_one, bias_one, gain_two, bias_two = (gains[i : i + 1] for i in range(4))
    first = gather_list(first, "fsdp", fsdp_bits)
    w_up, w_down = lax.optimization_barrier((w_up, w_down, left, gains, first[-1]))[:2]
    left = jnp.stack([left, exch(left, "ctx", bit_a)], axis=1)
    right = jnp.stack([right, exch(right, "ctx", bit_b)], axis=1)
    left = jnp.stack([left, exch(left, "ctx", bit_b)], axis=2)
    right = jnp.stack([right, exch(right, "ctx", bit_a)], axis=1)
    left = gather_list(left.reshape(1, zys, rows, half), "ctx", share_bits)
    right = gather_list(right.reshape(1, zys, rows, half), "ctx", share_bits)

    both_cores = lambda pieces: [pieces, [exch(piece, "ctx", 1) for piece in pieces]]
    first = both_cores(first)
    if split == width:
        ups = gather_list(rest_part(scalars, w_up, w_down, parts), "fsdp", fsdp_bits)
        downs = []
    else:
        ups = gather_list(up_part(scalars, w_up, parts)[None], "fsdp", fsdp_bits)
        downs = gather_list(at(w_down.reshape(2, split, width), core)[None], "fsdp", fsdp_bits)

    dtop = jnp.where(valid[..., None], cotangent, jnp.zeros_like(cotangent)).reshape(nseq * rows, width)
    dtop_other = exch(dtop, "ctx", 1)
    left[0], taps, gain_one, bias_one = lax.optimization_barrier(
        (left[0], taps, gain_one, bias_one, gain_two, bias_two, dtop)
    )[:4]
    h_one, pre, attn_t, o, lse, q, k, kt, v = attention(
        scalars, left, right, first, taps, gain_one, bias_one, share, hp, hd
    )
    classes = [[i for i in range(count) if i % share == s] for s in range(share)]
    swap = lambda x: lax.all_to_all(x, "ctx", 0, 0, tiled=True, axis_index_groups=classes)
    attn_t = swap(attn_t).reshape(nseq, width, rows)

    order = Order()
    y_one, h_two, w_out_full = mix(scalars, attn_t, tokens, gain_two, bias_two, first, parts)
    h_other = exch(h_two, "ctx", 1)
    r, dupper, dh_keep, dh_send, y_keep, y_send, down_far = feed(
        scalars, h_two, h_other, dtop, dtop_other, ups, downs, split
    )
    dh_other = exch(dh_send, "ctx", 1)
    dtop_pair = jnp.concatenate([dtop, dtop_other])

    near_base = index // (parts // 2) * (parts // 2)

    def near(term):
        return jnp.stack([term(near_base + p) for p in range(parts // 2)])

    def fsdp_more(keep, got):
        for i, mask in enumerate(reversed(fsdp_bits[:-1])):
            keep, send = fold(scalars, keep.reshape(1, 2, mask, *keep.shape[1:]), got, at_x + 1 + i)
            keep, got = keep[0], exch(send[0], "fsdp", mask)
        return keep, got

    down_term = lambda p: tn(at(r, p), dtop_pair)
    down_got = exch(down_far, "fsdp", parts // 2)
    dh_keep, dh_other = order(dh_keep, dh_other)
    dy_one, dout_t, small_two, out_keep, out_send = mix_back(
        scalars, dh_keep, dh_other, y_one, dtop, gain_two, w_out_full, attn_t, parts
    )
    order.mark(dout_t)
    r, dupper, y_keep, y_send, h_two, h_other = order(r, dupper, y_keep, y_send, h_two, h_other)
    h_pair = jnp.concatenate([h_two, h_other], axis=1)
    dout_t = swap(dout_t.reshape(zys, gw, rows))

    def cut(held, axis, bit):
        keep = lax.dynamic_slice_in_dim(held, bit, 1, axis)
        send = lax.dynamic_slice_in_dim(held, 1 - bit, 1, axis)
        return keep, send.astype(BF16)

    zy_bits = {"s": (0, bit_s, zy // 4), "a": (1, bit_a, zy // 2 % 2), "b": (2, bit_b, zy % 2)}
    out_keep = out_keep.reshape(1, 2, parts // 2, *out_keep.shape[1:])
    out_keep, out_send = fold(scalars, out_keep, exch(out_send, "ctx", 1), at_x)
    out_keep, out_got = out_keep[0], exch(out_send[0], "fsdp", parts // 2)
    grad_up = jnp.einsum("pnk,nf->pkf", h_pair, dupper, preferred_element_type=F32)
    grad_up = grad_up.reshape(parts, 2, 2, 2, own_rows // zys, hidden // 2)
    up_keep, up_send = cut(grad_up, 2, zy_bits["a"][2])
    down_keep = near(down_term)
    y_got = exch(y_send, "ctx", 1)

    dout_t, up_keep, up_send, down_keep, out_keep, y_got = lax.optimization_barrier(
        (dout_t, up_keep, up_send, down_keep, out_keep, y_got)
    )
    up_got = exch(up_send, "ctx", bit_a)
    lows = down_keep.shape[1] // zys
    outs = out_keep.shape[1] // zys
    high = own_rows // zys
    up_rest = (high, hidden // 2)
    tail_rows = own_rows // 2 + TAIL
    dw_rest = (tail_rows, 3 * gw)

    keep = {"up": up_keep, "down": down_keep, "out": out_keep, "dout": dout_t}
    got = {"up": up_got, "down": down_got, "out": out_got}
    heads_keep, heads_got = [], []
    done = {}

    def fold_step(x, which, shape, axis, mask):
        def run():
            kept, send = fold(scalars, order(keep[x]).reshape(shape), got[x], which)
            order.mark(send)
            keep[x] = kept
            got[x] = exch(send, axis, mask)

        return run

    def join_step(x, shape, mask):
        def run():
            keep[x] = order.mark(join(scalars, order(keep[x]).reshape(shape), got[x]))
            got[x] = exch(keep[x], "ctx", mask)

        return run

    def append_step(x, mask):
        def run():
            keep[x] = order.mark(append(scalars, order(keep[x]), got[x]))
            got[x] = exch(keep[x], "ctx", mask)

        return run

    def head(h):
        def run():
            kept, sent = attend_back(scalars, h, q, k, kt, v, order(keep["dout"]), o, lse, share, rows)
            heads_keep.append(order.mark(kept))
            heads_got.extend(exch(sent[x - 1 : x], "ctx", x) for x in range(1, share))

        return run

    def low_first():
        keep["down"], keep["out"] = order(keep["down"], keep["out"])
        for x in ("down", "out"):
            keep[x], got[x] = fsdp_more(keep[x], got[x])
        kept, send = merge_low(
            scalars,
            keep["down"].reshape(zys, lows, width),
            got["down"],
            keep["out"].reshape(zys, outs, width),
            got["out"],
            at_b,
        )
        order.mark(send)
        keep["low"] = kept
        got["low"] = exch(send, "ctx", bit_b)

    low_rest = (lows + outs + -outs % 16, width)

    def up_between():
        keep["up"], got["up"] = fsdp_more(keep["up"].reshape(parts // 2, 2, 2, *up_rest), got["up"])
        fold_step("up", at_b, (2, 2, *up_rest), "ctx", bit_b)()

    def back():
        last = order(heads_keep[-1])
        left_keep, left_send, right_keep, right_send, dw_keep, dw_send = project_back(
            scalars, heads_keep[:-1] + [last], heads_got, left[0], right[0], h_one, pre, taps, small_two, first,
            share, rows, parts,
        )
        order.mark(dw_send)
        keep.update(left=left_keep, right=right_keep, qkv=dw_keep)
        got["left"] = exch(left_send, "ctx", bit_a)
        got["right"] = exch(right_send, "ctx", bit_b)
        got["qkv"] = exch(dw_send, "ctx", 1)

    def qkv_between():
        keep["qkv"], got["qkv"] = fsdp_more(keep["qkv"].reshape(parts // 2, *dw_rest), got["qkv"])
        join_step("qkv", dw_rest, bit_s)()

    def qkv_whole():
        block = join(scalars, order(keep["qkv"]), got["qkv"])
        for mask in share_bits[1:]:
            block = join(scalars, block, exch(block, "ctx", mask))
        keep["qkv"] = order.mark(block[None])
        got["qkv"] = exch(keep["qkv"], "ctx", bit_a)

    def halves():
        kept = order(keep["left"], keep["right"])
        keep["left"], keep["right"], send = fold_halves(scalars, kept[0], got["left"], kept[1], got["right"])
        order.mark(send)
        got["input"] = exch(send, "ctx", bit_s)

    def input_end():
        kept = (keep["left"], keep["right"], got["input"])
        total = (order(y_keep) + y_got.astype(F32)).reshape(nseq, rows, width)
        done["output"] = order.mark(jnp.where(valid[..., None], y_one + total, 0.0).astype(BF16))
        done["input"] = order.mark(first_norm_back(scalars, tokens, order(dy_one), gain_one, kept))

    def qkv_end():
        grad, gains, convs = qkv_rows(scalars, (order(keep["qkv"]), got["qkv"]), own_rows // 2)
        done["qkv"] = order.mark(grad.reshape(own_rows, 3 * width))
        share_cols = 3 * width // parts
        done["gains"] = gains
        done["conv"] = lax.dynamic_slice_in_dim(convs, index * share_cols, share_cols, 1)

    def low_end():
        down_grad, out_grad = low_rows(scalars, order(keep["low"]), got["low"], lows, outs)
        done["down"] = order.mark(down_grad.reshape(hidden // parts, width))
        done["out"] = out_grad.reshape(own_rows, width)

    def up_end():
        grad = up_rows(scalars, order(keep["up"]), got["up"], parts)
        done["up"] = order.mark(grad.reshape(own_rows, hidden))

    steps = {
        "head 0": head(0),
        "head 1": head(1),
        "head 2": head(2),
        "low b": low_first,
        "low a": fold_step("low", at_a, (2, 2, *low_rest), "ctx", bit_a),
        "low s": fold_step("low", at_s, (1, 2, *low_rest), "ctx", bit_s),
        "low sum": join_step("low", (1, *low_rest), bit_s),
        "low gather b": append_step("low", bit_b),
        "low gather a": append_step("low", bit_a),
        "low core": append_step("low", 1),
        "low end": low_end,
        "up x": fold_step("up", at_x, (1, 2, parts // 2 * 4 * high, hidden // 2), "fsdp", parts // 2),
        "up b": up_between,
        "up s": fold_step("up", at_s, (1, 2, *up_rest), "ctx", bit_s),
        "up sum": join_step("up", (1, *up_rest), bit_s),
        "up gather a": append_step("up", bit_a),
        "up gather b": append_step("up", bit_b),
        "up core": append_step("up", 1),
        "up end": up_end,
        "back": back,
        "qkv x": fold_step("qkv", at_x, (1, 2, parts // 2, *dw_rest), "fsdp", parts // 2),
        "qkv s": qkv_between,
        "qkv a": qkv_whole,
        "qkv gather b": append_step("qkv", bit_b),
        "qkv core": append_step("qkv", 1),
        "qkv end": qkv_end,
        "right a": fold_step("right", None, (1, 2, 2, rows, half), "ctx", bit_a),
        "left b": fold_step("left", None, (1, 2, 2, rows, half), "ctx", bit_b),
        "input s": halves,
        "input end": input_end,
    }
    for name in LINE:
        steps[name]()
    output, input_grad, gains = done["output"], done["input"], done["gains"]
    w_qkv_grad, w_conv_grad, w_out_grad = done["qkv"], done["conv"], done["out"]
    w_up_grad, w_down_grad = done["up"], done["down"]

    return (
        output,
        input_grad,
        gains[0],
        gains[1],
        w_qkv_grad,
        w_conv_grad,
        w_out_grad,
        gains[2],
        gains[3],
        w_up_grad,
        w_down_grad,
    )


def solution(mesh):
    rows = P("fsdp", "ctx", None)
    first = P("fsdp")
    weight = P("fsdp", None)
    second = P(None, "fsdp")
    in_specs = (rows, rows, first, first, first, weight, second, weight, first, first, weight, weight)
    out_specs = (rows, rows, first, first, weight, second, weight, first, first, weight, weight)
    return jax.shard_map(per_device, mesh=mesh, in_specs=in_specs, out_specs=out_specs, check_vma=False)
```
